32 devices in a mesh: fsdp: 4 (over x, core), ctx: 2 (over y), tp: 4 (over z).
Axes of the slice: x: 2, y: 2, z: 4, core: 2. Of those that a mesh axis runs over, the one named last changes fastest.
Arguments:
- tokens: bfloat16 [4, 512, 2048], P('fsdp', 'ctx'), may hold values from -6 to 6
- cotangent: bfloat16 [4, 512, 2048], P('fsdp', 'ctx'), may hold values from -6 to 6
- doc_lengths: int32 [4, 5], P('fsdp'), may hold values from 1 to 508, as said below
- norm_gains: bfloat16 [2, 2, 2048], P(None, None, ('fsdp', 'ctx')), may hold values from 0.5 to 1.5
- norm_biases: bfloat16 [2, 2, 2048], P(None, None, ('fsdp', 'ctx')), may hold values from -3 to 3
- qkv_weight: bfloat16 [2, 2048, 3, 2048], P(None, ('fsdp', 'ctx'), None, 'tp'), may hold values from -0.125 to 0.125
- qkv_bias: bfloat16 [2, 3, 2048], P(None, None, ('fsdp', 'ctx')), may hold values from -3 to 3
- out_weight: bfloat16 [2, 2048, 2048], P(None, 'tp', ('fsdp', 'ctx')), may hold values from -1 to 1
- gate_up_weight: bfloat16 [2, 2048, 2, 5632], P(None, ('fsdp', 'ctx'), None, 'tp'), may hold values from -0.125 to 0.125
- down_weight: bfloat16 [2, 5632, 2048], P(None, 'tp', ('fsdp', 'ctx')), may hold values from -0.078125 to 0.078125
Outputs:
- output: bfloat16 [4, 512, 2048], P('fsdp', 'ctx')
- grad_input: float32 [4, 512, 2048], P('fsdp', 'ctx')
- grad_norm_gains: float32 [2, 2, 2048], P(None, None, ('fsdp', 'ctx'))
- grad_norm_biases: float32 [2, 2, 2048], P(None, None, ('fsdp', 'ctx'))
- grad_qkv_weight: float32 [2, 2048, 3, 2048], P(None, ('fsdp', 'ctx'), None, 'tp')
- grad_qkv_bias: float32 [2, 3, 2048], P(None, None, ('fsdp', 'ctx'))
- grad_out_weight: float32 [2, 2048, 2048], P(None, 'tp', ('fsdp', 'ctx'))
- grad_gate_up: float32 [2, 2048, 2, 5632], P(None, ('fsdp', 'ctx'), None, 'tp')
- grad_down: float32 [2, 5632, 2048], P(None, 'tp', ('fsdp', 'ctx'))
The draws below stay inside these ranges and needn't reach their ends.
Inputs may be any that keep to these rules, and one draw needn't show every extreme that they name: `doc_lengths`: each row holds the lengths of 5 documents packed in order into one sequence of 512 tokens and sums to 512; the first two together and the last two together hold at most 255 tokens each, so the middle document starts among the first 256 tokens and ends among the last 256; in one row the first two and the last two hold 2 tokens each.
All inputs are finite; a program needn't handle non-finite values.
Results may differ from the reference program's by a relative error of at most 0.028.
Values may be sent and summed in bfloat16 or wider, within the bound.
No kernel may reach another device: no remote copies, remote signals or barrier semaphores. Data moves between devices by JAX's collectives and lax.ppermute only.
A program may use at most 256 MiB of HBM per device.

```python
import jax
import jax.numpy as jnp
from jax import lax

D = 2048
FF = 5632
HD = 64
ROT = 16
LAYERS = 2
SEQ_DEV = 256
NSEQ = 4
LEN = 512


def draw_doc_lengths(key, part):
    key = jax.random.fold_in(key, 11)
    key_set = jax.random.split(key, 5)
    row_pick = jax.random.randint(key_set[4], (), 0, NSEQ)
    chosen = jnp.arange(NSEQ, dtype=jnp.int32) == row_pick
    head_rows = jnp.where(chosen, 2, jax.random.randint(key_set[0], (NSEQ,), 2, SEQ_DEV))
    tail_rows = jnp.where(chosen, 2, jax.random.randint(key_set[1], (NSEQ,), 2, SEQ_DEV))
    first_doc = jax.random.randint(key_set[2], (NSEQ,), 1, head_rows)
    last_doc = jax.random.randint(key_set[3], (NSEQ,), 1, tail_rows)
    middle_doc = LEN - head_rows - tail_rows
    return jnp.stack([first_doc, head_rows - first_doc, middle_doc, last_doc, tail_rows - last_doc], axis=1).astype(jnp.int32)


def levels(rng, dims, shards, low, high):
    factor_of, own = 1.0, jax.random.fold_in(rng, 6)
    for dim, shards_of in shards:
        heights = jnp.exp(jax.random.uniform(jax.random.fold_in(own, dim), (shards_of,), jnp.float32, low / len(shards), high / len(shards)))
        factor_of = factor_of * jnp.repeat(heights, dims[dim] // shards_of).reshape([-1 if axis == dim else 1 for axis in range(len(dims))])
    return factor_of


def noise(own_key, dims, width, reach, cuts=(), held_as=jnp.bfloat16):
    values = jax.random.normal(own_key, dims, jnp.float32) * width
    if len(cuts) > 0:
        values = levels(own_key, dims, cuts, -0.22, 0.18) * values
    return jnp.clip(values, min=-reach, max=reach).astype(held_as)


def setup_inputs(seed: int = 0) -> dict:
    key_of = jax.random.split(jax.random.key(seed), 11)
    return {
        "tokens": noise(key_of[0], (NSEQ, LEN, D), 1.0, 6.0, ((0, 4), (1, 2))),
        "cotangent": noise(key_of[1], (NSEQ, LEN, D), 1.0, 6.0, ((0, 4), (1, 2))),
        "doc_lengths": draw_doc_lengths(jax.random.fold_in(key_of[10], 71), 0),
        "norm_gains": jnp.clip(1.0 + 0.1 * jax.random.normal(key_of[3], (LAYERS, 2, D), jnp.float32), 0.5, 1.5).astype(jnp.bfloat16),
        "norm_biases": noise(key_of[4], (LAYERS, 2, D), 0.3, 3.0, ((2, 8),)),
        "qkv_weight": noise(key_of[5], (LAYERS, D, 3, D), D ** -0.5, 0.125, ((1, 8), (3, 4))),
        "qkv_bias": noise(key_of[6], (LAYERS, 3, D), 0.5, 3.0, ((2, 8),)),
        "out_weight": noise(key_of[7], (LAYERS, D, D), (D // 64) ** -0.5, 1.0, ((1, 4), (2, 8))),
        "gate_up_weight": noise(key_of[8], (LAYERS, D, 2, FF), D ** -0.5, 0.125, ((1, 8), (3, 4))),
        "down_weight": noise(key_of[9], (LAYERS, FF, D), FF ** -0.5, 0.078125, ((1, 4), (2, 8))),
    }


@jax.custom_vjp
def low(v):
    return lax.optimization_barrier(v.astype(jnp.bfloat16)).astype(jnp.float32)

@jax.custom_vjp
def low_back(v):
    return v

def low_keep(v):
    return (low(v), None)

def low_pass(kept, grad):
    return (grad,)

def back_keep(v):
    return (v, None)

def back_low(kept, grad):
    return (low(grad),)
low.defvjp(low_keep, low_pass)
low_back.defvjp(back_keep, back_low)

def layout(lengths, first_row, row_count):
    token_index = first_row + jnp.arange(row_count, dtype=jnp.int32)
    doc_ends = jnp.cumsum(lengths).astype(jnp.int32)
    starts = (doc_ends - lengths).astype(jnp.int32)
    segment = lax.optimization_barrier(jnp.sum((token_index[:, None] >= doc_ends[None, :]).astype(jnp.int32), axis=1, dtype=jnp.int32))
    doc_begin = lax.optimization_barrier(jnp.max(jnp.where(token_index[:, None] >= starts[None, :], starts[None, :], 0), axis=1)).astype(jnp.int32)
    return (segment, token_index - doc_begin, token_index)

def rotary_tables(position):
    frequency = 10000.0 ** (-jnp.arange(0, ROT, 2, dtype=jnp.float32) / ROT)
    angles = position.astype(jnp.float32)[:, None] * frequency[None, :]
    return (jnp.cos(angles), jnp.sin(angles))

def rotate(field, cos_table, sin_table):
    half_rot = cos_table.shape[1]
    cos_part = cos_table[:, None, :]
    sin_part = sin_table[:, None, :]
    lower = field[..., :half_rot]
    upper = field[..., half_rot:2 * half_rot]
    return jnp.concatenate([lower * cos_part - upper * sin_part, upper * cos_part + lower * sin_part, field[..., 2 * half_rot:]], axis=-1)

def layer_norm(stream, gain_row, shift_row):
    centered = stream - lax.optimization_barrier(jnp.mean(stream, axis=-1, keepdims=True))
    variance = lax.optimization_barrier(jnp.mean(centered * centered, axis=-1, keepdims=True))
    return centered * lax.rsqrt(variance + 1e-05) * gain_row + shift_row

def attention(queries, key_rows, values, segment, token_index):
    length = queries.shape[0]
    block_rows = min(512, length)
    blocks = length // block_rows
    query_blocks = queries.reshape(blocks, block_rows, queries.shape[1], queries.shape[2])
    seg_blocks = segment.reshape(blocks, block_rows)
    index_blocks = token_index.reshape(blocks, block_rows)

    def one_block(inputs):
        query_part, seg_part, index_part = inputs
        scores = low_back(jnp.einsum('qhd,khd->hqk', query_part, key_rows, precision=lax.Precision.HIGHEST) * (1.0 / HD ** 0.5))
        allowed = (seg_part[:, None] == segment[None, :]) & (index_part[:, None] >= token_index[None, :])
        scores = jnp.where(allowed[None], scores, -1e+30)
        row_max = lax.optimization_barrier(jnp.max(scores, axis=2, keepdims=True))
        exponent = jnp.exp(scores - row_max)
        probs = exponent / lax.optimization_barrier(jnp.sum(exponent, axis=2, keepdims=True))
        return jnp.einsum('hqk,khd->qhd', low(probs), values, precision=lax.Precision.HIGHEST)
    result = lax.map(jax.checkpoint(one_block), (query_blocks, seg_blocks, index_blocks))
    return result.reshape(length, queries.shape[1], queries.shape[2])

def run_layers(weights, stream, segment, token_index, cos_table, sin_table):
    gain_set, shift_set, w_qkv, b_qkv, w_out, w_gate_up, w_down = weights
    length = stream.shape[0]
    heads_all = w_qkv.shape[3] // HD
    for layer_index in range(gain_set.shape[0]):
        first_in = low(layer_norm(stream, gain_set[layer_index, 0], shift_set[layer_index, 0]))
        qkv = low_back(jnp.einsum('sd,dch->sch', first_in, w_qkv[layer_index], precision=lax.Precision.HIGHEST) + b_qkv[layer_index][None])
        queries = low(rotate(qkv[:, 0].reshape(length, heads_all, HD), cos_table, sin_table))
        key_rows = low(rotate(qkv[:, 1].reshape(length, heads_all, HD), cos_table, sin_table))
        values = low(qkv[:, 2].reshape(length, heads_all, HD))
        mixed = attention(queries, key_rows, values, segment, token_index)
        mixed = low_back(low(mixed)).reshape(length, heads_all * HD)
        stream = stream + low_back(jnp.dot(mixed, w_out[layer_index], precision=lax.Precision.HIGHEST, preferred_element_type=jnp.float32))
        second_in = low(layer_norm(stream, gain_set[layer_index, 1], shift_set[layer_index, 1]))
        gate_up = low_back(jnp.einsum('sd,dcf->scf', second_in, w_gate_up[layer_index], precision=lax.Precision.HIGHEST))
        hidden = low(jax.nn.silu(gate_up[:, 0]) * gate_up[:, 1])
        stream = stream + low_back(jnp.dot(hidden, w_down[layer_index], precision=lax.Precision.HIGHEST, preferred_element_type=jnp.float32))
    return stream

def reference(tokens, cotangent, doc_lengths, norm_gains, norm_biases, qkv_weight, qkv_bias, out_weight, gate_up_weight, down_weight):
    weights = tuple((array.astype(jnp.float32) for array in (norm_gains, norm_biases, qkv_weight, qkv_bias, out_weight, gate_up_weight, down_weight)))

    def one_sequence(totals, inputs):
        seq_tokens, seq_cotangent, lengths = inputs
        segment, position, token_index = layout(lengths, 0, seq_tokens.shape[0])
        cos_table, sin_table = rotary_tables(position)

        def forward(weight_set, stream):
            return run_layers(weight_set, stream, segment, token_index, cos_table, sin_table)
        result, pullback = jax.vjp(forward, weights, seq_tokens.astype(jnp.float32))
        weight_grads, input_grad = pullback(seq_cotangent.astype(jnp.float32))
        totals = jax.tree.map(lambda first_sum, second_sum: first_sum + second_sum, totals, weight_grads)
        return (totals, (result.astype(jnp.bfloat16), input_grad))
    start_grads = jax.tree.map(jnp.zeros_like, weights)
    totals, (output, grad_input) = lax.scan(one_sequence, start_grads, (tokens, cotangent, doc_lengths))
    return (output, grad_input, totals[0], totals[1], totals[2], totals[3], totals[4], totals[5], totals[6])
```

```python
import functools

import jax
import jax.numpy as jnp
from jax import lax
from jax.experimental import pallas as pl
from jax.experimental.pallas import tpu as pltpu
from jax.sharding import PartitionSpec as P

HD = 64
ROT = 16
LANES = 128
VMEM_LIMIT = 48 * 1024 * 1024
NN = (((1,), (0,)), ((), ()))
NT = (((1,), (1,)), ((), ()))
TN = (((0,), (0,)), ((), ()))
BF = jnp.bfloat16
F32 = jnp.float32


def mm(lhs, rhs, dims):
    return lax.dot_general(lhs, rhs, dims, preferred_element_type=F32)


def spec_vmem():
    return pl.BlockSpec(memory_space=pltpu.VMEM)


def spec_any():
    return pl.BlockSpec(memory_space=pl.ANY)


def spec_smem():
    return pl.BlockSpec(memory_space=pltpu.SMEM)


def call(body, outs, args, specs, scratch, flops, name, out_specs=None):
    moved = sum(a.size * a.dtype.itemsize for a in args) + sum(
        o.size * jnp.dtype(o.dtype).itemsize for o in outs
    )
    return pl.pallas_call(
        body,
        out_shape=outs,
        in_specs=specs,
        out_specs=out_specs if out_specs is not None else [spec_vmem()] * len(outs),
        scratch_shapes=scratch,
        compiler_params=pltpu.CompilerParams(vmem_limit_bytes=VMEM_LIMIT),
        cost_estimate=pl.CostEstimate(flops=flops, bytes_accessed=moved, transcendentals=0),
        name=name,
    )(*args)


def shape(dims, dtype):
    return jax.ShapeDtypeStruct(tuple(dims), dtype)


def weight_copies(offs, pieces, held, sems, matrices):
    copies = []
    for slot, matrix in enumerate(matrices):
        row = []
        for index, piece in enumerate(pieces):
            start = pl.multiple_of(offs[index], LANES)
            row.append(
                pltpu.make_async_copy(
                    piece.at[matrix],
                    held.at[slot, pl.ds(start, piece.shape[1]), :],
                    sems.at[slot, index],
                )
            )
        copies.append(row)
    for row in copies:
        for copy in row:
            copy.start()
    return copies


def finish(copies):
    for copy in copies:
        copy.wait()


def normalized(v):
    centered = v - jnp.mean(v, axis=1, keepdims=True)
    variance = jnp.mean(centered * centered, axis=1, keepdims=True)
    scale = lax.rsqrt(variance + 1e-05)
    return centered * scale, scale


def norm_back(v, cot, gain):
    n, scale = normalized(v)
    e = cot * gain
    grad = scale * (
        e - jnp.mean(e, axis=1, keepdims=True) - n * jnp.mean(e * n, axis=1, keepdims=True)
    )
    return grad, n


def turn(tile, tables, sign):
    return (
        tile * tables[0]
        + sign * (pltpu.roll(tile, 8, 1) * tables[1] + pltpu.roll(tile, LANES - 8, 1) * tables[2])
    )


def turn_wide(wide, tables, sign):
    tabs = (tables[0], tables[1], tables[2])
    return jnp.concatenate(
        [
            turn(wide[:, at : at + LANES], tabs, sign)
            for at in range(0, wide.shape[1], LANES)
        ],
        axis=1,
    )


def qkv_body(n_pieces, has_delta, *refs):
    refs = list(refs)
    offs = refs.pop(0)
    base = refs.pop(0)
    delta = refs.pop(0) if has_delta else None
    gain, shift, bias, tables = refs[:4]
    pieces = refs[4 : 4 + n_pieces]
    rest = refs[4 + n_pieces :]
    if has_delta:
        stream_out = rest.pop(0)
    first_out, q_out, k_out, v_out, held, sems = rest
    copies = weight_copies(offs, pieces, held, sems, (0, 1, 2))
    stream = base[...].astype(F32)
    if has_delta:
        stream = stream + delta[...].astype(F32)
        stream_out[...] = stream
    n, _ = normalized(stream)
    first_out[...] = (n * gain[...] + shift[...]).astype(BF)
    for index, out in enumerate((q_out, k_out, v_out)):
        finish(copies[index])
        part = mm(first_out[...], held[index], NN) + bias[index : index + 1, :]
        if index < 2:
            part = turn_wide(part, tables, 1.0)
        out[...] = part.astype(BF)


def attend_body(n_pieces, n_blocks, *refs):
    offs, q_ref = refs[:2]
    ks = refs[2 : 2 + n_blocks]
    vs = refs[2 + n_blocks : 2 + 2 * n_blocks]
    masks = refs[2 + 2 * n_blocks : 2 + 3 * n_blocks]
    pieces = refs[2 + 3 * n_blocks : 2 + 3 * n_blocks + n_pieces]
    mixed_out, total_out, part_out, held, sems = refs[2 + 3 * n_blocks + n_pieces :]
    copies = weight_copies(offs, pieces, held, sems, (3,))
    for head in range(q_ref.shape[1] // HD):
        span = slice(head * HD, (head + 1) * HD)
        query = q_ref[:, span]
        scores = [
            mm(k[:, span], query, NT) * (1.0 / HD**0.5) + mask[...]
            for k, mask in zip(ks, masks, strict=True)
        ]
        top = functools.reduce(
            jnp.maximum, [jnp.max(s, axis=0, keepdims=True) for s in scores]
        )
        exps = [jnp.exp(s - top) for s in scores]
        total = functools.reduce(jnp.add, [jnp.sum(e, axis=0, keepdims=True) for e in exps])
        inverse = 1.0 / total
        result = functools.reduce(
            jnp.add,
            [mm((e * inverse).astype(BF), v[:, span], TN) for e, v in zip(exps, vs, strict=True)],
        )
        total_out[head : head + 1, :] = top + jnp.log(total)
        mixed_out[:, span] = result.astype(BF)
    finish(copies[0])
    part_out[...] = mm(mixed_out[...], held[0], NT).astype(BF)


def mlp_body(n_pieces, *refs):
    offs, base, delta, gain, shift = refs[:5]
    pieces = refs[5 : 5 + n_pieces]
    mid_out, second_out, gate_out, up_out, hidden_out, part_out, held, sems = refs[5 + n_pieces :]
    copies = weight_copies(offs, pieces, held, sems, (0, 1, 2))
    stream = base[...].astype(F32) + delta[...].astype(F32)
    mid_out[...] = stream
    n, _ = normalized(stream)
    second_out[...] = (n * gain[...] + shift[...]).astype(BF)
    finish(copies[0])
    gate = mm(second_out[...], held[0], NN)
    gate_out[...] = gate.astype(BF)
    act = gate * jax.nn.sigmoid(gate)
    finish(copies[1])
    up = mm(second_out[...], held[1], NN)
    up_out[...] = up.astype(BF)
    hidden_out[...] = (act * up).astype(BF)
    finish(copies[2])
    part_out[...] = mm(hidden_out[...], held[2], NT).astype(BF)


def mlp_back_body(n_pieces, *refs):
    offs, grad_in, gate_ref, up_ref = refs[:4]
    pieces = refs[4 : 4 + n_pieces]
    d_mlp_out, d_gate_out, d_up_out, part_out, held, sems = refs[4 + n_pieces :]
    copies = weight_copies(offs, pieces, held, sems, (2, 0, 1))
    d_mlp_out[...] = grad_in[...].astype(BF)
    gate = gate_ref[...].astype(F32)
    sig = jax.nn.sigmoid(gate)
    finish(copies[0])
    d_hidden = mm(d_mlp_out[...], held[0], NN)
    d_up_out[...] = (d_hidden * (gate * sig)).astype(BF)
    d_gate_out[...] = (
        d_hidden * up_ref[...].astype(F32) * (sig * (1.0 + gate * (1.0 - sig)))
    ).astype(BF)
    finish(copies[1])
    part = mm(d_gate_out[...], held[1], NT)
    finish(copies[2])
    part_out[...] = (part + mm(d_up_out[...], held[2], NT)).astype(BF)


def attend_back_body(n_pieces, n_blocks, *refs):
    offs, mid, cot, gain, grad_in, tables, q_ref, total_ref = refs[:8]
    at = 8
    ks = refs[at : at + n_blocks]
    vs = refs[at + n_blocks : at + 2 * n_blocks]
    masks = refs[at + 2 * n_blocks : at + 3 * n_blocks]
    at += 3 * n_blocks
    pieces = refs[at : at + n_pieces]
    at += n_pieces
    grad_out, d_attn_out, sums_out, dq_out = refs[at : at + 4]
    dkv_outs = refs[at + 4 : at + 4 + n_blocks]
    held, d_mixed, sems = refs[at + 4 + n_blocks :]
    copies = weight_copies(offs, pieces, held, sems, (3,))
    c = cot[...].astype(F32)
    grad, n = norm_back(mid[...], c, gain[...])
    sums_out[0:1, :] = jnp.sum(n * c, axis=0, keepdims=True)
    sums_out[1:2, :] = jnp.sum(c, axis=0, keepdims=True)
    grad = grad_in[...].astype(F32) + grad
    grad_out[...] = grad
    d_attn_out[...] = grad.astype(BF)
    finish(copies[0])
    d_mixed[...] = mm(d_attn_out[...], held[0], NN).astype(BF)
    d_queries = []
    for head in range(q_ref.shape[1] // HD):
        span = slice(head * HD, (head + 1) * HD)
        query = q_ref[:, span]
        d_out = d_mixed[:, span]
        log_total = total_ref[head : head + 1, :]
        probs = [
            jnp.exp(mm(k[:, span], query, NT) * (1.0 / HD**0.5) + mask[...] - log_total)
            for k, mask in zip(ks, masks, strict=True)
        ]
        d_probs = [mm(v[:, span], d_out, NT) for v in vs]
        delta = functools.reduce(
            jnp.add,
            [
                jnp.sum(p * dp, axis=0, keepdims=True)
                for p, dp in zip(probs, d_probs, strict=True)
            ],
        )
        d_scores = [
            (p * (dp - delta)).astype(BF) for p, dp in zip(probs, d_probs, strict=True)
        ]
        d_query = functools.reduce(
            jnp.add, [mm(ds, k[:, span], TN) for ds, k in zip(d_scores, ks, strict=True)]
        )
        d_queries.append(d_query * (1.0 / HD**0.5))
        for ds, p, dkv in zip(d_scores, probs, dkv_outs, strict=True):
            dkv[0, :, span] = (mm(ds, query, NN) * (1.0 / HD**0.5)).astype(dkv.dtype)
            dkv[1, :, span] = mm(p.astype(BF), d_out, NN).astype(dkv.dtype)
    dq_out[...] = turn_wide(jnp.concatenate(d_queries, axis=1), tables, -1.0).astype(BF)


def qkv_back_body(n_pieces, has_other, *refs):
    refs = list(refs)
    offs, dq_ref, own = refs[:3]
    refs = refs[3:]
    other = refs.pop(0) if has_other else None
    tables, stream, n_ref_unused = refs[:3]
    pieces = refs[3 : 3 + n_pieces]
    d_qkv_out, bias_out, part_out, sums_out, held, sems = refs[3 + n_pieces :]
    copies = weight_copies(offs, pieces, held, sems, (0, 1, 2))
    d_key = own[0].astype(F32)
    d_value = own[1].astype(F32)
    if has_other:
        d_key = d_key + other[0].astype(F32)
        d_value = d_value + other[1].astype(F32)
    d_qkv_out[0] = dq_ref[...]
    d_qkv_out[1] = turn_wide(d_key, tables, -1.0).astype(BF)
    d_qkv_out[2] = d_value.astype(BF)
    for index in range(3):
        bias_out[index : index + 1, :] = jnp.sum(
            d_qkv_out[index].astype(F32), axis=0, keepdims=True
        )
    part = None
    for index in range(3):
        finish(copies[index])
        term = mm(d_qkv_out[index], held[index], NT)
        part = term if part is None else part + term
    part_out[...] = part.astype(BF)
    n, _ = normalized(stream[...].astype(F32))
    sums_out[0:1, :] = jnp.sum(n * part, axis=0, keepdims=True)
    sums_out[1:2, :] = jnp.sum(part, axis=0, keepdims=True)


def norm_back_body(stream, cot, gain, grad_in, grad_out):
    grad, _ = norm_back(stream[...].astype(F32), cot[...].astype(F32), gain[...])
    grad_out[...] = grad_in[...] + grad


def weight_grad_body(n_left, n_right, pairs, *refs):
    ids = refs[0]
    n_in = n_left + n_right
    own = refs[1 : 1 + n_in]
    peer = refs[1 + n_in : 1 + 2 * n_in]
    outs = refs[1 + 2 * n_in : 6 + 2 * n_in]
    held = refs[6 + 2 * n_in : 6 + 3 * n_in]
    stage, in_sems, out_sems = refs[6 + 3 * n_in :]
    rows = own[0].shape[0]
    loads = []
    for index in range(n_in):
        for part, source in enumerate((own[index], peer[index])):
            copy = pltpu.make_async_copy(
                source,
                held[index].at[pl.ds(part * rows, rows), :],
                in_sems.at[index, part],
            )
            copy.start()
            loads.append(copy)
    finish(loads)
    half = stage.shape[2]
    own_out, x1, y1, x2, y2 = outs
    targets = (
        (x1.at[0], y1.at[0]),
        (x1.at[1], x2),
        (y2, y1.at[1]),
        (own_out.at[0], own_out.at[1]),
    )
    stores = []
    for block in range(4):
        start = pl.multiple_of(ids[block], LANES)
        for matrix, (left, right) in enumerate(pairs):
            lhs = held[left][:, pl.ds(start, 2 * half)]
            result = mm(lhs, held[n_left + right][...], TN).astype(BF)
            stage[2 * block, matrix] = result[:half]
            stage[2 * block + 1, matrix] = result[half:]
        for part in range(2):
            copy = pltpu.make_async_copy(
                stage.at[2 * block + part], targets[block][part], out_sems.at[block, part]
            )
            copy.start()
            stores.append(copy)
    finish(stores)


def pairs_of(axis, bit):
    return [(index, index ^ bit) for index in range(lax.axis_size(axis))]


def swap_x(array):
    return lax.ppermute(array, "fsdp", pairs_of("fsdp", 2))


def swap_core(array):
    return lax.ppermute(array, "fsdp", pairs_of("fsdp", 1))


def swap_y(array):
    return lax.ppermute(array, "ctx", pairs_of("ctx", 1))


def place():
    fsdp = lax.axis_index("fsdp")
    return fsdp // 2, fsdp % 2, lax.axis_index("ctx")


def gather_pieces(shard, fast):
    if not fast:
        whole = lax.all_gather(shard, ("fsdp", "ctx"), axis=1, tiled=True)
        return [whole], jnp.zeros((1,), jnp.int32)
    rows = shard.shape[1]
    half = rows // 2
    from_x = swap_x(shard)
    from_y = swap_y(shard)
    far_low = swap_x(from_y[:, :half])
    far_high = swap_y(from_x[:, half:])
    mine = [shard, from_x, from_y, far_low, far_high]
    peers = [swap_core(piece) for piece in mine]
    x, core, y = place()

    def row(x_at, core_at, y_at):
        return ((x_at * 2 + core_at) * 2 + y_at) * rows

    offs = []
    for core_at in (core, 1 - core):
        offs += [
            row(x, core_at, y),
            row(1 - x, core_at, y),
            row(x, core_at, 1 - y),
            row(1 - x, core_at, 1 - y),
            row(1 - x, core_at, 1 - y) + half,
        ]
    return mine + peers, jnp.stack(offs).astype(jnp.int32)


def gather_small(packed, fast):
    if not fast:
        return lax.all_gather(packed, ("fsdp", "ctx"), axis=1, tiled=True)
    x, core, y = place()

    def join(array, other, bit):
        return jnp.where(
            bit == 0, jnp.stack([array, other]), jnp.stack([other, array])
        )

    held = join(packed, swap_y(packed), y)
    held = join(held, swap_core(held), core)
    held = join(held, swap_x(held), x)
    rows, cols = packed.shape
    return held.reshape(8, rows, cols).transpose(1, 0, 2).reshape(rows, 8 * cols)


def reduce_small(sums, fast):
    if not fast:
        part = lax.psum_scatter(sums, ("fsdp", "ctx"), scatter_dimension=1, tiled=True)
        return lax.psum(part, "tp")
    x, core, y = place()
    rows, width = sums.shape
    held = sums.reshape(rows, 2, 2, 2, width // 8).transpose(1, 2, 3, 0, 4)
    for bit, swap in ((x, swap_x), (core, swap_core), (y, swap_y)):
        keep = jnp.where(bit == 0, held[0], held[1])
        send = jnp.where(bit == 0, held[1], held[0])
        held = keep + swap(send)
    tensor_size = lax.axis_size("tp")
    step = 1
    while step < tensor_size:
        held = held + lax.ppermute(held, "tp", pairs_of("tp", step))
        step *= 2
    return held


def tensor_sum(part):
    return lax.psum(part, "tp")


def weight_grads(lefts, rights, pairs, fast, name):
    n_left, n_right = len(lefts), len(rights)
    columns = rights[0].shape[1]
    tokens, width = lefts[0].shape
    if not fast:
        whole = jnp.stack([mm(lefts[a], rights[b], TN).astype(BF) for a, b in pairs])
        return lax.psum_scatter(
            whole, ("fsdp", "ctx"), scatter_dimension=1, tiled=True
        ).astype(F32)
    own = list(lefts) + list(rights)
    peer = [swap_core(array) for array in own]
    rows = width // 8
    half = rows // 2
    x, core, y = place()
    ids = jnp.stack(
        [
            ((x_at * 2 + core) * 2 + y_at) * rows
            for x_at, y_at in ((1 - x, 1 - y), (1 - x, y), (x, 1 - y), (x, y))
        ]
    ).astype(jnp.int32)
    k = len(pairs)
    block = (k, half, columns)
    outs = [
        shape((2,) + block, BF),
        shape((2,) + block, BF),
        shape((2,) + block, BF),
        shape(block, BF),
        shape(block, BF),
    ]
    scratch = [pltpu.VMEM((2 * tokens, array.shape[1]), BF) for array in own]
    scratch += [
        pltpu.VMEM((8,) + block, BF),
        pltpu.SemaphoreType.DMA((n_left + n_right, 2)),
        pltpu.SemaphoreType.DMA((4, 2)),
    ]
    own_sum, x1, y1, x2, y2 = call(
        functools.partial(weight_grad_body, n_left, n_right, pairs),
        outs,
        [ids] + own + peer,
        [spec_smem()] + [spec_any()] * (2 * len(own)),
        scratch,
        2 * 2 * tokens * (4 * rows) * columns * k,
        name,
        [spec_any()] * 5,
    )
    got_x1 = swap_x(x1)
    got_y1 = swap_y(y1)
    got_x2 = swap_x((x2.astype(F32) + got_y1[0].astype(F32)).astype(BF))
    got_y2 = swap_y((y2.astype(F32) + got_x1[0].astype(F32)).astype(BF))
    low = own_sum[0].astype(F32) + got_x1[1].astype(F32) + got_y2.astype(F32)
    high = own_sum[1].astype(F32) + got_y1[1].astype(F32) + got_x2.astype(F32)
    return jnp.concatenate([low, high], axis=1)


def layout(lengths, first_row, row_count):
    token_index = first_row + jnp.arange(row_count, dtype=jnp.int32)
    doc_ends = jnp.cumsum(lengths)
    starts = doc_ends - lengths
    segment = jnp.sum(
        (token_index[:, None] >= doc_ends[None, :]).astype(jnp.int32), axis=1, dtype=jnp.int32
    )
    doc_begin = jnp.max(
        jnp.where(token_index[:, None] >= starts[None, :], starts[None, :], 0), axis=1
    )
    return (segment, token_index - doc_begin, token_index)


def rotary_tables(position):
    frequency = 10000.0 ** (-jnp.arange(0, ROT, 2, dtype=F32) / ROT)
    angles = position.astype(F32)[:, None] * frequency[None, :]
    cos, sin = jnp.cos(angles), jnp.sin(angles)
    rows = position.shape[0]
    blank = jnp.zeros((rows, ROT // 2), F32)
    rest = HD - ROT
    keep = jnp.concatenate([cos, cos, jnp.ones((rows, rest), F32)], axis=1)
    below = jnp.concatenate([blank, sin, jnp.zeros((rows, rest), F32)], axis=1)
    above = jnp.concatenate([-sin, blank, jnp.zeros((rows, rest), F32)], axis=1)
    return jnp.stack([jnp.tile(t, (1, LANES // HD)) for t in (keep, below, above)])


def local(
    tokens,
    cotangent,
    doc_lengths,
    norm_gains,
    norm_biases,
    qkv_weight,
    qkv_bias,
    out_weight,
    gate_up_weight,
    down_weight,
):
    rows = tokens.shape[1]
    width = tokens.shape[2]
    heads_width = qkv_weight.shape[3]
    hidden_width = gate_up_weight.shape[3]
    heads = heads_width // HD
    layers = norm_gains.shape[0]
    ctx_size = lax.axis_size("ctx")
    fast = lax.axis_size("fsdp") == 4 and ctx_size == 2
    ctx_rank = lax.axis_index("ctx")
    tensor_rank = lax.axis_index("tp")

    small = jnp.concatenate(
        [
            norm_gains.reshape(2 * layers, -1),
            norm_biases.reshape(2 * layers, -1),
            qkv_bias.reshape(3 * layers, -1),
        ]
    )
    small = gather_small(small, fast).astype(F32)
    gains = small[: 2 * layers].reshape(layers, 2, width)
    shifts = small[2 * layers : 4 * layers].reshape(layers, 2, width)
    biases = lax.dynamic_slice_in_dim(
        small[4 * layers :], tensor_rank * heads_width, heads_width, 1
    ).reshape(layers, 3, heads_width)
    attn_groups, mlp_groups = [], []
    for layer in range(layers):
        attn_groups.append(
            gather_pieces(
                jnp.concatenate(
                    [qkv_weight[layer].transpose(1, 0, 2), out_weight[layer].T[None]]
                ),
                fast,
            )
        )
        mlp_groups.append(
            gather_pieces(
                jnp.concatenate(
                    [gate_up_weight[layer].transpose(1, 0, 2), down_weight[layer].T[None]]
                ),
                fast,
            )
        )

    lengths = doc_lengths[0]
    seg_query, pos_query, index_query = layout(lengths, ctx_rank * rows, rows)
    tables = rotary_tables(pos_query)

    def mask_of(first, count, usable):
        seg_key, _, index_key = layout(lengths, first, count)
        allowed = (seg_query[None, :] == seg_key[:, None]) & (
            index_query[None, :] >= index_key[:, None]
        )
        return jnp.where(allowed & usable, 0.0, -1e30).astype(F32)

    if fast:
        masks = [
            mask_of(jnp.int32(0), rows, ctx_rank > 0),
            mask_of(ctx_rank * rows, rows, True),
        ]
    else:
        masks = [mask_of(jnp.int32(0), rows * ctx_size, True)]
    n_blocks = len(masks)

    def weight_scratch(count, columns, n_pieces):
        return [
            pltpu.VMEM((count, width, columns), BF),
            pltpu.SemaphoreType.DMA((count, n_pieces)),
        ]

    base, delta = tokens[0], None
    saved = []
    for layer in range(layers):
        pieces, offs = attn_groups[layer]
        n_pieces = len(pieces)
        args = [offs, base] + ([] if delta is None else [delta])
        args += [gains[layer, 0][None], shifts[layer, 0][None], biases[layer], tables]
        outs = [] if delta is None else [shape((rows, width), F32)]
        outs += [shape((rows, width), BF)] + [shape((rows, heads_width), BF)] * 3
        results = call(
            functools.partial(qkv_body, n_pieces, delta is not None),
            outs,
            args + pieces,
            [spec_smem()] + [spec_vmem()] * (len(args) - 1) + [spec_any()] * n_pieces,
            weight_scratch(3, heads_width, n_pieces),
            2 * rows * width * heads_width * 3,
            "qkv",
        )
        stream = base if delta is None else results[0]
        first_in, queries, keys, values = results[-4:]
        if fast:
            kv = jnp.stack([keys, values])
            prev = lax.ppermute(kv, "ctx", [(0, 1)])
            key_blocks, value_blocks = [prev[0], keys], [prev[1], values]
        else:
            kv = lax.all_gather(jnp.stack([keys, values]), "ctx", axis=1, tiled=True)
            key_blocks, value_blocks = [kv[0]], [kv[1]]
        args = [offs, queries] + key_blocks + value_blocks + masks
        mixed, log_total, part = call(
            functools.partial(attend_body, n_pieces, n_blocks),
            [
                shape((rows, heads_width), BF),
                shape((heads, rows), F32),
                shape((rows, width), BF),
            ],
            args + pieces,
            [spec_smem()] + [spec_vmem()] * (len(args) - 1) + [spec_any()] * n_pieces,
            weight_scratch(1, heads_width, n_pieces),
            2 * rows * width * heads_width + 4 * rows * rows * n_blocks * heads_width,
            "attend",
        )
        delta = tensor_sum(part)
        pieces, offs = mlp_groups[layer]
        n_pieces = len(pieces)
        args = [offs, stream, delta, gains[layer, 1][None], shifts[layer, 1][None]]
        mid, second_in, gate, up, hidden, part = call(
            functools.partial(mlp_body, n_pieces),
            [
                shape((rows, width), F32),
                shape((rows, width), BF),
                shape((rows, hidden_width), BF),
                shape((rows, hidden_width), BF),
                shape((rows, hidden_width), BF),
                shape((rows, width), BF),
            ],
            args + pieces,
            [spec_smem()] + [spec_vmem()] * 4 + [spec_any()] * n_pieces,
            weight_scratch(3, hidden_width, n_pieces),
            2 * rows * width * hidden_width * 3,
            "mlp",
        )
        delta = tensor_sum(part)
        saved.append(
            (stream, first_in, queries, key_blocks, value_blocks, mixed, log_total)
            + (mid, second_in, gate, up, hidden)
        )
        base = mid
    output = (base + delta.astype(F32)).astype(BF)[None]

    grad_stream = cotangent[0]
    grads = [None] * layers
    sums = [None] * layers
    on_first = (tensor_rank == 0).astype(F32)
    for layer in reversed(range(layers)):
        (stream, first_in, queries, key_blocks, value_blocks, mixed, log_total) = saved[layer][:7]
        (mid, second_in, gate, up, hidden) = saved[layer][7:]
        pieces, offs = mlp_groups[layer]
        n_pieces = len(pieces)
        d_mlp, d_gate, d_up, part = call(
            functools.partial(mlp_back_body, n_pieces),
            [
                shape((rows, width), BF),
                shape((rows, hidden_width), BF),
                shape((rows, hidden_width), BF),
                shape((rows, width), BF),
            ],
            [offs, grad_stream, gate, up] + pieces,
            [spec_smem()] + [spec_vmem()] * 3 + [spec_any()] * n_pieces,
            weight_scratch(3, hidden_width, n_pieces),
            2 * rows * width * hidden_width * 3,
            "mlp_back",
        )
        d_second = tensor_sum(part)
        mlp_grad = weight_grads(
            [second_in, d_mlp], [d_gate, d_up, hidden], ((0, 0), (0, 1), (1, 2)), fast, "mlp_grads"
        )
        pieces, offs = attn_groups[layer]
        n_pieces = len(pieces)
        args = [offs, mid, d_second, gains[layer, 1][None], grad_stream, tables, queries]
        args += [log_total] + key_blocks + value_blocks + masks
        kv_outs = [shape((2,) + block.shape, BF) for block in key_blocks]
        if fast:
            kv_outs[-1] = shape((2, rows, heads_width), F32)
        results = call(
            functools.partial(attend_back_body, n_pieces, n_blocks),
            [
                shape((rows, width), F32),
                shape((rows, width), BF),
                shape((2, width), F32),
                shape((rows, heads_width), BF),
            ]
            + kv_outs,
            args + pieces,
            [spec_smem()] + [spec_vmem()] * (len(args) - 1) + [spec_any()] * n_pieces,
            weight_scratch(1, heads_width, n_pieces)[:1]
            + [pltpu.VMEM((rows, heads_width), BF)]
            + weight_scratch(1, heads_width, n_pieces)[1:],
            2 * rows * width * heads_width + 10 * rows * rows * n_blocks * heads_width,
            "attend_back",
        )
        grad_mid, d_attn, sums_two, d_query = results[:4]
        if fast:
            own = results[5]
            other = [lax.ppermute(results[4], "ctx", [(1, 0)])]
        else:
            own = lax.psum_scatter(results[4], "ctx", scatter_dimension=1, tiled=True)
            other = []
        args = [offs, d_query, own] + other + [tables, stream, gains[layer, 0][None]]
        d_qkv, bias_sums, part, sums_one = call(
            functools.partial(qkv_back_body, n_pieces, fast),
            [
                shape((3, rows, heads_width), BF),
                shape((3, heads_width), F32),
                shape((rows, width), BF),
                shape((2, width), F32),
            ],
            args + pieces,
            [spec_smem()] + [spec_vmem()] * (len(args) - 1) + [spec_any()] * n_pieces,
            weight_scratch(3, heads_width, n_pieces),
            2 * rows * width * heads_width * 3,
            "qkv_back",
        )
        d_first = tensor_sum(part)
        attn_grad = weight_grads(
            [first_in, d_attn],
            [d_qkv[0], d_qkv[1], d_qkv[2], mixed],
            ((0, 0), (0, 1), (0, 2), (1, 3)),
            fast,
            "attn_grads",
        )
        (grad_stream,) = call(
            norm_back_body,
            [shape((rows, width), F32)],
            [stream, d_first, gains[layer, 0][None], grad_mid],
            [spec_vmem()] * 4,
            [],
            20 * rows * width,
            "norm_back",
        )
        bias_rows = lax.dynamic_update_slice_in_dim(
            jnp.zeros((3, width), F32), bias_sums, tensor_rank * heads_width, 1
        )
        sums[layer] = jnp.concatenate(
            [
                sums_one[0:1],
                sums_two[0:1] * on_first,
                sums_one[1:2],
                sums_two[1:2] * on_first,
                bias_rows,
            ]
        )
        grads[layer] = (
            attn_grad[:3].transpose(1, 0, 2),
            attn_grad[3].T,
            mlp_grad[:2].transpose(1, 0, 2),
            mlp_grad[2].T,
        )
    totals = reduce_small(jnp.concatenate(sums), fast).reshape(layers, 7, -1)
    stacked = [jnp.stack([terms[member] for terms in grads]) for member in range(4)]
    return (
        output,
        grad_stream[None],
        totals[:, 0:2],
        totals[:, 2:4],
        stacked[0],
        totals[:, 4:7],
        stacked[1],
        stacked[2],
        stacked[3],
    )


def solution(mesh):
    return jax.shard_map(
        local,
        mesh=mesh,
        in_specs=(
            P("fsdp", "ctx", None),
            P("fsdp", "ctx", None),
            P("fsdp", None),
            P(None, None, ("fsdp", "ctx")),
            P(None, None, ("fsdp", "ctx")),
            P(None, ("fsdp", "ctx"), None, "tp"),
            P(None, None, ("fsdp", "ctx")),
            P(None, "tp", ("fsdp", "ctx")),
            P(None, ("fsdp", "ctx"), None, "tp"),
            P(None, "tp", ("fsdp", "ctx")),
        ),
        out_specs=(
            P("fsdp", "ctx", None),
            P("fsdp", "ctx", None),
            P(None, None, ("fsdp", "ctx")),
            P(None, None, ("fsdp", "ctx")),
            P(None, ("fsdp", "ctx"), None, "tp"),
            P(None, None, ("fsdp", "ctx")),
            P(None, "tp", ("fsdp", "ctx")),
            P(None, ("fsdp", "ctx"), None, "tp"),
            P(None, "tp", ("fsdp", "ctx")),
        ),
        check_vma=False,
    )
```

```python
import functools

import jax
import jax.numpy as jnp
from jax import lax
from jax.experimental import pallas as pl
from jax.experimental.pallas import tpu as pltpu
from jax.sharding import PartitionSpec as P

HD = 64
ROT = 16
LANES = 128
SCALE = 1.0 / HD**0.5
VMEM_LIMIT = 50 * 1024 * 1024
NN = (((1,), (0,)), ((), ()))
NT = (((1,), (1,)), ((), ()))
TN = (((0,), (0,)), ((), ()))
BF = jnp.bfloat16
F32 = jnp.float32
EACH = -1
TIMES = {
    "pack": 7.0,
    "qkv": 8.5,
    "attend": 8.0,
    "norm": 3.0,
    "mlp": 11.5,
    "mlp_back": 14.0,
    "norm_back": 3.5,
    "attend_back": 10.0,
    "qkv_back": 9.0,
    "mlp_grads": 10.5,
    "attn_grads": 7.0,
    "mlp_add": 4.0,
    "attn_add": 3.0,
    "mlp_finish": 7.5,
    "attn_finish": 4.5,
    "sum": 3.0,
}


def cost(name):
    return pl.CostEstimate(flops=0, bytes_accessed=int(TIMES[name] * 3.0e6), transcendentals=0)


def mm(lhs, rhs, dims):
    return lax.dot_general(lhs, rhs, dims, preferred_element_type=F32)


def shape(dims, dtype):
    return jax.ShapeDtypeStruct(tuple(dims), dtype)


class Free:
    def __init__(self, array):
        self.array = array


class Io:
    def __init__(self, ins, loads, outs, stores, held, weights, started, extra):
        self.ins, self.loads, self.outs, self.stores = ins, loads, outs, stores
        self.held, self.weights, self.started, self.extra = held, weights, started, extra
        self.there, self.gone = set(), []

    def get(self, index):
        if index not in self.there:
            self.loads[index].wait()
            self.there.add(index)
        return self.ins[index]

    def weight(self, slot):
        for copy in self.weights[slot]:
            copy.wait()
        self.begin(slot + 2)
        return self.held[slot]

    def begin(self, count):
        while self.started < min(count, len(self.weights)):
            for copy in self.weights[self.started]:
                copy.start()
            self.started += 1

    def put(self, index):
        for copy in self.stores[index]:
            copy.start()
            self.gone.append(copy)


def kernel(body, name, spots, loads, outs, slots=(), eager=1, extra=(), reuse=()):
    free = [isinstance(item, Free) for item in loads]
    loads = [item.array if isinstance(item, Free) else item for item in loads]
    loads = [item if isinstance(item, tuple) else (item, None) for item in loads]
    outs = [item if isinstance(item, tuple) else (item, None) for item in outs]
    pieces, place_of = [], {}
    for group, _, _ in slots:
        for piece in group:
            if id(piece) not in place_of:
                place_of[id(piece)] = len(pieces)
                pieces.append(piece)
    slot_at = [([place_of[id(piece)] for piece in group], m, at) for group, m, at in slots]
    out_shapes = [item[0] for item in outs]
    n_in, n_piece, n_reuse = len(loads), len(pieces), len(reuse)

    def part(item):
        return tuple(item[0].shape) if item[1] is None else tuple(item[0].shape[1:])

    def view(ref, index):
        return ref if index is None else ref.at[index]

    def run(*refs):
        refs = list(refs)

        def take(count):
            taken = refs[:count]
            del refs[:count]
            return taken

        starts = take(1)[0]
        in_hbm, piece_hbm, _ = take(n_in), take(n_piece), take(n_reuse)
        out_hbm = take(len(out_shapes))
        ins, results, held = take(n_in), take(len(outs)), take(len(slots))
        in_sems, out_sems = take(2)
        slot_sems = take(len(slots))
        load_copies = [
            pltpu.make_async_copy(view(ref, index), ins[at], in_sems.at[at])
            for at, (ref, (_, index)) in enumerate(zip(in_hbm, loads, strict=True))
        ]
        for copy in load_copies:
            copy.start()
        weight_sets = []
        for slot, (members, matrix, first) in enumerate(slot_at):
            copies = []
            for number, member in enumerate(members):
                piece = piece_hbm[member]
                row = pl.multiple_of(starts[first + number], 64)
                copies.append(
                    pltpu.make_async_copy(
                        piece.at[matrix],
                        held[slot].at[pl.ds(row, piece.shape[1]), :],
                        slot_sems[slot].at[number],
                    )
                )
            weight_sets.append(copies)
        stores = []
        for at, (ref, (_, index)) in enumerate(zip(out_hbm, outs, strict=True)):
            if index == EACH:
                stores.append(
                    [
                        pltpu.make_async_copy(results[at], ref.at[each], out_sems.at[at, each])
                        for each in range(ref.shape[0])
                    ]
                )
            else:
                stores.append(
                    [pltpu.make_async_copy(results[at], view(ref, index), out_sems.at[at, 0])]
                )
        io = Io(ins, load_copies, results, stores, held, weight_sets, 0, refs)
        io.begin(eager)
        body(io)
        for at in range(n_in):
            io.get(at)
        for copy in io.gone:
            copy.wait()

    def in_hbm_now(array):
        return pltpu.with_memory_space_constraint(array, pltpu.HBM)

    args = [spots]
    args += [a if any_place else in_hbm_now(a) for (a, _), any_place in zip(loads, free, strict=True)]
    args += [in_hbm_now(piece) for piece in pieces]
    aliases = {len(args) + at: out for at, (_, out) in enumerate(reuse)}
    args += [in_hbm_now(array) for array, _ in reuse]
    hbm = pl.BlockSpec(memory_space=pltpu.HBM)
    most = max([out.shape[0] for out, index in outs if index == EACH], default=1)
    scratch = [pltpu.VMEM(part(item), item[0].dtype) for item in loads]
    scratch += [pltpu.VMEM(part(item), item[0].dtype) for item in outs]
    scratch += [
        pltpu.VMEM((sum(piece.shape[1] for piece in group), group[0].shape[2]), group[0].dtype)
        for group, _, _ in slots
    ]
    scratch += [
        pltpu.SemaphoreType.DMA((max(n_in, 1),)),
        pltpu.SemaphoreType.DMA((len(outs), most)),
    ]
    scratch += [pltpu.SemaphoreType.DMA((len(group),)) for group, _, _ in slots]
    return pl.pallas_call(
        run,
        out_shape=[pltpu.HBM(out.shape, out.dtype) for out in out_shapes],
        in_specs=[pl.BlockSpec(memory_space=pltpu.SMEM)]
        + [pl.BlockSpec(memory_space=pl.ANY) if any_place else hbm for any_place in free]
        + [hbm] * (n_piece + n_reuse),
        out_specs=[hbm] * len(out_shapes),
        scratch_shapes=scratch + list(extra),
        input_output_aliases=aliases,
        compiler_params=pltpu.CompilerParams(vmem_limit_bytes=VMEM_LIMIT),
        cost_estimate=cost(name),
        name=name,
    )(*args)


def normalized(v):
    centered = v - jnp.mean(v, axis=1, keepdims=True)
    variance = jnp.mean(centered * centered, axis=1, keepdims=True)
    scale = lax.rsqrt(variance + 1e-05)
    return centered * scale, scale


def norm_back(v, cot, gain):
    n, scale = normalized(v)
    e = cot * gain
    grad = scale * (
        e - jnp.mean(e, axis=1, keepdims=True) - n * jnp.mean(e * n, axis=1, keepdims=True)
    )
    return grad, n


def turn_wide(wide, tables, sign):
    keep, below, above = tables[0], tables[1], tables[2]
    turned = []
    for at in range(0, wide.shape[1], LANES):
        tile = wide[:, at : at + LANES]
        moved = pltpu.roll(tile, 8, 1) * below + pltpu.roll(tile, LANES - 8, 1) * above
        turned.append(tile * keep + sign * moved)
    return jnp.concatenate(turned, axis=1)


def total_of(terms):
    return functools.reduce(jnp.add, terms)


def qkv_body(has_norm, io):
    queries, kv = io.outs[:2]
    if has_norm:
        first_in = io.outs[2]
        n, _ = normalized(io.get(4)[...].astype(F32))
        first_in[...] = (n * io.get(2)[...] + io.get(3)[...]).astype(BF)
        io.put(2)
    else:
        first_in = io.get(2)
    bias, tables = io.get(0), io.get(1)
    for slot, index in enumerate((1, 2, 0)):
        part = mm(first_in[...], io.weight(slot)[...], NN) + bias[index : index + 1, :]
        if index < 2:
            part = turn_wide(part, tables, 1.0)
        if index == 0:
            queries[...] = part.astype(BF)
        else:
            kv[index - 1] = part.astype(BF)
    io.put(1)
    io.put(0)


def attend_body(n_blocks, io):
    queries = io.get(0)
    kvs = [io.get(1 + at) for at in range(n_blocks)]
    masks = [io.get(1 + n_blocks + at) for at in range(n_blocks)]
    mixed, log_total, part = io.outs
    for head in range(queries.shape[1] // HD):
        span = slice(head * HD, (head + 1) * HD)
        query = queries[:, span]
        scores = [
            mm(kv[0, :, span], query, NT) * SCALE + mask[...]
            for kv, mask in zip(kvs, masks, strict=True)
        ]
        top = functools.reduce(jnp.maximum, [jnp.max(s, axis=0, keepdims=True) for s in scores])
        exps = [jnp.exp(s - top) for s in scores]
        total = total_of([jnp.sum(e, axis=0, keepdims=True) for e in exps])
        inverse = 1.0 / total
        result = total_of(
            [
                mm((e * inverse).astype(BF), kv[1, :, span], TN)
                for e, kv in zip(exps, kvs, strict=True)
            ]
        )
        log_total[head : head + 1, :] = top + jnp.log(total)
        mixed[:, span] = result.astype(BF)
    io.put(0)
    io.put(1)
    part[...] = mm(mixed[...], io.weight(0)[...], NT).astype(BF)
    io.put(2)


def terms_sum(terms):
    return total_of([terms[at].astype(F32) for at in range(terms.shape[0])])


def norm_body(io):
    stream = terms_sum(io.get(0)) + io.get(1)[...].astype(F32)
    io.outs[0][...] = stream
    io.put(0)
    n, _ = normalized(stream)
    io.outs[1][...] = (n * io.get(2)[...] + io.get(3)[...]).astype(BF)
    io.put(1)


def sum_body(io):
    io.outs[0][...] = (terms_sum(io.get(0)) + io.get(1)[...].astype(F32)).astype(BF)
    io.put(0)


def mlp_body(io):
    gate_out, up_out, hidden, part = io.outs
    second_in = io.get(0)
    gate = mm(second_in[...], io.weight(0)[...], NN)
    gate_out[...] = gate.astype(BF)
    io.put(0)
    act = gate * jax.nn.sigmoid(gate)
    up = mm(second_in[...], io.weight(1)[...], NN)
    up_out[...] = up.astype(BF)
    io.put(1)
    hidden[...] = (act * up).astype(BF)
    io.put(2)
    part[...] = mm(hidden[...], io.weight(2)[...], NT).astype(BF)
    io.put(3)


def mlp_back_body(io):
    d_gate_up, part = io.outs
    d_mlp = io.get(2)
    gate = io.get(0)[...].astype(F32)
    sig = jax.nn.sigmoid(gate)
    d_hidden = mm(d_mlp[...], io.weight(0)[...], NN)
    d_gate_up[1] = (d_hidden * (gate * sig)).astype(BF)
    d_gate_up[0] = (
        d_hidden * io.get(1)[...].astype(F32) * (sig * (1.0 + gate * (1.0 - sig)))
    ).astype(BF)
    io.put(0)
    total = mm(d_gate_up[0], io.weight(1)[...], NT)
    total = total + mm(d_gate_up[1], io.weight(2)[...], NT)
    part[...] = total.astype(BF)
    io.put(1)


def norm_back_body(io):
    c = terms_sum(io.get(0))
    grad, n = norm_back(io.get(1)[...].astype(F32), c, io.get(2)[...])
    grad = io.get(3)[...].astype(F32) + grad
    io.outs[0][...] = grad
    io.put(0)
    io.outs[1][...] = grad.astype(BF)
    io.put(1)
    io.outs[2][0:1, :] = jnp.sum(n * c, axis=0, keepdims=True)
    io.outs[2][1:2, :] = jnp.sum(c, axis=0, keepdims=True)
    io.put(2)


def attend_back_body(n_blocks, io):
    d_query, d_kvs = io.outs[0], io.outs[1:]
    d_mixed = io.extra[0]
    d_mixed[...] = mm(io.get(0)[...], io.weight(0)[...], NN).astype(BF)
    queries, log_total, tables = io.get(1), io.get(2), io.get(3)
    kvs = [io.get(4 + at) for at in range(n_blocks)]
    masks = [io.get(4 + n_blocks + at) for at in range(n_blocks)]
    pair = []
    for head in range(queries.shape[1] // HD):
        span = slice(head * HD, (head + 1) * HD)
        query = queries[:, span]
        d_out = d_mixed[:, span]
        row_log = log_total[head : head + 1, :]
        probs = [
            jnp.exp(mm(kv[0, :, span], query, NT) * SCALE + mask[...] - row_log)
            for kv, mask in zip(kvs, masks, strict=True)
        ]
        d_probs = [mm(kv[1, :, span], d_out, NT) for kv in kvs]
        delta = total_of(
            [jnp.sum(p * dp, axis=0, keepdims=True) for p, dp in zip(probs, d_probs, strict=True)]
        )
        d_scores = [
            (p * (dp - delta)).astype(BF) for p, dp in zip(probs, d_probs, strict=True)
        ]
        pair.append(
            total_of([mm(ds, kv[0, :, span], TN) for ds, kv in zip(d_scores, kvs, strict=True)])
            * SCALE
        )
        if len(pair) == LANES // HD:
            wide = slice((head + 1) * HD - LANES, (head + 1) * HD)
            d_query[:, wide] = turn_wide(jnp.concatenate(pair, axis=1), tables, -1.0).astype(BF)
            pair = []
        for ds, p, d_kv in zip(d_scores, probs, d_kvs, strict=True):
            d_kv[0, :, span] = (mm(ds, query, NN) * SCALE).astype(d_kv.dtype)
            d_kv[1, :, span] = mm(p.astype(BF), d_out, NN).astype(d_kv.dtype)
    for at in range(1 + n_blocks):
        io.put(at)


def qkv_back_body(n_other, io):
    d_qkv, bias, part = io.outs
    tables = io.get(1)
    terms = [io.get(2 + at) for at in range(1 + n_other)]
    d_qkv[0] = io.get(0)[...]
    d_qkv[1] = turn_wide(
        total_of([term[0].astype(F32) for term in terms]), tables, -1.0
    ).astype(BF)
    d_qkv[2] = total_of([term[1].astype(F32) for term in terms]).astype(BF)
    io.put(0)
    for index in range(3):
        bias[index : index + 1, :] = jnp.sum(d_qkv[index].astype(F32), axis=0, keepdims=True)
    io.put(1)
    part[...] = total_of(
        [mm(d_qkv[index], io.weight(index)[...], NT) for index in range(3)]
    ).astype(BF)
    io.put(2)


def pack_body(io):
    gate_up, down = io.get(0), io.get(1)
    for part in range(2):
        io.outs[part][0] = gate_up[:, part, :]
        io.put(part)
    io.outs[2][0] = down[...].T
    io.put(2)


def add_body(io):
    io.outs[0][...] = (io.get(0)[...].astype(F32) + io.get(2)[...].astype(F32)).astype(BF)
    io.put(0)
    io.outs[1][...] = (io.get(1)[...].astype(F32) + io.get(3)[...].astype(F32)).astype(BF)
    io.put(1)


def finish_body(is_mlp, io):
    own, x1, y1, x2, y2 = (io.get(at) for at in range(5))
    half = own.shape[2]
    main, other = io.outs
    matrices = own.shape[1]
    for side, (one, two) in enumerate(((x1, y2), (y1, x2))):
        rows = slice(side * half, (side + 1) * half)
        for matrix in range(matrices):
            whole = (
                own[side, matrix].astype(F32) + one[matrix].astype(F32) + two[matrix].astype(F32)
            )
            if matrix == matrices - 1:
                other[:, rows] = whole.T
            elif is_mlp:
                main[rows, matrix, :] = whole
            else:
                main[matrix, rows, :] = whole
    io.put(0)
    io.put(1)


def weight_grad_body(counts, n_left, pairs, *refs):
    ids = refs[0]
    n_in, n_held = len(counts), sum(counts)
    own = refs[1 : 1 + n_in]
    peer = refs[1 + n_in : 1 + 2 * n_in]
    outs = refs[1 + 2 * n_in : 6 + 2 * n_in]
    held = refs[6 + 2 * n_in : 6 + 2 * n_in + n_held]
    stage, in_sems, out_sems = refs[6 + 2 * n_in + n_held :]
    rows = held[0].shape[0] // 2
    loads = []
    for part, side in enumerate((own, peer)):
        at = 0
        for source, count in zip(side, counts, strict=True):
            for index in range(count):
                copy = pltpu.make_async_copy(
                    source if len(source.shape) == 2 else source.at[index],
                    held[at].at[pl.ds(part * rows, rows), :],
                    in_sems.at[at, part],
                )
                copy.start()
                loads.append(copy)
                at += 1
    for copy in loads:
        copy.wait()
    half = stage.shape[2]
    own_out, x1, y1, x2, y2 = outs
    targets = (
        (x1.at[0], y1.at[0]),
        (x1.at[1], x2),
        (y2, y1.at[1]),
        (own_out.at[0], own_out.at[1]),
    )
    stores = []
    for block in range(4):
        start = pl.multiple_of(ids[block], LANES)
        for matrix, (left, right) in enumerate(pairs):
            lhs = held[left][:, pl.ds(start, 2 * half)]
            result = mm(lhs, held[n_left + right][...], TN).astype(BF)
            stage[2 * block, matrix] = result[:half]
            stage[2 * block + 1, matrix] = result[half:]
        for part in range(2):
            copy = pltpu.make_async_copy(
                stage.at[2 * block + part], targets[block][part], out_sems.at[block, part]
            )
            copy.start()
            stores.append(copy)
    for copy in stores:
        copy.wait()


def after(array, *earlier):
    return lax.optimization_barrier((array,) + earlier)[0]


def pairs_of(axis, bit):
    return [(index, index ^ bit) for index in range(lax.axis_size(axis))]


def swap_x(array):
    return lax.ppermute(array, "fsdp", pairs_of("fsdp", 2))


def swap_core(array):
    return lax.ppermute(array, "fsdp", pairs_of("fsdp", 1))


def swap_y(array):
    return lax.ppermute(array, "ctx", pairs_of("ctx", 1))


def place():
    fsdp = lax.axis_index("fsdp")
    return fsdp // 2, fsdp % 2, lax.axis_index("ctx")


class Gather:
    def __init__(self, shard):
        self.shard = shard
        self.rows = shard.shape[1]

    def near_x(self, wait=()):
        self.from_x = swap_x(after(self.shard, *wait))

    def near_y(self, wait=()):
        self.from_y = swap_y(after(self.shard, *wait))
        self.mine = [self.shard, self.from_x, self.from_y]

    def near(self, wait_x=(), wait_y=()):
        self.near_x(wait_x)
        self.near_y(wait_y)

    def swap(self, *wait):
        self.peers = [swap_core(after(piece, *wait)) for piece in self.mine]

    def far(self, way, wait_x=(), wait_y=()):
        half = self.rows // 2
        self.way = way
        if way == "x":
            self.pieces = [swap_x(after(self.from_y, *wait_x))]
        elif way == "y":
            self.pieces = [swap_y(after(self.from_x, *wait_y))]
        else:
            self.pieces = [
                swap_x(after(self.from_y[:, :half], *wait_x)),
                swap_y(after(self.from_x[:, half:], *wait_y)),
            ]

    def all(self):
        far_peers = [swap_core(piece) for piece in self.pieces]
        return self.mine + self.pieces + self.peers + far_peers


def piece_rows(rows):
    x, core, y = place()

    def row(x_at, core_at, y_at):
        return ((x_at * 2 + core_at) * 2 + y_at) * rows

    offs = []
    for halves in (0, 1):
        for core_at in (core, 1 - core):
            offs += [row(x, core_at, y), row(1 - x, core_at, y), row(x, core_at, 1 - y)]
            offs.append(row(1 - x, core_at, 1 - y))
            if halves:
                offs.append(row(1 - x, core_at, 1 - y) + rows // 2)
    return offs


def gather_whole(shard):
    return [lax.all_gather(shard, ("fsdp", "ctx"), axis=1, tiled=True)]


def gather_small(packed, fast):
    if not fast:
        return lax.all_gather(packed, ("fsdp", "ctx"), axis=1, tiled=True)
    x, core, y = place()

    def join(array, other, bit):
        return jnp.where(bit == 0, jnp.stack([array, other]), jnp.stack([other, array]))

    held = join(packed, swap_core(packed), core)
    held = join(held, swap_x(held), x)
    held = join(held, swap_y(held), y)
    rows, cols = packed.shape
    return held.transpose(3, 1, 2, 0, 4).reshape(rows, 8 * cols)


def reduce_small(sums, fast):
    if not fast:
        part = lax.psum_scatter(sums, ("fsdp", "ctx"), scatter_dimension=1, tiled=True)
        return lax.psum(part, "tp"), part
    x, core, y = place()
    rows, width = sums.shape
    held = sums.reshape(rows, 2, 2, 2, width // 8).transpose(1, 3, 2, 0, 4)
    for bit, swap in ((x, swap_x), (y, swap_y), (core, swap_core)):
        keep = jnp.where(bit == 0, held[0], held[1])
        send = jnp.where(bit == 0, held[1], held[0])
        held = keep + swap(send)
        if swap is swap_y:
            halfway = held
    step = 1
    while step < lax.axis_size("tp"):
        held = held + lax.ppermute(held, "tp", pairs_of("tp", step))
        step *= 2
    return held, halfway


def tensor_scatter(part, *earlier):
    size = lax.axis_size("tp")
    blocks = after(part, *earlier).reshape(size, part.shape[0] // size, part.shape[1])
    return lax.all_to_all(blocks, "tp", 0, 0, tiled=True)


def tensor_gather(copies):
    size, block, width = copies.shape
    return lax.all_to_all(copies, "tp", 0, 0, tiled=True).reshape(size * block, width)


def weight_grads(own, n_left, pairs, earlier, wait, name):
    counts = tuple(1 if array.ndim == 2 else array.shape[0] for array in own)
    columns = own[-1].shape[-1]
    tokens, width = own[0].shape
    peer = [swap_core(after(array, *earlier)) for array in own]
    rows = width // 8
    half = rows // 2
    x, core, y = place()
    ids = jnp.stack(
        [
            ((x_at * 2 + core) * 2 + y_at) * rows
            for x_at, y_at in ((1 - x, 1 - y), (1 - x, y), (x, 1 - y), (x, y))
        ]
    ).astype(jnp.int32)
    block = (len(pairs), half, columns)
    hbm = pl.BlockSpec(memory_space=pltpu.HBM)
    scratch = [
        pltpu.VMEM((2 * tokens, array.shape[-1]), BF)
        for array, count in zip(own, counts, strict=True)
        for _ in range(count)
    ]
    scratch += [
        pltpu.VMEM((8,) + block, BF),
        pltpu.SemaphoreType.DMA((sum(counts), 2)),
        pltpu.SemaphoreType.DMA((4, 2)),
    ]
    own_sum, x1, y1, x2, y2 = pl.pallas_call(
        functools.partial(weight_grad_body, counts, n_left, pairs),
        out_shape=[pltpu.HBM((2,) + block, BF)] * 3 + [pltpu.HBM(block, BF)] * 2,
        in_specs=[pl.BlockSpec(memory_space=pltpu.SMEM)] + [hbm] * (2 * len(own)),
        out_specs=[hbm] * 5,
        scratch_shapes=scratch,
        compiler_params=pltpu.CompilerParams(vmem_limit_bytes=VMEM_LIMIT),
        cost_estimate=cost(name),
        name=name,
    )(ids, *[pltpu.with_memory_space_constraint(a, pltpu.HBM) for a in list(own) + peer])
    return (own_sum, x2, y2), (swap_x(after(x1, *wait)), swap_y(after(y1, *wait)))


def reduce_second(spots, parts, received, earlier_add, earlier_send, name):
    own_sum, x2, y2 = parts
    got_x1, got_y1 = received
    block = shape(x2.shape, BF)
    send_x, send_y = kernel(
        add_body,
        name,
        spots,
        [after(x2, *earlier_add), y2, (got_y1, 0), (got_x1, 0)],
        [block, block],
    )
    far_x = swap_x(after(send_x, *earlier_send))
    far_y = swap_y(after(send_y, *earlier_send))
    return [own_sum, (got_x1, 1), (got_y1, 1), far_x, far_y], send_x


def layout(lengths, first_row, row_count):
    token_index = first_row + jnp.arange(row_count, dtype=jnp.int32)
    doc_ends = jnp.cumsum(lengths)
    starts = doc_ends - lengths
    segment = jnp.sum(
        (token_index[:, None] >= doc_ends[None, :]).astype(jnp.int32), axis=1, dtype=jnp.int32
    )
    doc_begin = jnp.max(
        jnp.where(token_index[:, None] >= starts[None, :], starts[None, :], 0), axis=1
    )
    return (segment, token_index - doc_begin, token_index)


def rotary_tables(position):
    frequency = 10000.0 ** (-jnp.arange(0, ROT, 2, dtype=F32) / ROT)
    angles = position.astype(F32)[:, None] * frequency[None, :]
    cos, sin = jnp.cos(angles), jnp.sin(angles)
    rows = position.shape[0]
    blank = jnp.zeros((rows, ROT // 2), F32)
    rest = HD - ROT
    keep = jnp.concatenate([cos, cos, jnp.ones((rows, rest), F32)], axis=1)
    below = jnp.concatenate([blank, sin, jnp.zeros((rows, rest), F32)], axis=1)
    above = jnp.concatenate([-sin, blank, jnp.zeros((rows, rest), F32)], axis=1)
    return jnp.stack([jnp.tile(t, (1, LANES // HD)) for t in (keep, below, above)])


def local(
    tokens,
    cotangent,
    doc_lengths,
    norm_gains,
    norm_biases,
    qkv_weight,
    qkv_bias,
    out_weight,
    gate_up_weight,
    down_weight,
):
    rows = tokens.shape[1]
    width = tokens.shape[2]
    heads_width = qkv_weight.shape[3]
    hidden_width = gate_up_weight.shape[3]
    heads = heads_width // HD
    layers = norm_gains.shape[0]
    block_rows = qkv_weight.shape[1]
    ctx_size = lax.axis_size("ctx")
    fast = lax.axis_size("fsdp") == 4 and ctx_size == 2
    ctx_rank = lax.axis_index("ctx")
    tensor_rank = lax.axis_index("tp")

    small = jnp.concatenate(
        [
            norm_gains.reshape(2 * layers, -1),
            norm_biases.reshape(2 * layers, -1),
            qkv_bias.reshape(3 * layers, -1),
        ]
    )
    small = gather_small(small, fast).astype(F32)
    gains = small[: 2 * layers].reshape(layers, 2, width)
    shifts = small[2 * layers : 4 * layers].reshape(layers, 2, width)
    biases = lax.dynamic_slice_in_dim(
        small[4 * layers :], tensor_rank * heads_width, heads_width, 1
    ).reshape(layers, 3, heads_width)

    tensor_size = lax.axis_size("tp")
    block = rows // tensor_size
    spots = piece_rows(block_rows) if fast else [jnp.int32(0)]
    spots = jnp.stack([jnp.asarray(spot, jnp.int32) for spot in spots])
    spots_at = {8: 0, 10: 8, 1: 0}

    def slot(pieces, matrix):
        return (pieces, matrix, spots_at[len(pieces)])

    shards = []
    for layer in range(layers):
        if fast:
            mlp_shards = kernel(
                pack_body,
                "pack",
                spots,
                [(gate_up_weight, layer), (down_weight, layer)],
                [shape((1, block_rows, hidden_width), BF)] * 3,
            )
        else:
            mlp_shards = [gate_up_weight[layer][None, :, part] for part in range(2)]
            mlp_shards.append(down_weight[layer].T[None])
        shards.append((qkv_weight[layer].transpose(1, 0, 2), out_weight[layer].T[None], *mlp_shards))

    lengths = doc_lengths[0]
    seg_query, pos_query, index_query = layout(lengths, ctx_rank * rows, rows)
    tables = rotary_tables(pos_query)

    def mask_of(first, count, usable):
        seg_key, _, index_key = layout(lengths, first, count)
        allowed = (seg_query[None, :] == seg_key[:, None]) & (
            index_query[None, :] >= index_key[:, None]
        )
        return jnp.where(allowed & usable, 0.0, -1e30).astype(F32)

    if fast:
        masks = [
            mask_of(jnp.int32(0), rows, ctx_rank > 0),
            mask_of(ctx_rank * rows, rows, True),
        ]
    else:
        masks = [mask_of(jnp.int32(0), rows * ctx_size, True)]
    n_blocks = len(masks)

    wide = shape((rows, width), BF)
    inner = shape((rows, hidden_width), BF)
    headed = shape((rows, heads_width), BF)
    block_f = shape((block, width), F32)
    copies_b = (shape((tensor_size, block, width), BF), EACH)

    stream = lax.dynamic_slice_in_dim(tokens[0], tensor_rank * block, block, 0)
    first_in = None
    saved, groups = [], []
    if fast:
        qkv_g, out_g, gate_g, up_g, down_g = (Gather(shard) for shard in shards[0])
        qkv_g.near()
        qkv_g.swap()
        qkv_g.far("both")
        out_g.near(qkv_g.pieces, qkv_g.pieces)
    for layer in range(layers):
        if fast:
            qkv_pieces = qkv_g.all()
        else:
            qkv_pieces, *others = (gather_whole(shard) for shard in shards[layer])
            out_pieces, gate_pieces, up_pieces, down_pieces = others
        outs = [headed, shape((2, rows, heads_width), BF)]
        if layer == 0:
            args = [biases[0], tables, gains[0, 0][None], shifts[0, 0][None], tokens[0]]
            if fast:
                args[0] = after(args[0], gate_g.shard)
            outs.append(wide)
        else:
            args = [biases[layer], tables, Free(first_in)]
        queries, kv, *normed = kernel(
            functools.partial(qkv_body, layer == 0),
            "qkv",
            spots,
            args,
            outs,
            [slot(qkv_pieces, index) for index in (1, 2, 0)],
        )
        if layer == 0:
            first_in = normed[0]
        if fast:
            prev = lax.ppermute(kv, "ctx", [(0, 1)])
            kv_blocks = [prev, kv]
            out_g.swap(queries)
            if layer == 0:
                out_g.far("x", (queries,))
                gate_g.near((*out_g.pieces, out_g.from_x), (prev,))
            else:
                out_g.far("x", (queries, up_g.from_x))
                gate_g.swap(queries)
                gate_g.far("x", (queries, *out_g.pieces))
                up_g.near_y((prev,))
            out_pieces = out_g.all()
        else:
            kv_blocks = [lax.all_gather(kv, "ctx", axis=1, tiled=True)]
        mixed, log_total, part = kernel(
            functools.partial(attend_body, n_blocks),
            "attend",
            spots,
            [queries] + kv_blocks + masks,
            [headed, shape((heads, rows), F32), wide],
            [slot(out_pieces, 0)],
        )
        terms = tensor_scatter(part)
        if fast:
            if layer == 0:
                up_g.near((part, gate_g.from_x), (part, gate_g.from_y))
                gate_g.swap(part)
                gate_g.far("both", (part,), (part,))
            else:
                down_g.near((part, *gate_g.pieces), (part, up_g.from_y))
                up_g.swap(part)
                up_g.far("both", (part,), (part,))
        mid, normed = kernel(
            norm_body,
            "norm",
            spots,
            [Free(terms), stream, gains[layer, 1][None], shifts[layer, 1][None]],
            [block_f, copies_b],
        )
        second_in = tensor_gather(normed)
        if fast:
            if layer == 0:
                down_g.near((mid, gate_g.pieces[0]), (mid, gate_g.pieces[1]))
                up_g.swap(mid)
                up_g.far("both", (mid,), (mid,))
                down_g.swap()
            else:
                down_g.swap(mid)
            down_g.far("both", (mid, up_g.pieces[0]), (mid, up_g.pieces[1]))
            gate_pieces, up_pieces, down_pieces = gate_g.all(), up_g.all(), down_g.all()
        gate, up, hidden, part = kernel(
            mlp_body,
            "mlp",
            spots,
            [Free(second_in)],
            [inner, inner, inner, wide],
            [slot(gate_pieces, 0), slot(up_pieces, 0), slot(down_pieces, 0)],
        )
        saved.append((stream, first_in, queries, kv_blocks, mixed, log_total, mid))
        saved[-1] += (second_in, gate, up, hidden)
        groups.append((qkv_pieces, out_pieces, gate_pieces, up_pieces, down_pieces))
        if layer == layers - 1:
            break
        terms = tensor_scatter(part)
        if fast:
            sent = down_g.pieces
            qkv_g, out_g, gate_g, up_g, down_g = (Gather(shard) for shard in shards[layer + 1])
            qkv_g.near(sent[:1], sent[1:])
            qkv_g.swap(part)
            qkv_g.far("y", (), (part,))
            out_g.near((qkv_g.from_x, part), (qkv_g.pieces[0],))
            gate_g.near((out_g.from_x,), (out_g.from_y,))
            up_g.near_x((gate_g.from_x,))
            terms = after(terms, gate_g.shard)
        stream, normed = kernel(
            norm_body,
            "norm",
            spots,
            [Free(terms), mid, gains[layer + 1, 0][None], shifts[layer + 1, 0][None]],
            [block_f, copies_b],
        )
        first_in = tensor_gather(normed)
    last_part, last_mid = part, mid

    attn_outs, mlp_outs, pending = None, None, None
    sums = [None] * layers
    plain = [None] * layers
    grad = lax.dynamic_slice_in_dim(cotangent[0], tensor_rank * block, block, 0)
    d_mlp = cotangent[0]
    for layer in reversed(range(layers)):
        (stream, first_in, queries, kv_blocks, mixed, log_total, mid) = saved[layer][:7]
        (second_in, gate, up, hidden) = saved[layer][7:]
        qkv_pieces, out_pieces, gate_pieces, up_pieces, down_pieces = groups[layer]
        d_gate_up, part = kernel(
            mlp_back_body,
            "mlp_back",
            spots,
            [gate, up, Free(d_mlp)],
            [shape((2, rows, hidden_width), BF), wide],
            [slot(down_pieces, 0), slot(gate_pieces, 0), slot(up_pieces, 0)],
        )
        terms = tensor_scatter(part)
        pairs = ((0, 0), (0, 1), (1, 2))
        if fast:
            ready, attn_added = [], ()
            if pending is not None:
                attn_terms, attn_added = reduce_second(spots, *pending, (part,), (), "attn_add")
                attn_added = (attn_added,)
                ready += attn_terms[3:]
            mlp_parts, mlp_sent = weight_grads(
                [second_in, d_mlp, d_gate_up, hidden],
                2,
                pairs,
                (part, *attn_added),
                ready,
                "mlp_grads",
            )
            ready.append(mlp_parts[0])
            terms = after(terms, *ready)
        else:
            mlp_grad = plain_grads(
                [second_in, d_mlp], [d_gate_up[0], d_gate_up[1], hidden], pairs
            )
        grad_mid, normed, sums_two = kernel(
            norm_back_body,
            "norm_back",
            spots,
            [Free(terms), mid, gains[layer, 1][None], grad],
            [block_f, copies_b, shape((2, width), F32)],
        )
        d_attn = tensor_gather(normed)
        if pending is not None:
            attn_terms[0] = after(attn_terms[0], grad_mid)
            attn_outs = attn_finish(spots, attn_outs, attn_terms, layer + 1, layers)
            d_attn = after(d_attn, attn_outs[0])
        if layer == layers - 1:
            (summed,) = kernel(
                sum_body, "sum", spots, [tensor_scatter(last_part, d_attn), last_mid], [copies_b]
            )
        elif layer == layers - 2:
            output = tensor_gather(after(summed, d_attn))
        kv_outs = [shape(kv.shape, BF) for kv in kv_blocks]
        if fast:
            kv_outs[-1] = shape((2, rows, heads_width), F32)
        d_query, *d_kvs = kernel(
            functools.partial(attend_back_body, n_blocks),
            "attend_back",
            spots,
            [Free(d_attn), queries, log_total, tables] + kv_blocks + masks,
            [headed] + kv_outs,
            [slot(out_pieces, 0)],
            extra=[pltpu.VMEM((rows, heads_width), BF)],
        )
        if fast:
            own = d_kvs[1]
            other = [lax.ppermute(after(d_kvs[0], *mlp_sent), "ctx", [(1, 0)])]
            mlp_terms, mlp_added = reduce_second(
                spots, mlp_parts, mlp_sent, (d_kvs[0],), (), "mlp_add"
            )
            own = after(own, mlp_added)
        else:
            own = lax.psum_scatter(d_kvs[0], "ctx", scatter_dimension=1, tiled=True)
            other = []
        d_qkv, bias_sums, part = kernel(
            functools.partial(qkv_back_body, len(other)),
            "qkv_back",
            spots,
            [d_query, tables, own] + other,
            [shape((3, rows, heads_width), BF), shape((3, heads_width), F32), wide],
            [slot(qkv_pieces, index) for index in range(3)],
        )
        terms = tensor_scatter(part)
        if layer == layers - 1:
            terms = after(terms, summed)
        elif layer == layers - 2:
            terms = after(terms, output)
        pairs = ((0, 0), (0, 1), (0, 2), (1, 3))
        if fast:
            pending = weight_grads(
                [first_in, d_attn, d_qkv, mixed], 2, pairs, (part,), (), "attn_grads"
            )
            terms = after(terms, pending[0][0], *mlp_terms[3:])
        else:
            rights = [d_qkv[0], d_qkv[1], d_qkv[2], mixed]
            plain[layer] = (plain_grads([first_in, d_attn], rights, pairs), mlp_grad)
        grad, normed, sums_one = kernel(
            norm_back_body,
            "norm_back",
            spots,
            [Free(terms), stream, gains[layer, 0][None], grad_mid],
            [block_f, copies_b, shape((2, width), F32)],
        )
        d_mlp = tensor_gather(normed)
        if fast:
            mlp_terms[0] = after(mlp_terms[0], grad)
            mlp_outs = kernel(
                functools.partial(finish_body, True),
                "mlp_finish",
                spots,
                mlp_terms,
                [
                    (shape((layers, block_rows, 2, hidden_width), F32), layer),
                    (shape((layers, hidden_width, block_rows), F32), layer),
                ],
                reuse=() if mlp_outs is None else ((mlp_outs[0], 0), (mlp_outs[1], 1)),
            )
            d_mlp = after(d_mlp, mlp_outs[0], *pending[1])
        bias_rows = lax.dynamic_update_slice_in_dim(
            jnp.zeros((3, width), F32), bias_sums, tensor_rank * heads_width, 1
        )
        sums[layer] = jnp.concatenate(
            [sums_one[0:1], sums_two[0:1], sums_one[1:2], sums_two[1:2], bias_rows]
        )
    totals, halfway = reduce_small(jnp.concatenate(sums), fast)
    totals = totals.reshape(layers, 7, -1)
    if fast:
        attn_terms, _ = reduce_second(spots, *pending, (grad,), (), "attn_add")
        attn_outs = attn_finish(spots, attn_outs, attn_terms, 0, layers)
    grad_input = d_mlp.astype(F32)
    if fast:
        grads = (attn_outs[0].transpose(0, 2, 1, 3), attn_outs[1], mlp_outs[0], mlp_outs[1])
    else:
        attn = jnp.stack([pair[0] for pair in plain])
        mlp = jnp.stack([pair[1] for pair in plain])
        grads = (
            attn[:, :3].transpose(0, 2, 1, 3),
            attn[:, 3].transpose(0, 2, 1),
            mlp[:, :2].transpose(0, 2, 1, 3),
            mlp[:, 2].transpose(0, 2, 1),
        )
    return (
        output[None],
        grad_input[None],
        totals[:, 0:2],
        totals[:, 2:4],
        grads[0],
        totals[:, 4:7],
        grads[1],
        grads[2],
        grads[3],
    )


def attn_finish(spots, outs, terms, layer, layers):
    matrices, half, columns = terms[3].shape
    rows = 2 * half
    return kernel(
        functools.partial(finish_body, False),
        "attn_finish",
        spots,
        terms,
        [
            (shape((layers, matrices - 1, rows, columns), F32), layer),
            (shape((layers, columns, rows), F32), layer),
        ],
        reuse=() if outs is None else ((outs[0], 0), (outs[1], 1)),
    )


def plain_grads(lefts, rights, pairs):
    whole = jnp.stack([mm(lefts[a], rights[b], TN).astype(BF) for a, b in pairs])
    return lax.psum_scatter(whole, ("fsdp", "ctx"), scatter_dimension=1, tiled=True).astype(F32)


def solution(mesh):
    return jax.shard_map(
        local,
        mesh=mesh,
        in_specs=(
            P("fsdp", "ctx", None),
            P("fsdp", "ctx", None),
            P("fsdp", None),
            P(None, None, ("fsdp", "ctx")),
            P(None, None, ("fsdp", "ctx")),
            P(None, ("fsdp", "ctx"), None, "tp"),
            P(None, None, ("fsdp", "ctx")),
            P(None, "tp", ("fsdp", "ctx")),
            P(None, ("fsdp", "ctx"), None, "tp"),
            P(None, "tp", ("fsdp", "ctx")),
        ),
        out_specs=(
            P("fsdp", "ctx", None),
            P("fsdp", "ctx", None),
            P(None, None, ("fsdp", "ctx")),
            P(None, None, ("fsdp", "ctx")),
            P(None, ("fsdp", "ctx"), None, "tp"),
            P(None, None, ("fsdp", "ctx")),
            P(None, "tp", ("fsdp", "ctx")),
            P(None, ("fsdp", "ctx"), None, "tp"),
            P(None, "tp", ("fsdp", "ctx")),
        ),
        check_vma=False,
    )
```

```python
import functools

import jax
import jax.numpy as jnp
from jax import lax
from jax.experimental import pallas as pl
from jax.experimental.pallas import tpu as pltpu
from jax.sharding import PartitionSpec as P

HD = 64
ROT = 16
LANES = 128
SCALE = 1.0 / HD**0.5
VMEM_LIMIT = 50 * 1024 * 1024
NN = (((1,), (0,)), ((), ()))
NT = (((1,), (1,)), ((), ()))
TN = (((0,), (0,)), ((), ()))
BF = jnp.bfloat16
F32 = jnp.float32
EACH = -1
TIMES = {
    "pack": 7.0,
    "qkv": 8.5,
    "attend": 8.0,
    "norm": 3.0,
    "mlp": 11.5,
    "mlp_back": 14.0,
    "mlp_both": 18.0,
    "norm_back": 3.5,
    "attend_back": 10.0,
    "qkv_back": 9.0,
    "mlp_grads": 10.5,
    "attn_grads": 7.0,
    "mlp_add": 4.0,
    "attn_add": 3.0,
    "mlp_finish": 7.5,
    "attn_finish": 4.5,
    "sum": 3.0,
}


def cost(name):
    return pl.CostEstimate(flops=0, bytes_accessed=int(TIMES[name] * 3.0e6), transcendentals=0)


def mm(lhs, rhs, dims):
    return lax.dot_general(lhs, rhs, dims, preferred_element_type=F32)


def shape(dims, dtype):
    return jax.ShapeDtypeStruct(tuple(dims), dtype)


class Free:
    def __init__(self, array):
        self.array = array


class Io:
    def __init__(self, ins, loads, outs, stores, held, weights, started, extra):
        self.ins, self.loads, self.outs, self.stores = ins, loads, outs, stores
        self.held, self.weights, self.started, self.extra = held, weights, started, extra
        self.there, self.held_there, self.gone = set(), set(), []

    def get(self, index):
        if index not in self.there:
            self.loads[index].wait()
            self.there.add(index)
        return self.ins[index]

    def weight(self, slot):
        if slot not in self.held_there:
            self.held_there.add(slot)
            copies = self.weights[slot]
            for copy in copies[: len(copies) // 2]:
                copy.wait()
            self.begin(slot + 2)
            for copy in copies[len(copies) // 2 :]:
                copy.wait()
        return self.held[slot]

    def begin(self, count):
        while self.started < min(count, len(self.weights)):
            for copy in self.weights[self.started]:
                copy.start()
            self.started += 1

    def put(self, index):
        for copy in self.stores[index]:
            copy.start()
            self.gone.append(copy)


def kernel(body, name, spots, loads, outs, slots=(), eager=1, extra=(), reuse=()):
    free = [isinstance(item, Free) for item in loads]
    loads = [item.array if isinstance(item, Free) else item for item in loads]
    loads = [item if isinstance(item, tuple) else (item, None) for item in loads]
    outs = [item if isinstance(item, tuple) else (item, None) for item in outs]
    pieces, place_of = [], {}
    for group, _, _ in slots:
        for piece in group:
            if id(piece) not in place_of:
                place_of[id(piece)] = len(pieces)
                pieces.append(piece)
    slot_at = [([place_of[id(piece)] for piece in group], m, at) for group, m, at in slots]
    out_shapes = [item[0] for item in outs]
    n_in, n_piece, n_reuse = len(loads), len(pieces), len(reuse)

    def part(item):
        return tuple(item[0].shape) if item[1] is None else tuple(item[0].shape[1:])

    def view(ref, index):
        return ref if index is None else ref.at[index]

    def run(*refs):
        refs = list(refs)

        def take(count):
            taken = refs[:count]
            del refs[:count]
            return taken

        starts = take(1)[0]
        in_hbm, piece_hbm, _ = take(n_in), take(n_piece), take(n_reuse)
        out_hbm = take(len(out_shapes))
        ins, results, held = take(n_in), take(len(outs)), take(len(slots))
        in_sems, out_sems = take(2)
        slot_sems = take(len(slots))
        load_copies = [
            pltpu.make_async_copy(view(ref, index), ins[at], in_sems.at[at])
            for at, (ref, (_, index)) in enumerate(zip(in_hbm, loads, strict=True))
        ]
        for copy in load_copies:
            copy.start()
        weight_sets = []
        for slot, (members, matrix, first) in enumerate(slot_at):
            copies = []
            for number, member in enumerate(members):
                piece = piece_hbm[member]
                row = pl.multiple_of(starts[first + number], 64)
                copies.append(
                    pltpu.make_async_copy(
                        piece.at[matrix],
                        held[slot].at[pl.ds(row, piece.shape[1]), :],
                        slot_sems[slot].at[number],
                    )
                )
            weight_sets.append(copies)
        stores = []
        for at, (ref, (_, index)) in enumerate(zip(out_hbm, outs, strict=True)):
            if index == EACH:
                stores.append(
                    [
                        pltpu.make_async_copy(results[at], ref.at[each], out_sems.at[at, each])
                        for each in range(ref.shape[0])
                    ]
                )
            else:
                stores.append(
                    [pltpu.make_async_copy(results[at], view(ref, index), out_sems.at[at, 0])]
                )
        io = Io(ins, load_copies, results, stores, held, weight_sets, 0, refs)
        io.begin(eager)
        body(io)
        for at in range(n_in):
            io.get(at)
        for copy in io.gone:
            copy.wait()

    def in_hbm_now(array):
        return pltpu.with_memory_space_constraint(array, pltpu.HBM)

    args = [spots]
    args += [a if any_place else in_hbm_now(a) for (a, _), any_place in zip(loads, free, strict=True)]
    args += [in_hbm_now(piece) for piece in pieces]
    aliases = {len(args) + at: out for at, (_, out) in enumerate(reuse)}
    args += [in_hbm_now(array) for array, _ in reuse]
    hbm = pl.BlockSpec(memory_space=pltpu.HBM)
    most = max([out.shape[0] for out, index in outs if index == EACH], default=1)
    scratch = [pltpu.VMEM(part(item), item[0].dtype) for item in loads]
    scratch += [pltpu.VMEM(part(item), item[0].dtype) for item in outs]
    scratch += [
        pltpu.VMEM((sum(piece.shape[1] for piece in group), group[0].shape[2]), group[0].dtype)
        for group, _, _ in slots
    ]
    scratch += [
        pltpu.SemaphoreType.DMA((max(n_in, 1),)),
        pltpu.SemaphoreType.DMA((len(outs), most)),
    ]
    scratch += [pltpu.SemaphoreType.DMA((len(group),)) for group, _, _ in slots]
    return pl.pallas_call(
        run,
        out_shape=[pltpu.HBM(out.shape, out.dtype) for out in out_shapes],
        in_specs=[pl.BlockSpec(memory_space=pltpu.SMEM)]
        + [pl.BlockSpec(memory_space=pl.ANY) if any_place else hbm for any_place in free]
        + [hbm] * (n_piece + n_reuse),
        out_specs=[hbm] * len(out_shapes),
        scratch_shapes=scratch + list(extra),
        input_output_aliases=aliases,
        compiler_params=pltpu.CompilerParams(vmem_limit_bytes=VMEM_LIMIT),
        cost_estimate=cost(name),
        name=name,
    )(*args)


def normalized(v):
    centered = v - jnp.mean(v, axis=1, keepdims=True)
    variance = jnp.mean(centered * centered, axis=1, keepdims=True)
    scale = lax.rsqrt(variance + 1e-05)
    return centered * scale, scale


def norm_back(v, cot, gain):
    n, scale = normalized(v)
    e = cot * gain
    grad = scale * (
        e - jnp.mean(e, axis=1, keepdims=True) - n * jnp.mean(e * n, axis=1, keepdims=True)
    )
    return grad, n


def turn_wide(wide, tables, sign):
    keep, below, above = tables[0], tables[1], tables[2]
    turned = []
    for at in range(0, wide.shape[1], LANES):
        tile = wide[:, at : at + LANES]
        moved = pltpu.roll(tile, 8, 1) * below + pltpu.roll(tile, LANES - 8, 1) * above
        turned.append(tile * keep + sign * moved)
    return jnp.concatenate(turned, axis=1)


def total_of(terms):
    return functools.reduce(jnp.add, terms)


def qkv_body(has_norm, io):
    queries, kv = io.outs[:2]
    if has_norm:
        first_in = io.outs[2]
        n, _ = normalized(io.get(4)[...].astype(F32))
        first_in[...] = (n * io.get(2)[...] + io.get(3)[...]).astype(BF)
        io.put(2)
    else:
        first_in = io.get(2)
    bias, tables = io.get(0), io.get(1)
    for slot, index in enumerate((1, 2, 0)):
        part = mm(first_in[...], io.weight(slot)[...], NN) + bias[index : index + 1, :]
        if index < 2:
            part = turn_wide(part, tables, 1.0)
        if index == 0:
            queries[...] = part.astype(BF)
        else:
            kv[index - 1] = part.astype(BF)
    io.put(1)
    io.put(0)


def attend_body(n_blocks, io):
    queries = io.get(0)
    kvs = [io.get(1 + at) for at in range(n_blocks)]
    masks = [io.get(1 + n_blocks + at) for at in range(n_blocks)]
    mixed, log_total, part = io.outs
    for head in range(queries.shape[1] // HD):
        span = slice(head * HD, (head + 1) * HD)
        query = queries[:, span]
        scores = [
            mm(kv[0, :, span], query, NT) * SCALE + mask[...]
            for kv, mask in zip(kvs, masks, strict=True)
        ]
        top = functools.reduce(jnp.maximum, [jnp.max(s, axis=0, keepdims=True) for s in scores])
        exps = [jnp.exp(s - top) for s in scores]
        total = total_of([jnp.sum(e, axis=0, keepdims=True) for e in exps])
        inverse = 1.0 / total
        result = total_of(
            [
                mm((e * inverse).astype(BF), kv[1, :, span], TN)
                for e, kv in zip(exps, kvs, strict=True)
            ]
        )
        log_total[head : head + 1, :] = top + jnp.log(total)
        mixed[:, span] = result.astype(BF)
    io.put(0)
    io.put(1)
    part[...] = mm(mixed[...], io.weight(0)[...], NT).astype(BF)
    io.put(2)


def terms_sum(terms):
    return total_of([terms[at].astype(F32) for at in range(terms.shape[0])])


def norm_body(io):
    stream = terms_sum(io.get(0)) + io.get(1)[...].astype(F32)
    io.outs[0][...] = stream
    io.put(0)
    n, _ = normalized(stream)
    io.outs[1][...] = (n * io.get(2)[...] + io.get(3)[...]).astype(BF)
    io.put(1)


def sum_body(io):
    io.outs[0][...] = (terms_sum(io.get(0)) + io.get(1)[...].astype(F32)).astype(BF)
    io.put(0)


def mlp_body(io):
    gate_out, up_out, hidden, part = io.outs
    second_in = io.get(0)
    gate = mm(second_in[...], io.weight(0)[...], NN)
    gate_out[...] = gate.astype(BF)
    io.put(0)
    act = gate * jax.nn.sigmoid(gate)
    up = mm(second_in[...], io.weight(1)[...], NN)
    up_out[...] = up.astype(BF)
    io.put(1)
    hidden[...] = (act * up).astype(BF)
    io.put(2)
    part[...] = mm(hidden[...], io.weight(2)[...], NT).astype(BF)
    io.put(3)


def mlp_back_body(io):
    d_gate_up, part = io.outs
    d_mlp = io.get(2)
    gate = io.get(0)[...].astype(F32)
    sig = jax.nn.sigmoid(gate)
    d_hidden = mm(d_mlp[...], io.weight(0)[...], NN)
    d_gate_up[1] = (d_hidden * (gate * sig)).astype(BF)
    d_gate_up[0] = (
        d_hidden * io.get(1)[...].astype(F32) * (sig * (1.0 + gate * (1.0 - sig)))
    ).astype(BF)
    io.put(0)
    total = mm(d_gate_up[0], io.weight(1)[...], NT)
    total = total + mm(d_gate_up[1], io.weight(2)[...], NT)
    part[...] = total.astype(BF)
    io.put(1)


def mlp_both_body(io):
    hidden, part_out, d_gate_up, part = io.outs
    second_in = io.get(0)
    gate = mm(second_in[...], io.weight(0)[...], NN)
    sig = jax.nn.sigmoid(gate)
    act = gate * sig
    slope = sig * (1.0 + gate * (1.0 - sig))
    up = mm(second_in[...], io.weight(1)[...], NN)
    hidden[...] = (act * up).astype(BF)
    io.put(0)
    down = io.weight(2)
    d_hidden = mm(io.get(1)[...], down[...], NN)
    d_gate_up[1] = (d_hidden * act).astype(BF)
    d_gate_up[0] = (d_hidden * up * slope).astype(BF)
    io.put(2)
    total = mm(d_gate_up[0], io.weight(0)[...], NT)
    total = total + mm(d_gate_up[1], io.weight(1)[...], NT)
    part[...] = total.astype(BF)
    io.put(3)
    part_out[...] = mm(hidden[...], down[...], NT).astype(BF)
    io.put(1)


def norm_back_body(io):
    c = terms_sum(io.get(0))
    grad, n = norm_back(io.get(1)[...].astype(F32), c, io.get(2)[...])
    grad = io.get(3)[...].astype(F32) + grad
    io.outs[0][...] = grad
    io.put(0)
    io.outs[1][...] = grad.astype(BF)
    io.put(1)
    io.outs[2][0:1, :] = jnp.sum(n * c, axis=0, keepdims=True)
    io.outs[2][1:2, :] = jnp.sum(c, axis=0, keepdims=True)
    io.put(2)


def attend_back_body(n_blocks, io):
    d_query, d_kvs = io.outs[0], io.outs[1:]
    d_mixed = io.extra[0]
    d_mixed[...] = mm(io.get(0)[...], io.weight(0)[...], NN).astype(BF)
    queries, log_total, tables = io.get(1), io.get(2), io.get(3)
    kvs = [io.get(4 + at) for at in range(n_blocks)]
    masks = [io.get(4 + n_blocks + at) for at in range(n_blocks)]
    pair = []
    for head in range(queries.shape[1] // HD):
        span = slice(head * HD, (head + 1) * HD)
        query = queries[:, span]
        d_out = d_mixed[:, span]
        row_log = log_total[head : head + 1, :]
        probs = [
            jnp.exp(mm(kv[0, :, span], query, NT) * SCALE + mask[...] - row_log)
            for kv, mask in zip(kvs, masks, strict=True)
        ]
        d_probs = [mm(kv[1, :, span], d_out, NT) for kv in kvs]
        delta = total_of(
            [jnp.sum(p * dp, axis=0, keepdims=True) for p, dp in zip(probs, d_probs, strict=True)]
        )
        d_scores = [
            (p * (dp - delta)).astype(BF) for p, dp in zip(probs, d_probs, strict=True)
        ]
        pair.append(
            total_of([mm(ds, kv[0, :, span], TN) for ds, kv in zip(d_scores, kvs, strict=True)])
            * SCALE
        )
        if len(pair) == LANES // HD:
            wide = slice((head + 1) * HD - LANES, (head + 1) * HD)
            d_query[:, wide] = turn_wide(jnp.concatenate(pair, axis=1), tables, -1.0).astype(BF)
            pair = []
        for ds, p, d_kv in zip(d_scores, probs, d_kvs, strict=True):
            d_kv[0, :, span] = (mm(ds, query, NN) * SCALE).astype(d_kv.dtype)
            d_kv[1, :, span] = mm(p.astype(BF), d_out, NN).astype(d_kv.dtype)
    for at in range(1 + n_blocks):
        io.put(at)


def qkv_back_body(n_other, io):
    d_qkv, bias, part = io.outs
    tables = io.get(1)
    terms = [io.get(2 + at) for at in range(1 + n_other)]
    d_qkv[0] = io.get(0)[...]
    d_qkv[1] = turn_wide(
        total_of([term[0].astype(F32) for term in terms]), tables, -1.0
    ).astype(BF)
    d_qkv[2] = total_of([term[1].astype(F32) for term in terms]).astype(BF)
    io.put(0)
    for index in range(3):
        bias[index : index + 1, :] = jnp.sum(d_qkv[index].astype(F32), axis=0, keepdims=True)
    io.put(1)
    part[...] = total_of(
        [mm(d_qkv[index], io.weight(index)[...], NT) for index in range(3)]
    ).astype(BF)
    io.put(2)


def pack_body(io):
    gate_up, down = io.get(0), io.get(1)
    for part in range(2):
        io.outs[0][part] = gate_up[:, part, :]
    if len(io.outs) == 1:
        io.outs[0][2] = down[...].T
        io.put(0)
    else:
        io.put(0)
        io.outs[1][0] = down[...].T
        io.put(1)


def add_body(io):
    io.outs[0][...] = (io.get(0)[...].astype(F32) + io.get(2)[...].astype(F32)).astype(BF)
    io.put(0)
    io.outs[1][...] = (io.get(1)[...].astype(F32) + io.get(3)[...].astype(F32)).astype(BF)
    io.put(1)


def finish_body(is_mlp, io):
    own, x1, y1, x2, y2 = (io.get(at) for at in range(5))
    half = own.shape[2]
    main, other = io.outs
    matrices = own.shape[1]
    for side, (one, two) in enumerate(((x1, y2), (y1, x2))):
        rows = slice(side * half, (side + 1) * half)
        for matrix in range(matrices):
            whole = (
                own[side, matrix].astype(F32) + one[matrix].astype(F32) + two[matrix].astype(F32)
            )
            if matrix == matrices - 1:
                other[:, rows] = whole.T
            elif is_mlp:
                main[rows, matrix, :] = whole
            else:
                main[matrix, rows, :] = whole
    io.put(0)
    io.put(1)


def weight_grad_body(counts, n_left, pairs, *refs):
    ids = refs[0]
    n_in, n_held = len(counts), sum(counts)
    own = refs[1 : 1 + n_in]
    peer = refs[1 + n_in : 1 + 2 * n_in]
    outs = refs[1 + 2 * n_in : 6 + 2 * n_in]
    held = refs[6 + 2 * n_in : 6 + 2 * n_in + n_held]
    stage, in_sems, out_sems = refs[6 + 2 * n_in + n_held :]
    rows = held[0].shape[0] // 2
    loads = []
    for part, side in enumerate((own, peer)):
        at = 0
        for source, count in zip(side, counts, strict=True):
            for index in range(count):
                copy = pltpu.make_async_copy(
                    source if len(source.shape) == 2 else source.at[index],
                    held[at].at[pl.ds(part * rows, rows), :],
                    in_sems.at[at, part],
                )
                copy.start()
                loads.append(copy)
                at += 1
    for copy in loads:
        copy.wait()
    half = stage.shape[2]
    own_out, x1, y1, x2, y2 = outs
    targets = (
        (x1.at[0], y1.at[0]),
        (x1.at[1], x2),
        (y2, y1.at[1]),
        (own_out.at[0], own_out.at[1]),
    )
    stores = []
    for block in range(4):
        start = pl.multiple_of(ids[block], LANES)
        for matrix, (left, right) in enumerate(pairs):
            lhs = held[left][:, pl.ds(start, 2 * half)]
            result = mm(lhs, held[n_left + right][...], TN).astype(BF)
            stage[2 * block, matrix] = result[:half]
            stage[2 * block + 1, matrix] = result[half:]
        for part in range(2):
            copy = pltpu.make_async_copy(
                stage.at[2 * block + part], targets[block][part], out_sems.at[block, part]
            )
            copy.start()
            stores.append(copy)
    for copy in stores:
        copy.wait()


def after(array, *earlier):
    return lax.optimization_barrier((array,) + earlier)[0]


def pairs_of(axis, bit):
    return [(index, index ^ bit) for index in range(lax.axis_size(axis))]


def swap_x(array):
    return lax.ppermute(array, "fsdp", pairs_of("fsdp", 2))


def swap_core(array):
    return lax.ppermute(array, "fsdp", pairs_of("fsdp", 1))


def swap_y(array):
    return lax.ppermute(array, "ctx", pairs_of("ctx", 1))


def place():
    fsdp = lax.axis_index("fsdp")
    return fsdp // 2, fsdp % 2, lax.axis_index("ctx")


class Gather:
    def __init__(self, shard):
        self.shard = shard
        self.rows = shard.shape[1]

    def near_x(self, wait=()):
        self.from_x = swap_x(after(self.shard, *wait))

    def near_y(self, wait=()):
        self.from_y = swap_y(after(self.shard, *wait))
        self.mine = [self.shard, self.from_x, self.from_y]

    def near(self, wait_x=(), wait_y=()):
        self.near_x(wait_x)
        self.near_y(wait_y)

    def swap(self, *wait):
        self.peers = [swap_core(after(piece, *wait)) for piece in self.mine]

    def far(self, way, wait_x=(), wait_y=()):
        half = self.rows // 2
        self.way = way
        if way == "x":
            self.pieces = [swap_x(after(self.from_y, *wait_x))]
        elif way == "y":
            self.pieces = [swap_y(after(self.from_x, *wait_y))]
        else:
            self.pieces = [
                swap_x(after(self.from_y[:, :half], *wait_x)),
                swap_y(after(self.from_x[:, half:], *wait_y)),
            ]

    def all(self, *wait):
        far_peers = [swap_core(after(piece, *wait)) for piece in self.pieces]
        return self.mine + self.pieces + self.peers + far_peers


def piece_rows(rows):
    x, core, y = place()

    def row(x_at, core_at, y_at):
        return ((x_at * 2 + core_at) * 2 + y_at) * rows

    offs = []
    for halves in (0, 1):
        for core_at in (core, 1 - core):
            offs += [row(x, core_at, y), row(1 - x, core_at, y), row(x, core_at, 1 - y)]
            offs.append(row(1 - x, core_at, 1 - y))
            if halves:
                offs.append(row(1 - x, core_at, 1 - y) + rows // 2)
    return offs


def gather_whole(shard):
    return [lax.all_gather(shard, ("fsdp", "ctx"), axis=1, tiled=True)]


def gather_small(packed, fast):
    if not fast:
        return lax.all_gather(packed, ("fsdp", "ctx"), axis=1, tiled=True), ()
    x, core, y = place()

    def join(array, other, bit):
        return jnp.where(bit == 0, jnp.stack([array, other]), jnp.stack([other, array]))

    from_y = swap_y(packed)
    held = join(packed, from_y, y)
    held = join(held, swap_core(held), core)
    held = join(held, swap_x(held), x)
    rows, cols = packed.shape
    return held.transpose(3, 0, 1, 2, 4).reshape(rows, 8 * cols), (from_y,)


def reduce_small(sums, fast, *wait):
    if not fast:
        part = lax.psum_scatter(sums, ("fsdp", "ctx"), scatter_dimension=1, tiled=True)
        return lax.psum(part, "tp")
    x, core, y = place()
    rows, width = sums.shape
    held = sums.reshape(rows, 2, 2, 2, width // 8).transpose(1, 3, 2, 0, 4)
    for bit, swap in ((x, swap_x), (y, swap_y), (core, swap_core)):
        keep = jnp.where(bit == 0, held[0], held[1])
        send = jnp.where(bit == 0, held[1], held[0])
        held = keep + swap(after(send, *wait) if swap is swap_y else send)
    step = 1
    while step < lax.axis_size("tp"):
        held = held + lax.ppermute(held, "tp", pairs_of("tp", step))
        step *= 2
    return held


def tensor_scatter(part, *earlier):
    size = lax.axis_size("tp")
    blocks = after(part, *earlier).reshape(size, part.shape[0] // size, part.shape[1])
    return lax.all_to_all(blocks, "tp", 0, 0, tiled=True)


def tensor_gather(copies):
    return lax.all_to_all(copies, "tp", 0, 0, tiled=True)


def flat(blocks):
    return blocks.reshape(-1, blocks.shape[-1])


def weight_grads(own, peer, n_left, pairs, earlier, name):
    counts = tuple(1 if array.ndim == 2 else array.shape[0] for array in own)
    columns = own[-1].shape[-1]
    tokens, width = own[0].shape
    peer = [
        swap_core(after(array, *earlier)) if other is None else other
        for array, other in zip(own, peer, strict=True)
    ]
    rows = width // 8
    half = rows // 2
    x, core, y = place()
    ids = jnp.stack(
        [
            ((x_at * 2 + core) * 2 + y_at) * rows
            for x_at, y_at in ((1 - x, 1 - y), (1 - x, y), (x, 1 - y), (x, y))
        ]
    ).astype(jnp.int32)
    block = (len(pairs), half, columns)
    hbm = pl.BlockSpec(memory_space=pltpu.HBM)
    scratch = [
        pltpu.VMEM((2 * tokens, array.shape[-1]), BF)
        for array, count in zip(own, counts, strict=True)
        for _ in range(count)
    ]
    scratch += [
        pltpu.VMEM((8,) + block, BF),
        pltpu.SemaphoreType.DMA((sum(counts), 2)),
        pltpu.SemaphoreType.DMA((4, 2)),
    ]
    own_sum, x1, y1, x2, y2 = pl.pallas_call(
        functools.partial(weight_grad_body, counts, n_left, pairs),
        out_shape=[pltpu.HBM((2,) + block, BF)] * 3 + [pltpu.HBM(block, BF)] * 2,
        in_specs=[pl.BlockSpec(memory_space=pltpu.SMEM)] + [hbm] * (2 * len(own)),
        out_specs=[hbm] * 5,
        scratch_shapes=scratch,
        compiler_params=pltpu.CompilerParams(vmem_limit_bytes=VMEM_LIMIT),
        cost_estimate=cost(name),
        name=name,
    )(ids, *[pltpu.with_memory_space_constraint(a, pltpu.HBM) for a in list(own) + peer])
    return (own_sum, x2, y2), (x1, y1)


def add_received(spots, parts, received, earlier, name):
    _, x2, y2 = parts
    got_x1, got_y1 = received
    block = shape(x2.shape, BF)
    return kernel(
        add_body,
        name,
        spots,
        [after(x2, *earlier), y2, (got_y1, 0), (got_x1, 0)],
        [block, block],
    )


def send_second(parts, received, sums, earlier):
    far_x = swap_x(after(sums[0], *earlier))
    far_y = swap_y(after(sums[1], *earlier))
    return [parts[0], (received[0], 1), (received[1], 1), far_x, far_y]


def reduce_second(spots, parts, received, earlier_add, earlier_send, name):
    sums = add_received(spots, parts, received, earlier_add, name)
    return send_second(parts, received, sums, earlier_send), sums[0]


def layout(lengths, first_row, row_count):
    token_index = first_row + jnp.arange(row_count, dtype=jnp.int32)
    doc_ends = jnp.cumsum(lengths)
    starts = doc_ends - lengths
    segment = jnp.sum(
        (token_index[:, None] >= doc_ends[None, :]).astype(jnp.int32), axis=1, dtype=jnp.int32
    )
    doc_begin = jnp.max(
        jnp.where(token_index[:, None] >= starts[None, :], starts[None, :], 0), axis=1
    )
    return (segment, token_index - doc_begin, token_index)


def rotary_tables(position):
    frequency = 10000.0 ** (-jnp.arange(0, ROT, 2, dtype=F32) / ROT)
    angles = position.astype(F32)[:, None] * frequency[None, :]
    cos, sin = jnp.cos(angles), jnp.sin(angles)
    rows = position.shape[0]
    blank = jnp.zeros((rows, ROT // 2), F32)
    rest = HD - ROT
    keep = jnp.concatenate([cos, cos, jnp.ones((rows, rest), F32)], axis=1)
    below = jnp.concatenate([blank, sin, jnp.zeros((rows, rest), F32)], axis=1)
    above = jnp.concatenate([-sin, blank, jnp.zeros((rows, rest), F32)], axis=1)
    return jnp.stack([jnp.tile(t, (1, LANES // HD)) for t in (keep, below, above)])


def local(
    tokens,
    cotangent,
    doc_lengths,
    norm_gains,
    norm_biases,
    qkv_weight,
    qkv_bias,
    out_weight,
    gate_up_weight,
    down_weight,
):
    rows = tokens.shape[1]
    width = tokens.shape[2]
    heads_width = qkv_weight.shape[3]
    hidden_width = gate_up_weight.shape[3]
    heads = heads_width // HD
    layers = norm_gains.shape[0]
    block_rows = qkv_weight.shape[1]
    ctx_size = lax.axis_size("ctx")
    fast = lax.axis_size("fsdp") == 4 and ctx_size == 2
    ctx_rank = lax.axis_index("ctx")
    tensor_rank = lax.axis_index("tp")

    small = jnp.concatenate(
        [
            norm_gains.reshape(2 * layers, -1),
            norm_biases.reshape(2 * layers, -1),
            qkv_bias.reshape(3 * layers, -1),
        ]
    )
    small, sent_small = gather_small(small, fast)
    small = small.astype(F32)
    gains = small[: 2 * layers].reshape(layers, 2, width)
    shifts = small[2 * layers : 4 * layers].reshape(layers, 2, width)
    biases = lax.dynamic_slice_in_dim(
        small[4 * layers :], tensor_rank * heads_width, heads_width, 1
    ).reshape(layers, 3, heads_width)

    tensor_size = lax.axis_size("tp")
    block = rows // tensor_size
    spots = piece_rows(block_rows) if fast else [jnp.int32(0)]
    spots = jnp.stack([jnp.asarray(spot, jnp.int32) for spot in spots])
    spots_at = {8: 0, 10: 8, 1: 0}

    def slot(pieces, matrix):
        return (pieces, matrix, spots_at[len(pieces)])

    shards = []
    for layer in range(layers):
        if fast:
            counts = (3,) if layer == 0 else (2, 1)
            mlp_shards = kernel(
                pack_body,
                "pack",
                spots,
                [(gate_up_weight, layer), (down_weight, layer)],
                [shape((count, block_rows, hidden_width), BF) for count in counts],
            )
        else:
            mlp_shards = [
                jnp.concatenate(
                    [gate_up_weight[layer].transpose(1, 0, 2), down_weight[layer].T[None]]
                )
            ]
        qkv_shard, out_shard = qkv_weight[layer].transpose(1, 0, 2), out_weight[layer].T[None]
        shards.append((jnp.concatenate([qkv_shard, out_shard]), *mlp_shards))

    lengths = doc_lengths[0]
    seg_query, pos_query, index_query = layout(lengths, ctx_rank * rows, rows)
    tables = rotary_tables(pos_query)

    def mask_of(first, count, usable):
        seg_key, _, index_key = layout(lengths, first, count)
        allowed = (seg_query[None, :] == seg_key[:, None]) & (
            index_query[None, :] >= index_key[:, None]
        )
        return jnp.where(allowed & usable, 0.0, -1e30).astype(F32)

    if fast:
        masks = [
            mask_of(jnp.int32(0), rows, ctx_rank > 0),
            mask_of(ctx_rank * rows, rows, True),
        ]
    else:
        masks = [mask_of(jnp.int32(0), rows * ctx_size, True)]
    n_blocks = len(masks)

    wide = shape((rows, width), BF)
    inner = shape((rows, hidden_width), BF)
    headed = shape((rows, heads_width), BF)
    block_f = shape((block, width), F32)
    copies_b = (shape((tensor_size, block, width), BF), EACH)

    stream = lax.dynamic_slice_in_dim(tokens[0], tensor_rank * block, block, 0)
    first_in = None
    saved, groups = [], []
    if fast:
        attn_g, mlp_g = (Gather(shard) for shard in shards[0])
        attn_g.near((), sent_small)
        attn_g.swap()
        attn_g.far("both")
        mlp_g.near_x(attn_g.pieces[:1])
    for layer in range(layers):
        if fast:
            attn_pieces = attn_g.all()
        else:
            attn_pieces, mlp_pieces = (gather_whole(shard) for shard in shards[layer])
            mlp_slots = [slot(mlp_pieces, index) for index in range(3)]
        outs = [headed, shape((2, rows, heads_width), BF)]
        if layer == 0:
            args = [biases[0], tables, gains[0, 0][None], shifts[0, 0][None], tokens[0]]
            if fast:
                args[0] = after(args[0], mlp_g.shard)
            outs.append(wide)
        else:
            args = [biases[layer], tables, Free(first_in)]
        queries, kv, *normed = kernel(
            functools.partial(qkv_body, layer == 0),
            "qkv",
            spots,
            args,
            outs,
            [slot(attn_pieces, index) for index in (1, 2, 0)],
        )
        if layer == 0:
            first_in = normed[0]
        if fast:
            prev = lax.ppermute(kv, "ctx", [(0, 1)])
            kv_blocks = [prev, kv]
            if layer == 0:
                mlp_g.near_y((prev,))
            else:
                down_g.near_y((prev,))
        else:
            kv_blocks = [lax.all_gather(kv, "ctx", axis=1, tiled=True)]
        mixed, log_total, part = kernel(
            functools.partial(attend_body, n_blocks),
            "attend",
            spots,
            [queries] + kv_blocks + masks,
            [headed, shape((heads, rows), F32), wide],
            [slot(attn_pieces, 3)],
        )
        terms = tensor_scatter(part)
        if fast and layer == 0:
            terms = after(terms, mlp_g.from_x)
        elif fast:
            gu_g.swap(part)
            gu_g.far("both", (part,), (part,))
            terms = after(terms, down_g.from_x)
        mid, normed = kernel(
            norm_body,
            "norm",
            spots,
            [Free(terms), stream, gains[layer, 1][None], shifts[layer, 1][None]],
            [block_f, copies_b],
        )
        second_in = tensor_gather(normed)
        if fast:
            if layer == 0:
                mlp_g.swap(mid)
                mlp_g.far("both", (mid,), (mid,))
                mlp_pieces = mlp_g.all(second_in)
                mlp_slots = [slot(mlp_pieces, index) for index in range(3)]
                sent = mlp_g.pieces
            else:
                down_g.swap(mid)
                down_g.far("both", (mid,), (mid,))
                gu_pieces, down_pieces = gu_g.all(), down_g.all(second_in)
                mlp_slots = [slot(gu_pieces, 0), slot(gu_pieces, 1), slot(down_pieces, 0)]
                sent = down_g.pieces
        second_in = flat(second_in)
        if layer < layers - 1:
            gate, up, hidden, part = kernel(
                mlp_body,
                "mlp",
                spots,
                [Free(second_in)],
                [inner, inner, inner, wide],
                mlp_slots,
            )
        else:
            peer = swap_core(cotangent[0]) if fast else ()
            hidden, last_part, d_gate_up, part = kernel(
                mlp_both_body,
                "mlp_both",
                spots,
                [Free(second_in), after(cotangent[0], peer)],
                [inner, wide, shape((2, rows, hidden_width), BF), wide],
                mlp_slots,
            )
            gate, up, last_mid = None, None, mid
        saved.append((stream, first_in, queries, kv_blocks, mixed, log_total, mid))
        saved[-1] += (second_in, gate, up, hidden)
        groups.append((attn_pieces, mlp_slots))
        if layer == layers - 1:
            break
        terms = tensor_scatter(part)
        if fast:
            attn_g, gu_g, down_g = (Gather(shard) for shard in shards[layer + 1])
            attn_g.near(sent[:1], sent[1:])
            attn_g.swap(part)
            attn_g.far("both", (part,), (part,))
            gu_g.near((attn_g.from_x, part), (attn_g.from_y, part))
            down_g.near_x((gu_g.from_x,))
            terms = after(terms, gu_g.shard, *attn_g.pieces, *attn_g.peers)
        stream, normed = kernel(
            norm_body,
            "norm",
            spots,
            [Free(terms), mid, gains[layer + 1, 0][None], shifts[layer + 1, 0][None]],
            [block_f, copies_b],
        )
        first_in = flat(tensor_gather(normed))
        if fast:
            first_in = after(first_in, gu_g.from_x, gu_g.from_y)

    attn_outs, mlp_outs, pending, mlp_pending = None, None, None, None
    sums = [None] * layers
    plain = [None] * layers
    grad = lax.dynamic_slice_in_dim(cotangent[0], tensor_rank * block, block, 0)
    d_mlp = cotangent[0]
    for layer in reversed(range(layers)):
        (stream, first_in, queries, kv_blocks, mixed, log_total, mid) = saved[layer][:7]
        (second_in, gate, up, hidden) = saved[layer][7:]
        attn_pieces, mlp_slots = groups[layer]
        late = layer == layers - 1
        mlp_peer = [None] * 4
        if late:
            mlp_peer[1] = peer
        else:
            if fast:
                mlp_peer[0], mlp_peer[3] = swap_core(second_in), swap_core(hidden)
                gate = after(gate, mlp_peer[0], mlp_peer[3])
            d_gate_up, part = kernel(
                mlp_back_body,
                "mlp_back",
                spots,
                [gate, up, Free(d_mlp)],
                [shape((2, rows, hidden_width), BF), wide],
                [mlp_slots[2], mlp_slots[0], mlp_slots[1]],
            )
        terms = tensor_scatter(part)
        pairs = ((0, 0), (0, 1), (1, 2))
        if fast:
            if pending is not None:
                part = after(part, *mlp_pending[3:])
            mlp_parts, (to_x, to_y) = weight_grads(
                [second_in, d_mlp, d_gate_up, hidden], mlp_peer, 2, pairs, (part,), "mlp_grads"
            )
            terms = after(terms, mlp_parts[0])
            if pending is not None:
                mlp_pending[0] = after(mlp_pending[0], mlp_parts[0])
                mlp_outs = mlp_finish(spots, mlp_outs, mlp_pending, layer + 1, layers)
                attn_sums = add_received(spots, *pending, (mlp_outs[0],), "attn_add")
                terms = after(terms, attn_sums[0])
            got_x = swap_x(to_x)
            got_y = None if late else swap_y(to_y)
        else:
            mlp_grad = plain_grads(
                [second_in, d_mlp], [d_gate_up[0], d_gate_up[1], hidden], pairs
            )
        grad_mid, normed, sums_two = kernel(
            norm_back_body,
            "norm_back",
            spots,
            [Free(terms), mid, gains[layer, 1][None], grad],
            [block_f, copies_b, shape((2, width), F32)],
        )
        gathered = tensor_gather(normed)
        d_attn = flat(gathered)
        if layer == layers - 1:
            out_terms = tensor_scatter(last_part, gathered)
            (summed,) = kernel(sum_body, "sum", spots, [out_terms, last_mid], [copies_b])
        elif layer == layers - 2:
            out_blocks = tensor_gather(after(summed, gathered))
        kv_outs = [shape(kv.shape, BF) for kv in kv_blocks]
        if fast:
            kv_outs[-1] = shape((2, rows, heads_width), F32)
        d_query, *d_kvs = kernel(
            functools.partial(attend_back_body, n_blocks),
            "attend_back",
            spots,
            [Free(d_attn), queries, log_total, tables] + kv_blocks + masks,
            [headed] + kv_outs,
            [slot(attn_pieces, 3)],
            extra=[pltpu.VMEM((rows, heads_width), BF)],
        )
        if fast:
            own = d_kvs[1]
            other = [lax.ppermute(d_kvs[0] if late else after(d_kvs[0], got_y), "ctx", [(1, 0)])]
            if late:
                got_y = swap_y(after(to_y, other[0]))
                own = after(own, got_x)
            else:
                mlp_sums = add_received(spots, mlp_parts, (got_x, got_y), (d_kvs[0],), "mlp_add")
                own = after(own, mlp_sums[0])
                if pending is not None:
                    attn_terms = send_second(*pending, attn_sums, (other[0],))
                mlp_terms = send_second(mlp_parts, (got_x, got_y), mlp_sums, ())
            attn_peer = [swap_core(after(a, d_kvs[0])) for a in (first_in, d_attn)]
            attn_peer += [None, swap_core(after(mixed, d_kvs[0]))]
            own = after(own, attn_peer[0], attn_peer[1], attn_peer[3])
        else:
            own = lax.psum_scatter(d_kvs[0], "ctx", scatter_dimension=1, tiled=True)
            other = []
        if layer == layers - 1:
            own = after(own, out_terms)
        elif layer == layers - 2:
            own = after(own, out_blocks)
        d_qkv, bias_sums, part = kernel(
            functools.partial(qkv_back_body, len(other)),
            "qkv_back",
            spots,
            [d_query, tables, own] + other,
            [shape((3, rows, heads_width), BF), shape((3, heads_width), F32), wide],
            [slot(attn_pieces, index) for index in range(3)],
        )
        terms = tensor_scatter(part)
        if layer == layers - 1:
            terms = after(terms, summed)
        pairs = ((0, 0), (0, 1), (0, 2), (1, 3))
        if fast:
            ready = (part,) if late else (part, *mlp_terms[3:])
            attn_parts, (to_x, to_y) = weight_grads(
                [first_in, d_attn, d_qkv, mixed], attn_peer, 2, pairs, ready, "attn_grads"
            )
            pending = (attn_parts, (swap_x(to_x), swap_y(to_y)))
            terms = after(terms, attn_parts[0])
        else:
            rights = [d_qkv[0], d_qkv[1], d_qkv[2], mixed]
            plain[layer] = (plain_grads([first_in, d_attn], rights, pairs), mlp_grad)
        grad, normed, sums_one = kernel(
            norm_back_body,
            "norm_back",
            spots,
            [Free(terms), stream, gains[layer, 0][None], grad_mid],
            [block_f, copies_b, shape((2, width), F32)],
        )
        d_mlp = flat(tensor_gather(normed))
        if fast:
            if late:
                mlp_pending, mlp_added = reduce_second(
                    spots, mlp_parts, (got_x, got_y), (grad,), (), "mlp_add"
                )
                d_mlp = after(d_mlp, mlp_added)
            else:
                if mlp_pending is not None:
                    attn_terms[0] = after(attn_terms[0], grad)
                    attn_outs = attn_finish(spots, attn_outs, attn_terms, layer + 1, layers)
                mlp_terms[0] = after(mlp_terms[0], grad)
                mlp_outs = mlp_finish(spots, mlp_outs, mlp_terms, layer, layers)
        bias_rows = lax.dynamic_update_slice_in_dim(
            jnp.zeros((3, width), F32), bias_sums, tensor_rank * heads_width, 1
        )
        sums[layer] = jnp.concatenate(
            [sums_one[0:1], sums_two[0:1], sums_one[1:2], sums_two[1:2], bias_rows]
        )
    wait = ()
    if fast:
        attn_terms, attn_added = reduce_second(
            spots, *pending, (grad, mlp_outs[0], attn_outs[0]), (), "attn_add"
        )
        wait = (attn_added,)
    totals = reduce_small(jnp.concatenate(sums), fast, *wait).reshape(layers, 7, -1)
    if fast:
        attn_outs = attn_finish(spots, attn_outs, attn_terms, 0, layers)
    grad_input = d_mlp.astype(F32)
    if fast:
        grads = (attn_outs[0].transpose(0, 2, 1, 3), attn_outs[1], mlp_outs[0], mlp_outs[1])
    else:
        attn = jnp.stack([pair[0] for pair in plain])
        mlp = jnp.stack([pair[1] for pair in plain])
        grads = (
            attn[:, :3].transpose(0, 2, 1, 3),
            attn[:, 3].transpose(0, 2, 1),
            mlp[:, :2].transpose(0, 2, 1, 3),
            mlp[:, 2].transpose(0, 2, 1),
        )
    return (
        flat(out_blocks)[None],
        grad_input[None],
        totals[:, 0:2],
        totals[:, 2:4],
        grads[0],
        totals[:, 4:7],
        grads[1],
        grads[2],
        grads[3],
    )


def mlp_finish(spots, outs, terms, layer, layers):
    _, half, columns = terms[3].shape
    rows = 2 * half
    return kernel(
        functools.partial(finish_body, True),
        "mlp_finish",
        spots,
        terms,
        [
            (shape((layers, rows, 2, columns), F32), layer),
            (shape((layers, columns, rows), F32), layer),
        ],
        reuse=() if outs is None else ((outs[0], 0), (outs[1], 1)),
    )


def attn_finish(spots, outs, terms, layer, layers):
    matrices, half, columns = terms[3].shape
    rows = 2 * half
    return kernel(
        functools.partial(finish_body, False),
        "attn_finish",
        spots,
        terms,
        [
            (shape((layers, matrices - 1, rows, columns), F32), layer),
            (shape((layers, columns, rows), F32), layer),
        ],
        reuse=() if outs is None else ((outs[0], 0), (outs[1], 1)),
    )


def plain_grads(lefts, rights, pairs):
    whole = jnp.stack([mm(lefts[a], rights[b], TN).astype(BF) for a, b in pairs])
    return lax.psum_scatter(whole, ("fsdp", "ctx"), scatter_dimension=1, tiled=True).astype(F32)


def solution(mesh):
    return jax.shard_map(
        local,
        mesh=mesh,
        in_specs=(
            P("fsdp", "ctx", None),
            P("fsdp", "ctx", None),
            P("fsdp", None),
            P(None, None, ("fsdp", "ctx")),
            P(None, None, ("fsdp", "ctx")),
            P(None, ("fsdp", "ctx"), None, "tp"),
            P(None, None, ("fsdp", "ctx")),
            P(None, "tp", ("fsdp", "ctx")),
            P(None, ("fsdp", "ctx"), None, "tp"),
            P(None, "tp", ("fsdp", "ctx")),
        ),
        out_specs=(
            P("fsdp", "ctx", None),
            P("fsdp", "ctx", None),
            P(None, None, ("fsdp", "ctx")),
            P(None, None, ("fsdp", "ctx")),
            P(None, ("fsdp", "ctx"), None, "tp"),
            P(None, None, ("fsdp", "ctx")),
            P(None, "tp", ("fsdp", "ctx")),
            P(None, ("fsdp", "ctx"), None, "tp"),
            P(None, "tp", ("fsdp", "ctx")),
        ),
        check_vma=False,
    )
```

```python
import functools

import jax
import jax.numpy as jnp
from jax import lax
from jax.experimental import pallas as pl
from jax.experimental.pallas import tpu as pltpu
from jax.sharding import PartitionSpec as P

HD = 64
ROT = 16
LANES = 128
SCALE = 1.0 / HD**0.5
VMEM_LIMIT = 50 * 1024 * 1024
NN = (((1,), (0,)), ((), ()))
NT = (((1,), (1,)), ((), ()))
TN = (((0,), (0,)), ((), ()))
BF = jnp.bfloat16
F32 = jnp.float32
EACH = -1
TIMES = {
    "pack": 7.0,
    "qkv": 8.5,
    "attend": 8.0,
    "key_value": 6.5,
    "attend_own": 5.5,
    "attend_other": 5.5,
    "norm": 3.0,
    "mlp": 11.5,
    "mlp_back": 14.0,
    "mlp_both": 18.0,
    "norm_back": 3.5,
    "attend_back": 10.0,
    "qkv_back": 9.0,
    "mlp_grads": 10.5,
    "attn_grads": 7.0,
    "mlp_add": 4.0,
    "attn_add": 3.0,
    "mlp_finish": 7.5,
    "attn_finish": 4.5,
    "sum": 3.0,
}


def cost(name):
    return pl.CostEstimate(flops=0, bytes_accessed=int(TIMES[name] * 3.0e6), transcendentals=0)


def mm(lhs, rhs, dims):
    return lax.dot_general(lhs, rhs, dims, preferred_element_type=F32)


def shape(dims, dtype):
    return jax.ShapeDtypeStruct(tuple(dims), dtype)


class Free:
    def __init__(self, array):
        self.array = array


class Io:
    def __init__(self, ins, loads, outs, stores, held, weights, started, extra):
        self.ins, self.loads, self.outs, self.stores = ins, loads, outs, stores
        self.held, self.weights, self.started, self.extra = held, weights, started, extra
        self.there, self.held_there, self.gone = set(), set(), []

    def get(self, index):
        if index not in self.there:
            self.loads[index].wait()
            self.there.add(index)
        return self.ins[index]

    def weight(self, slot):
        if slot not in self.held_there:
            self.held_there.add(slot)
            copies = self.weights[slot]
            for copy in copies[: len(copies) // 2]:
                copy.wait()
            self.begin(slot + 2)
            for copy in copies[len(copies) // 2 :]:
                copy.wait()
        return self.held[slot]

    def begin(self, count):
        while self.started < min(count, len(self.weights)):
            for copy in self.weights[self.started]:
                copy.start()
            self.started += 1

    def put(self, index):
        for copy in self.stores[index]:
            copy.start()
            self.gone.append(copy)


def kernel(body, name, spots, loads, outs, slots=(), eager=1, extra=(), reuse=()):
    free = [isinstance(item, Free) for item in loads]
    loads = [item.array if isinstance(item, Free) else item for item in loads]
    loads = [item if isinstance(item, tuple) else (item, None) for item in loads]
    outs = [item if isinstance(item, tuple) else (item, None) for item in outs]
    pieces, place_of = [], {}
    for group, _, _ in slots:
        for piece in group:
            if id(piece) not in place_of:
                place_of[id(piece)] = len(pieces)
                pieces.append(piece)
    slot_at = [([place_of[id(piece)] for piece in group], m, at) for group, m, at in slots]
    out_shapes = [item[0] for item in outs]
    n_in, n_piece, n_reuse = len(loads), len(pieces), len(reuse)

    def part(item):
        return tuple(item[0].shape) if item[1] is None else tuple(item[0].shape[1:])

    def view(ref, index):
        return ref if index is None else ref.at[index]

    def run(*refs):
        refs = list(refs)

        def take(count):
            taken = refs[:count]
            del refs[:count]
            return taken

        starts = take(1)[0]
        in_hbm, piece_hbm, _ = take(n_in), take(n_piece), take(n_reuse)
        out_hbm = take(len(out_shapes))
        ins, results, held = take(n_in), take(len(outs)), take(len(slots))
        in_sems, out_sems = take(2)
        slot_sems = take(len(slots))
        load_copies = [
            pltpu.make_async_copy(view(ref, index), ins[at], in_sems.at[at])
            for at, (ref, (_, index)) in enumerate(zip(in_hbm, loads, strict=True))
        ]
        for copy in load_copies:
            copy.start()
        weight_sets = []
        for slot, (members, matrix, first) in enumerate(slot_at):
            copies = []
            for number, member in enumerate(members):
                piece = piece_hbm[member]
                row = pl.multiple_of(starts[first + number], 64)
                copies.append(
                    pltpu.make_async_copy(
                        piece.at[matrix],
                        held[slot].at[pl.ds(row, piece.shape[1]), :],
                        slot_sems[slot].at[number],
                    )
                )
            weight_sets.append(copies)
        stores = []
        for at, (ref, (_, index)) in enumerate(zip(out_hbm, outs, strict=True)):
            if index == EACH:
                stores.append(
                    [
                        pltpu.make_async_copy(results[at], ref.at[each], out_sems.at[at, each])
                        for each in range(ref.shape[0])
                    ]
                )
            else:
                stores.append(
                    [pltpu.make_async_copy(results[at], view(ref, index), out_sems.at[at, 0])]
                )
        io = Io(ins, load_copies, results, stores, held, weight_sets, 0, refs)
        io.begin(eager)
        body(io)
        for at in range(n_in):
            io.get(at)
        for copy in io.gone:
            copy.wait()

    def in_hbm_now(array):
        return pltpu.with_memory_space_constraint(array, pltpu.HBM)

    args = [spots]
    args += [a if any_place else in_hbm_now(a) for (a, _), any_place in zip(loads, free, strict=True)]
    args += [in_hbm_now(piece) for piece in pieces]
    aliases = {len(args) + at: out for at, (_, out) in enumerate(reuse)}
    args += [in_hbm_now(array) for array, _ in reuse]
    hbm = pl.BlockSpec(memory_space=pltpu.HBM)
    most = max([out.shape[0] for out, index in outs if index == EACH], default=1)
    scratch = [pltpu.VMEM(part(item), item[0].dtype) for item in loads]
    scratch += [pltpu.VMEM(part(item), item[0].dtype) for item in outs]
    scratch += [
        pltpu.VMEM((sum(piece.shape[1] for piece in group), group[0].shape[2]), group[0].dtype)
        for group, _, _ in slots
    ]
    scratch += [
        pltpu.SemaphoreType.DMA((max(n_in, 1),)),
        pltpu.SemaphoreType.DMA((len(outs), most)),
    ]
    scratch += [pltpu.SemaphoreType.DMA((len(group),)) for group, _, _ in slots]
    return pl.pallas_call(
        run,
        out_shape=[pltpu.HBM(out.shape, out.dtype) for out in out_shapes],
        in_specs=[pl.BlockSpec(memory_space=pltpu.SMEM)]
        + [pl.BlockSpec(memory_space=pl.ANY) if any_place else hbm for any_place in free]
        + [hbm] * (n_piece + n_reuse),
        out_specs=[hbm] * len(out_shapes),
        scratch_shapes=scratch + list(extra),
        input_output_aliases=aliases,
        compiler_params=pltpu.CompilerParams(vmem_limit_bytes=VMEM_LIMIT),
        cost_estimate=cost(name),
        name=name,
    )(*args)


def normalized(v):
    centered = v - jnp.mean(v, axis=1, keepdims=True)
    variance = jnp.mean(centered * centered, axis=1, keepdims=True)
    scale = lax.rsqrt(variance + 1e-05)
    return centered * scale, scale


def norm_back(v, cot, gain):
    n, scale = normalized(v)
    e = cot * gain
    grad = scale * (
        e - jnp.mean(e, axis=1, keepdims=True) - n * jnp.mean(e * n, axis=1, keepdims=True)
    )
    return grad, n


def turn_wide(wide, tables, sign):
    keep, below, above = tables[0], tables[1], tables[2]
    turned = []
    for at in range(0, wide.shape[1], LANES):
        tile = wide[:, at : at + LANES]
        moved = pltpu.roll(tile, 8, 1) * below + pltpu.roll(tile, LANES - 8, 1) * above
        turned.append(tile * keep + sign * moved)
    return jnp.concatenate(turned, axis=1)


def total_of(terms):
    return functools.reduce(jnp.add, terms)


def qkv_body(has_norm, io):
    queries, kv = io.outs[:2]
    if has_norm:
        first_in = io.outs[2]
        n, _ = normalized(io.get(4)[...].astype(F32))
        first_in[...] = (n * io.get(2)[...] + io.get(3)[...]).astype(BF)
        io.put(2)
    else:
        first_in = io.get(2)
    bias, tables = io.get(0), io.get(1)
    for slot, index in enumerate((1, 2, 0)):
        part = mm(first_in[...], io.weight(slot)[...], NN) + bias[index : index + 1, :]
        if index < 2:
            part = turn_wide(part, tables, 1.0)
        if index == 0:
            queries[...] = part.astype(BF)
        else:
            kv[index - 1] = part.astype(BF)
    io.put(1)
    io.put(0)


def key_value_body(has_norm, io):
    kv = io.outs[0]
    if has_norm:
        first_in = io.outs[1]
        n, _ = normalized(io.get(4)[...].astype(F32))
        first_in[...] = (n * io.get(2)[...] + io.get(3)[...]).astype(BF)
        io.put(1)
    else:
        first_in = io.get(2)
    bias, tables = io.get(0), io.get(1)
    keys = mm(first_in[...], io.weight(0)[...], NN) + bias[1:2, :]
    kv[0] = turn_wide(keys, tables, 1.0).astype(BF)
    kv[1] = (mm(first_in[...], io.weight(1)[...], NN) + bias[2:3, :]).astype(BF)
    io.put(0)


def attend_own_body(io):
    queries, sums, stats = io.outs
    part = mm(io.get(2)[...], io.weight(0)[...], NN) + io.get(0)[0:1, :]
    queries[...] = turn_wide(part, io.get(1), 1.0).astype(BF)
    io.put(0)
    kv, mask = io.get(3), io.get(4)
    heads = queries.shape[1] // HD
    for head in range(heads):
        span = slice(head * HD, (head + 1) * HD)
        scores = mm(kv[0, :, span], queries[:, span], NT) * SCALE + mask[...]
        top = jnp.max(scores, axis=0, keepdims=True)
        exps = jnp.exp(scores - top)
        stats[head : head + 1, :] = top
        stats[heads + head : heads + head + 1, :] = jnp.sum(exps, axis=0, keepdims=True)
        sums[span, :] = mm(kv[1, :, span], exps.astype(BF), TN)
    io.put(1)
    io.put(2)


def attend_other_body(io):
    queries, kv, mask, sums, stats = (io.get(at) for at in range(5))
    mixed, log_total, part = io.outs
    heads = queries.shape[1] // HD
    pair = []
    for head in range(heads):
        span = slice(head * HD, (head + 1) * HD)
        scores = mm(kv[0, :, span], queries[:, span], NT) * SCALE + mask[...]
        own_top = stats[head : head + 1, :]
        top = jnp.maximum(own_top, jnp.max(scores, axis=0, keepdims=True))
        exps = jnp.exp(scores - top)
        scale = jnp.exp(own_top - top)
        total = stats[heads + head : heads + head + 1, :] * scale
        total = total + jnp.sum(exps, axis=0, keepdims=True)
        result = sums[span, :] * scale + mm(kv[1, :, span], exps.astype(BF), TN)
        log_total[head : head + 1, :] = top + jnp.log(total)
        pair.append(result * (1.0 / total))
        if len(pair) == LANES // HD:
            wide = slice((head + 1) * HD - LANES, (head + 1) * HD)
            mixed[:, wide] = jnp.concatenate(pair, axis=0).T.astype(BF)
            pair = []
    io.put(0)
    io.put(1)
    part[...] = mm(mixed[...], io.weight(0)[...], NT).astype(BF)
    io.put(2)


def attend_body(n_blocks, io):
    queries = io.get(0)
    kvs = [io.get(1 + at) for at in range(n_blocks)]
    masks = [io.get(1 + n_blocks + at) for at in range(n_blocks)]
    mixed, log_total, part = io.outs
    for head in range(queries.shape[1] // HD):
        span = slice(head * HD, (head + 1) * HD)
        query = queries[:, span]
        scores = [
            mm(kv[0, :, span], query, NT) * SCALE + mask[...]
            for kv, mask in zip(kvs, masks, strict=True)
        ]
        top = functools.reduce(jnp.maximum, [jnp.max(s, axis=0, keepdims=True) for s in scores])
        exps = [jnp.exp(s - top) for s in scores]
        total = total_of([jnp.sum(e, axis=0, keepdims=True) for e in exps])
        inverse = 1.0 / total
        result = total_of(
            [
                mm((e * inverse).astype(BF), kv[1, :, span], TN)
                for e, kv in zip(exps, kvs, strict=True)
            ]
        )
        log_total[head : head + 1, :] = top + jnp.log(total)
        mixed[:, span] = result.astype(BF)
    io.put(0)
    io.put(1)
    part[...] = mm(mixed[...], io.weight(0)[...], NT).astype(BF)
    io.put(2)


def terms_sum(terms):
    return total_of([terms[at].astype(F32) for at in range(terms.shape[0])])


def norm_body(io):
    stream = terms_sum(io.get(0)) + io.get(1)[...].astype(F32)
    io.outs[0][...] = stream
    io.put(0)
    n, _ = normalized(stream)
    io.outs[1][...] = (n * io.get(2)[...] + io.get(3)[...]).astype(BF)
    io.put(1)


def sum_body(io):
    io.outs[0][...] = (terms_sum(io.get(0)) + io.get(1)[...].astype(F32)).astype(BF)
    io.put(0)


def mlp_body(io):
    gate_out, up_out, hidden, part = io.outs
    second_in = io.get(0)
    gate = mm(second_in[...], io.weight(0)[...], NN)
    gate_out[...] = gate.astype(BF)
    io.put(0)
    act = gate * jax.nn.sigmoid(gate)
    up = mm(second_in[...], io.weight(1)[...], NN)
    up_out[...] = up.astype(BF)
    io.put(1)
    hidden[...] = (act * up).astype(BF)
    io.put(2)
    part[...] = mm(hidden[...], io.weight(2)[...], NT).astype(BF)
    io.put(3)


def mlp_back_body(io):
    d_gate_up, part = io.outs
    d_mlp = io.get(2)
    gate = io.get(0)[...].astype(F32)
    sig = jax.nn.sigmoid(gate)
    d_hidden = mm(d_mlp[...], io.weight(0)[...], NN)
    d_gate_up[1] = (d_hidden * (gate * sig)).astype(BF)
    d_gate_up[0] = (
        d_hidden * io.get(1)[...].astype(F32) * (sig * (1.0 + gate * (1.0 - sig)))
    ).astype(BF)
    io.put(0)
    total = mm(d_gate_up[0], io.weight(1)[...], NT)
    total = total + mm(d_gate_up[1], io.weight(2)[...], NT)
    part[...] = total.astype(BF)
    io.put(1)


def mlp_both_body(io):
    hidden, part_out, d_gate_up, part = io.outs
    second_in = io.get(0)
    gate = mm(second_in[...], io.weight(0)[...], NN)
    sig = jax.nn.sigmoid(gate)
    act = gate * sig
    slope = sig * (1.0 + gate * (1.0 - sig))
    up = mm(second_in[...], io.weight(1)[...], NN)
    hidden[...] = (act * up).astype(BF)
    io.put(0)
    down = io.weight(2)
    d_hidden = mm(io.get(1)[...], down[...], NN)
    d_gate_up[1] = (d_hidden * act).astype(BF)
    d_gate_up[0] = (d_hidden * up * slope).astype(BF)
    io.put(2)
    total = mm(d_gate_up[0], io.weight(0)[...], NT)
    total = total + mm(d_gate_up[1], io.weight(1)[...], NT)
    part[...] = total.astype(BF)
    io.put(3)
    part_out[...] = mm(hidden[...], down[...], NT).astype(BF)
    io.put(1)


def norm_back_body(io):
    c = terms_sum(io.get(0))
    grad, n = norm_back(io.get(1)[...].astype(F32), c, io.get(2)[...])
    grad = io.get(3)[...].astype(F32) + grad
    io.outs[0][...] = grad
    io.put(0)
    io.outs[1][...] = grad.astype(BF)
    io.put(1)
    io.outs[2][0:1, :] = jnp.sum(n * c, axis=0, keepdims=True)
    io.outs[2][1:2, :] = jnp.sum(c, axis=0, keepdims=True)
    io.put(2)


def attend_back_body(n_blocks, io):
    d_query, d_kvs = io.outs[0], io.outs[1:]
    d_mixed = io.extra[0]
    d_mixed[...] = mm(io.get(0)[...], io.weight(0)[...], NN).astype(BF)
    queries, log_total, tables = io.get(1), io.get(2), io.get(3)
    kvs = [io.get(4 + at) for at in range(n_blocks)]
    masks = [io.get(4 + n_blocks + at) for at in range(n_blocks)]
    pair = []
    for head in range(queries.shape[1] // HD):
        span = slice(head * HD, (head + 1) * HD)
        query = queries[:, span]
        d_out = d_mixed[:, span]
        row_log = log_total[head : head + 1, :]
        probs = [
            jnp.exp(mm(kv[0, :, span], query, NT) * SCALE + mask[...] - row_log)
            for kv, mask in zip(kvs, masks, strict=True)
        ]
        d_probs = [mm(kv[1, :, span], d_out, NT) for kv in kvs]
        delta = total_of(
            [jnp.sum(p * dp, axis=0, keepdims=True) for p, dp in zip(probs, d_probs, strict=True)]
        )
        d_scores = [
            (p * (dp - delta)).astype(BF) for p, dp in zip(probs, d_probs, strict=True)
        ]
        pair.append(
            total_of([mm(ds, kv[0, :, span], TN) for ds, kv in zip(d_scores, kvs, strict=True)])
            * SCALE
        )
        if len(pair) == LANES // HD:
            wide = slice((head + 1) * HD - LANES, (head + 1) * HD)
            d_query[:, wide] = turn_wide(jnp.concatenate(pair, axis=1), tables, -1.0).astype(BF)
            pair = []
        for ds, p, d_kv in zip(d_scores, probs, d_kvs, strict=True):
            d_kv[0, :, span] = (mm(ds, query, NN) * SCALE).astype(d_kv.dtype)
            d_kv[1, :, span] = mm(p.astype(BF), d_out, NN).astype(d_kv.dtype)
    for at in range(1 + n_blocks):
        io.put(at)


def qkv_back_body(n_other, io):
    d_qkv, bias, part = io.outs
    tables = io.get(1)
    terms = [io.get(2 + at) for at in range(1 + n_other)]
    d_qkv[0] = io.get(0)[...]
    d_qkv[1] = turn_wide(
        total_of([term[0].astype(F32) for term in terms]), tables, -1.0
    ).astype(BF)
    d_qkv[2] = total_of([term[1].astype(F32) for term in terms]).astype(BF)
    io.put(0)
    for index in range(3):
        bias[index : index + 1, :] = jnp.sum(d_qkv[index].astype(F32), axis=0, keepdims=True)
    io.put(1)
    part[...] = total_of(
        [mm(d_qkv[index], io.weight(index)[...], NT) for index in range(3)]
    ).astype(BF)
    io.put(2)


def pack_body(io):
    gate_up, down = io.get(0), io.get(1)
    for part in range(2):
        io.outs[0][part] = gate_up[:, part, :]
    if len(io.outs) == 1:
        io.outs[0][2] = down[...].T
        io.put(0)
    else:
        io.put(0)
        io.outs[1][0] = down[...].T
        io.put(1)


def add_body(io):
    io.outs[0][...] = (io.get(0)[...].astype(F32) + io.get(2)[...].astype(F32)).astype(BF)
    io.put(0)
    io.outs[1][...] = (io.get(1)[...].astype(F32) + io.get(3)[...].astype(F32)).astype(BF)
    io.put(1)


def finish_body(is_mlp, io):
    own, x1, y1, x2, y2 = (io.get(at) for at in range(5))
    half = own.shape[2]
    main, other = io.outs
    matrices = own.shape[1]
    for side, (one, two) in enumerate(((x1, y2), (y1, x2))):
        rows = slice(side * half, (side + 1) * half)
        for matrix in range(matrices):
            whole = (
                own[side, matrix].astype(F32) + one[matrix].astype(F32) + two[matrix].astype(F32)
            )
            if matrix == matrices - 1:
                other[:, rows] = whole.T
            elif is_mlp:
                main[rows, matrix, :] = whole
            else:
                main[matrix, rows, :] = whole
    io.put(0)
    io.put(1)


def weight_grad_body(counts, n_left, pairs, *refs):
    ids = refs[0]
    n_in, n_held = len(counts), sum(counts)
    own = refs[1 : 1 + n_in]
    peer = refs[1 + n_in : 1 + 2 * n_in]
    outs = refs[1 + 2 * n_in : 6 + 2 * n_in]
    held = refs[6 + 2 * n_in : 6 + 2 * n_in + n_held]
    stage, in_sems, out_sems = refs[6 + 2 * n_in + n_held :]
    rows = held[0].shape[0] // 2
    loads = []
    for part, side in enumerate((own, peer)):
        at = 0
        for source, count in zip(side, counts, strict=True):
            for index in range(count):
                copy = pltpu.make_async_copy(
                    source if len(source.shape) == 2 else source.at[index],
                    held[at].at[pl.ds(part * rows, rows), :],
                    in_sems.at[at, part],
                )
                copy.start()
                loads.append(copy)
                at += 1
    for copy in loads:
        copy.wait()
    half = stage.shape[2]
    own_out, x1, y1, x2, y2 = outs
    targets = (
        (x1.at[0], y1.at[0]),
        (x1.at[1], x2),
        (y2, y1.at[1]),
        (own_out.at[0], own_out.at[1]),
    )
    stores = []
    for block in range(4):
        start = pl.multiple_of(ids[block], LANES)
        for matrix, (left, right) in enumerate(pairs):
            lhs = held[left][:, pl.ds(start, 2 * half)]
            result = mm(lhs, held[n_left + right][...], TN).astype(BF)
            stage[2 * block, matrix] = result[:half]
            stage[2 * block + 1, matrix] = result[half:]
        for part in range(2):
            copy = pltpu.make_async_copy(
                stage.at[2 * block + part], targets[block][part], out_sems.at[block, part]
            )
            copy.start()
            stores.append(copy)
    for copy in stores:
        copy.wait()


def after(array, *earlier):
    return lax.optimization_barrier((array,) + earlier)[0]


def pairs_of(axis, bit):
    return [(index, index ^ bit) for index in range(lax.axis_size(axis))]


def swap_x(array):
    return lax.ppermute(array, "fsdp", pairs_of("fsdp", 2))


def swap_core(array):
    return lax.ppermute(array, "fsdp", pairs_of("fsdp", 1))


def swap_y(array):
    return lax.ppermute(array, "ctx", pairs_of("ctx", 1))


def place():
    fsdp = lax.axis_index("fsdp")
    return fsdp // 2, fsdp % 2, lax.axis_index("ctx")


class Gather:
    def __init__(self, shard):
        self.shard = shard
        self.rows = shard.shape[1]

    def near_x(self, wait=()):
        self.from_x = swap_x(after(self.shard, *wait))

    def near_y(self, wait=()):
        self.from_y = swap_y(after(self.shard, *wait))
        self.mine = [self.shard, self.from_x, self.from_y]

    def near(self, wait_x=(), wait_y=()):
        self.near_x(wait_x)
        self.near_y(wait_y)

    def swap(self, *wait):
        self.peers = [swap_core(after(piece, *wait)) for piece in self.mine]

    def far(self, way, wait_x=(), wait_y=()):
        half = self.rows // 2
        self.way = way
        if way == "x":
            self.pieces = [swap_x(after(self.from_y, *wait_x))]
        elif way == "y":
            self.pieces = [swap_y(after(self.from_x, *wait_y))]
        else:
            self.pieces = [
                swap_x(after(self.from_y[:, :half], *wait_x)),
                swap_y(after(self.from_x[:, half:], *wait_y)),
            ]

    def all(self, *wait):
        far_peers = [swap_core(after(piece, *wait)) for piece in self.pieces]
        return self.mine + self.pieces + self.peers + far_peers


def piece_rows(rows):
    x, core, y = place()

    def row(x_at, core_at, y_at):
        return ((x_at * 2 + core_at) * 2 + y_at) * rows

    offs = []
    for halves in (0, 1):
        for core_at in (core, 1 - core):
            offs += [row(x, core_at, y), row(1 - x, core_at, y), row(x, core_at, 1 - y)]
            offs.append(row(1 - x, core_at, 1 - y))
            if halves:
                offs.append(row(1 - x, core_at, 1 - y) + rows // 2)
    return offs


def gather_whole(shard):
    return [lax.all_gather(shard, ("fsdp", "ctx"), axis=1, tiled=True)]


def gather_small(packed, fast):
    if not fast:
        return lax.all_gather(packed, ("fsdp", "ctx"), axis=1, tiled=True), ()
    x, core, y = place()

    def join(array, other, bit):
        return jnp.where(bit == 0, jnp.stack([array, other]), jnp.stack([other, array]))

    from_y = swap_y(packed)
    held = join(packed, from_y, y)
    held = join(held, swap_core(held), core)
    held = join(held, swap_x(held), x)
    rows, cols = packed.shape
    return held.transpose(3, 0, 1, 2, 4).reshape(rows, 8 * cols), (from_y,)


def reduce_small(sums, fast, *wait):
    if not fast:
        part = lax.psum_scatter(sums, ("fsdp", "ctx"), scatter_dimension=1, tiled=True)
        return lax.psum(part, "tp")
    x, core, y = place()
    rows, width = sums.shape
    held = sums.reshape(rows, 2, 2, 2, width // 8).transpose(1, 3, 2, 0, 4)
    for bit, swap in ((x, swap_x), (y, swap_y), (core, swap_core)):
        keep = jnp.where(bit == 0, held[0], held[1])
        send = jnp.where(bit == 0, held[1], held[0])
        held = keep + swap(after(send, *wait) if swap is swap_y else send)
    step = 1
    while step < lax.axis_size("tp"):
        held = held + lax.ppermute(held, "tp", pairs_of("tp", step))
        step *= 2
    return held


def tensor_scatter(part, *earlier):
    size = lax.axis_size("tp")
    blocks = after(part, *earlier).reshape(size, part.shape[0] // size, part.shape[1])
    return lax.all_to_all(blocks, "tp", 0, 0, tiled=True)


def tensor_gather(copies):
    return lax.all_to_all(copies, "tp", 0, 0, tiled=True)


def flat(blocks):
    return blocks.reshape(-1, blocks.shape[-1])


def weight_grads(own, peer, n_left, pairs, earlier, name):
    counts = tuple(1 if array.ndim == 2 else array.shape[0] for array in own)
    columns = own[-1].shape[-1]
    tokens, width = own[0].shape
    peer = [
        swap_core(after(array, *earlier)) if other is None else other
        for array, other in zip(own, peer, strict=True)
    ]
    rows = width // 8
    half = rows // 2
    x, core, y = place()
    ids = jnp.stack(
        [
            ((x_at * 2 + core) * 2 + y_at) * rows
            for x_at, y_at in ((1 - x, 1 - y), (1 - x, y), (x, 1 - y), (x, y))
        ]
    ).astype(jnp.int32)
    block = (len(pairs), half, columns)
    hbm = pl.BlockSpec(memory_space=pltpu.HBM)
    scratch = [
        pltpu.VMEM((2 * tokens, array.shape[-1]), BF)
        for array, count in zip(own, counts, strict=True)
        for _ in range(count)
    ]
    scratch += [
        pltpu.VMEM((8,) + block, BF),
        pltpu.SemaphoreType.DMA((sum(counts), 2)),
        pltpu.SemaphoreType.DMA((4, 2)),
    ]
    own_sum, x1, y1, x2, y2 = pl.pallas_call(
        functools.partial(weight_grad_body, counts, n_left, pairs),
        out_shape=[pltpu.HBM((2,) + block, BF)] * 3 + [pltpu.HBM(block, BF)] * 2,
        in_specs=[pl.BlockSpec(memory_space=pltpu.SMEM)] + [hbm] * (2 * len(own)),
        out_specs=[hbm] * 5,
        scratch_shapes=scratch,
        compiler_params=pltpu.CompilerParams(vmem_limit_bytes=VMEM_LIMIT),
        cost_estimate=cost(name),
        name=name,
    )(ids, *[pltpu.with_memory_space_constraint(a, pltpu.HBM) for a in list(own) + peer])
    return (own_sum, x2, y2), (x1, y1)


def add_received(spots, parts, received, earlier, name):
    _, x2, y2 = parts
    got_x1, got_y1 = received
    block = shape(x2.shape, BF)
    return kernel(
        add_body,
        name,
        spots,
        [after(x2, *earlier), y2, (got_y1, 0), (got_x1, 0)],
        [block, block],
    )


def send_second(parts, received, sums, earlier):
    far_x = swap_x(after(sums[0], *earlier))
    far_y = swap_y(after(sums[1], *earlier))
    return [parts[0], (received[0], 1), (received[1], 1), far_x, far_y]


def reduce_second(spots, parts, received, earlier_add, earlier_send, name):
    sums = add_received(spots, parts, received, earlier_add, name)
    return send_second(parts, received, sums, earlier_send), sums[0]


def layout(lengths, first_row, row_count):
    token_index = first_row + jnp.arange(row_count, dtype=jnp.int32)
    doc_ends = jnp.cumsum(lengths)
    starts = doc_ends - lengths
    segment = jnp.sum(
        (token_index[:, None] >= doc_ends[None, :]).astype(jnp.int32), axis=1, dtype=jnp.int32
    )
    doc_begin = jnp.max(
        jnp.where(token_index[:, None] >= starts[None, :], starts[None, :], 0), axis=1
    )
    return (segment, token_index - doc_begin, token_index)


def rotary_tables(position):
    frequency = 10000.0 ** (-jnp.arange(0, ROT, 2, dtype=F32) / ROT)
    angles = position.astype(F32)[:, None] * frequency[None, :]
    cos, sin = jnp.cos(angles), jnp.sin(angles)
    rows = position.shape[0]
    blank = jnp.zeros((rows, ROT // 2), F32)
    rest = HD - ROT
    keep = jnp.concatenate([cos, cos, jnp.ones((rows, rest), F32)], axis=1)
    below = jnp.concatenate([blank, sin, jnp.zeros((rows, rest), F32)], axis=1)
    above = jnp.concatenate([-sin, blank, jnp.zeros((rows, rest), F32)], axis=1)
    return jnp.stack([jnp.tile(t, (1, LANES // HD)) for t in (keep, below, above)])


def local(
    tokens,
    cotangent,
    doc_lengths,
    norm_gains,
    norm_biases,
    qkv_weight,
    qkv_bias,
    out_weight,
    gate_up_weight,
    down_weight,
):
    rows = tokens.shape[1]
    width = tokens.shape[2]
    heads_width = qkv_weight.shape[3]
    hidden_width = gate_up_weight.shape[3]
    heads = heads_width // HD
    layers = norm_gains.shape[0]
    block_rows = qkv_weight.shape[1]
    ctx_size = lax.axis_size("ctx")
    fast = lax.axis_size("fsdp") == 4 and ctx_size == 2
    ctx_rank = lax.axis_index("ctx")
    tensor_rank = lax.axis_index("tp")

    small = jnp.concatenate(
        [
            norm_gains.reshape(2 * layers, -1),
            norm_biases.reshape(2 * layers, -1),
            qkv_bias.reshape(3 * layers, -1),
        ]
    )
    small, sent_small = gather_small(small, fast)
    small = small.astype(F32)
    gains = small[: 2 * layers].reshape(layers, 2, width)
    shifts = small[2 * layers : 4 * layers].reshape(layers, 2, width)
    biases = lax.dynamic_slice_in_dim(
        small[4 * layers :], tensor_rank * heads_width, heads_width, 1
    ).reshape(layers, 3, heads_width)

    tensor_size = lax.axis_size("tp")
    block = rows // tensor_size
    spots = piece_rows(block_rows) if fast else [jnp.int32(0)]
    spots = jnp.stack([jnp.asarray(spot, jnp.int32) for spot in spots])
    spots_at = {8: 0, 10: 8, 1: 0}

    def slot(pieces, matrix):
        return (pieces, matrix, spots_at[len(pieces)])

    shards = []
    for layer in range(layers):
        if fast:
            counts = (3,) if layer == 0 else (2, 1)
            mlp_shards = kernel(
                pack_body,
                "pack",
                spots,
                [(gate_up_weight, layer), (down_weight, layer)],
                [shape((count, block_rows, hidden_width), BF) for count in counts],
            )
        else:
            mlp_shards = [
                jnp.concatenate(
                    [gate_up_weight[layer].transpose(1, 0, 2), down_weight[layer].T[None]]
                )
            ]
        qkv_shard, out_shard = qkv_weight[layer].transpose(1, 0, 2), out_weight[layer].T[None]
        shards.append((jnp.concatenate([qkv_shard, out_shard]), *mlp_shards))

    lengths = doc_lengths[0]
    seg_query, pos_query, index_query = layout(lengths, ctx_rank * rows, rows)
    tables = rotary_tables(pos_query)

    def mask_of(first, count, usable):
        seg_key, _, index_key = layout(lengths, first, count)
        allowed = (seg_query[None, :] == seg_key[:, None]) & (
            index_query[None, :] >= index_key[:, None]
        )
        return jnp.where(allowed & usable, 0.0, -1e30).astype(F32)

    if fast:
        masks = [
            mask_of(jnp.int32(0), rows, ctx_rank > 0),
            mask_of(ctx_rank * rows, rows, True),
        ]
    else:
        masks = [mask_of(jnp.int32(0), rows * ctx_size, True)]
    n_blocks = len(masks)

    wide = shape((rows, width), BF)
    inner = shape((rows, hidden_width), BF)
    headed = shape((rows, heads_width), BF)
    block_f = shape((block, width), F32)
    copies_b = (shape((tensor_size, block, width), BF), EACH)

    stream = lax.dynamic_slice_in_dim(tokens[0], tensor_rank * block, block, 0)
    first_in = None
    saved, groups = [], []
    if fast:
        attn_g, mlp_g = (Gather(shard) for shard in shards[0])
        attn_g.near((), sent_small)
        attn_g.swap()
        attn_g.far("both")
        mlp_g.near_x(attn_g.pieces[:1])
    for layer in range(layers):
        if fast:
            attn_pieces = attn_g.all()
        else:
            attn_pieces, mlp_pieces = (gather_whole(shard) for shard in shards[layer])
            mlp_slots = [slot(mlp_pieces, index) for index in range(3)]
        kv_shape = shape((2, rows, heads_width), BF)
        if layer == 0:
            args = [biases[0], tables, gains[0, 0][None], shifts[0, 0][None], tokens[0]]
            if fast:
                args[0] = after(args[0], mlp_g.shard)
        else:
            args = [biases[layer], tables, Free(first_in)]
        if fast:
            kv, *normed = kernel(
                functools.partial(key_value_body, layer == 0),
                "key_value",
                spots,
                args,
                [kv_shape] + ([wide] if layer == 0 else []),
                [slot(attn_pieces, index) for index in (1, 2)],
            )
        else:
            queries, kv, *normed = kernel(
                functools.partial(qkv_body, layer == 0),
                "qkv",
                spots,
                args,
                [headed, kv_shape] + ([wide] if layer == 0 else []),
                [slot(attn_pieces, index) for index in (1, 2, 0)],
            )
        if layer == 0:
            first_in = normed[0]
        attended = [headed, shape((heads, rows), F32), wide]
        if fast:
            prev = lax.ppermute(kv, "ctx", [(0, 1)])
            kv_blocks = [prev, kv]
            queries, value_sums, stats = kernel(
                attend_own_body,
                "attend_own",
                spots,
                [biases[layer], tables, Free(first_in), kv, masks[1]],
                [headed, shape((heads_width, rows), F32), shape((2 * heads, rows), F32)],
                [slot(attn_pieces, 0)],
            )
            if layer == 0:
                mlp_g.near_y((prev, queries))
            else:
                down_g.near_y((prev, queries))
            mixed, log_total, part = kernel(
                attend_other_body,
                "attend_other",
                spots,
                [queries, after(prev, queries), masks[0], value_sums, stats],
                attended,
                [slot(attn_pieces, 3)],
            )
        else:
            kv_blocks = [lax.all_gather(kv, "ctx", axis=1, tiled=True)]
            mixed, log_total, part = kernel(
                functools.partial(attend_body, n_blocks),
                "attend",
                spots,
                [queries] + kv_blocks + masks,
                attended,
                [slot(attn_pieces, 3)],
            )
        terms = tensor_scatter(part)
        if fast and layer == 0:
            terms = after(terms, mlp_g.from_x)
        elif fast:
            gu_g.swap(part)
            gu_g.far("both", (part,), (part,))
            terms = after(terms, down_g.from_x)
        mid, normed = kernel(
            norm_body,
            "norm",
            spots,
            [Free(terms), stream, gains[layer, 1][None], shifts[layer, 1][None]],
            [block_f, copies_b],
        )
        second_in = tensor_gather(normed)
        if fast:
            if layer == 0:
                mlp_g.swap(mid)
                mlp_g.far("both", (mid,), (mid,))
                mlp_pieces = mlp_g.all(second_in)
                mlp_slots = [slot(mlp_pieces, index) for index in range(3)]
                sent = mlp_g.pieces
            else:
                down_g.swap(mid)
                down_g.far("both", (mid,), (mid,))
                gu_pieces, down_pieces = gu_g.all(), down_g.all(second_in)
                mlp_slots = [slot(gu_pieces, 0), slot(gu_pieces, 1), slot(down_pieces, 0)]
                sent = down_g.pieces
        second_in = flat(second_in)
        if layer < layers - 1:
            gate, up, hidden, part = kernel(
                mlp_body,
                "mlp",
                spots,
                [Free(second_in)],
                [inner, inner, inner, wide],
                mlp_slots,
            )
        else:
            peer = swap_core(cotangent[0]) if fast else ()
            hidden, last_part, d_gate_up, part = kernel(
                mlp_both_body,
                "mlp_both",
                spots,
                [Free(second_in), after(cotangent[0], peer)],
                [inner, wide, shape((2, rows, hidden_width), BF), wide],
                mlp_slots,
            )
            gate, up, last_mid = None, None, mid
        saved.append((stream, first_in, queries, kv_blocks, mixed, log_total, mid))
        saved[-1] += (second_in, gate, up, hidden)
        groups.append((attn_pieces, mlp_slots))
        if layer == layers - 1:
            break
        terms = tensor_scatter(part)
        if fast:
            attn_g, gu_g, down_g = (Gather(shard) for shard in shards[layer + 1])
            attn_g.near(sent[:1], sent[1:])
            attn_g.swap(part)
            attn_g.far("both", (part,), (part,))
            gu_g.near(sent[:1], sent[1:])
            down_g.near_x((gu_g.from_x,))
            terms = after(terms, gu_g.shard, *attn_g.pieces, *attn_g.peers)
        stream, normed = kernel(
            norm_body,
            "norm",
            spots,
            [Free(terms), mid, gains[layer + 1, 0][None], shifts[layer + 1, 0][None]],
            [block_f, copies_b],
        )
        first_in = flat(tensor_gather(normed))
        if fast:
            first_in = after(first_in, gu_g.from_x, gu_g.from_y)

    attn_outs, mlp_outs, pending, mlp_pending = None, None, None, None
    sums = [None] * layers
    plain = [None] * layers
    grad = lax.dynamic_slice_in_dim(cotangent[0], tensor_rank * block, block, 0)
    d_mlp = cotangent[0]
    for layer in reversed(range(layers)):
        (stream, first_in, queries, kv_blocks, mixed, log_total, mid) = saved[layer][:7]
        (second_in, gate, up, hidden) = saved[layer][7:]
        attn_pieces, mlp_slots = groups[layer]
        late = layer == layers - 1
        mlp_peer = [None] * 4
        if late:
            mlp_peer[1] = peer
        else:
            if fast:
                mlp_peer[0], mlp_peer[3] = swap_core(second_in), swap_core(hidden)
                gate = after(gate, mlp_peer[0], mlp_peer[3])
            d_gate_up, part = kernel(
                mlp_back_body,
                "mlp_back",
                spots,
                [gate, up, Free(d_mlp)],
                [shape((2, rows, hidden_width), BF), wide],
                [mlp_slots[2], mlp_slots[0], mlp_slots[1]],
            )
        terms = tensor_scatter(part)
        pairs = ((0, 0), (0, 1), (1, 2))
        if fast:
            if pending is not None:
                part = after(part, *mlp_pending[3:])
            mlp_parts, (to_x, to_y) = weight_grads(
                [second_in, d_mlp, d_gate_up, hidden], mlp_peer, 2, pairs, (part,), "mlp_grads"
            )
            terms = after(terms, mlp_parts[0])
            if pending is not None:
                mlp_pending[0] = after(mlp_pending[0], mlp_parts[0])
                mlp_outs = mlp_finish(spots, mlp_outs, mlp_pending, layer + 1, layers)
                terms = after(terms, mlp_outs[0], *pending[1])
            got_x = swap_x(to_x)
            got_y = None if late else swap_y(to_y)
        else:
            mlp_grad = plain_grads(
                [second_in, d_mlp], [d_gate_up[0], d_gate_up[1], hidden], pairs
            )
        grad_mid, normed, sums_two = kernel(
            norm_back_body,
            "norm_back",
            spots,
            [Free(terms), mid, gains[layer, 1][None], grad],
            [block_f, copies_b, shape((2, width), F32)],
        )
        gathered = tensor_gather(normed)
        d_attn = flat(gathered)
        if layer == layers - 1:
            out_terms = tensor_scatter(last_part, gathered)
            (summed,) = kernel(sum_body, "sum", spots, [out_terms, last_mid], [copies_b])
        elif layer == layers - 2:
            out_blocks = tensor_gather(after(summed, gathered))
        kv_outs = [shape(kv.shape, BF) for kv in kv_blocks]
        if fast:
            kv_outs[-1] = shape((2, rows, heads_width), F32)
        d_query, *d_kvs = kernel(
            functools.partial(attend_back_body, n_blocks),
            "attend_back",
            spots,
            [Free(d_attn), queries, log_total, tables] + kv_blocks + masks,
            [headed] + kv_outs,
            [slot(attn_pieces, 3)],
            extra=[pltpu.VMEM((rows, heads_width), BF)],
        )
        if fast:
            own = d_kvs[1]
            other = [lax.ppermute(d_kvs[0] if late else after(d_kvs[0], got_y), "ctx", [(1, 0)])]
            if late:
                got_y = swap_y(after(to_y, other[0]))
                own = after(own, got_x)
            else:
                mlp_sums = add_received(spots, mlp_parts, (got_x, got_y), (d_kvs[0],), "mlp_add")
                own = after(own, mlp_sums[0])
                if pending is not None:
                    attn_sums = add_received(spots, *pending, (mlp_sums[0],), "attn_add")
                    own = after(own, attn_sums[0])
                    attn_terms = send_second(*pending, attn_sums, (other[0],))
                mlp_terms = send_second(mlp_parts, (got_x, got_y), mlp_sums, ())
            attn_peer = [swap_core(after(a, d_kvs[0])) for a in (first_in, d_attn)]
            attn_peer += [None, swap_core(after(mixed, d_kvs[0]))]
            own = after(own, attn_peer[0], attn_peer[1], attn_peer[3])
        else:
            own = lax.psum_scatter(d_kvs[0], "ctx", scatter_dimension=1, tiled=True)
            other = []
        if layer == layers - 1:
            own = after(own, out_terms)
        elif layer == layers - 2:
            own = after(own, out_blocks)
        d_qkv, bias_sums, part = kernel(
            functools.partial(qkv_back_body, len(other)),
            "qkv_back",
            spots,
            [d_query, tables, own] + other,
            [shape((3, rows, heads_width), BF), shape((3, heads_width), F32), wide],
            [slot(attn_pieces, index) for index in range(3)],
        )
        terms = tensor_scatter(part)
        if layer == layers - 1:
            terms = after(terms, summed)
        pairs = ((0, 0), (0, 1), (0, 2), (1, 3))
        if fast:
            ready = (part,) if late else (part, *mlp_terms[3:])
            attn_parts, (to_x, to_y) = weight_grads(
                [first_in, d_attn, d_qkv, mixed], attn_peer, 2, pairs, ready, "attn_grads"
            )
            pending = (attn_parts, (swap_x(to_x), swap_y(to_y)))
            terms = after(terms, attn_parts[0])
        else:
            rights = [d_qkv[0], d_qkv[1], d_qkv[2], mixed]
            plain[layer] = (plain_grads([first_in, d_attn], rights, pairs), mlp_grad)
        grad, normed, sums_one = kernel(
            norm_back_body,
            "norm_back",
            spots,
            [Free(terms), stream, gains[layer, 0][None], grad_mid],
            [block_f, copies_b, shape((2, width), F32)],
        )
        d_mlp = flat(tensor_gather(normed))
        if fast:
            if late:
                mlp_pending, mlp_added = reduce_second(
                    spots, mlp_parts, (got_x, got_y), (grad,), (), "mlp_add"
                )
                d_mlp = after(d_mlp, mlp_added)
            else:
                if mlp_pending is not None:
                    attn_terms[0] = after(attn_terms[0], grad)
                    attn_outs = attn_finish(spots, attn_outs, attn_terms, layer + 1, layers)
                mlp_terms[0] = after(mlp_terms[0], grad)
                mlp_outs = mlp_finish(spots, mlp_outs, mlp_terms, layer, layers)
        bias_rows = lax.dynamic_update_slice_in_dim(
            jnp.zeros((3, width), F32), bias_sums, tensor_rank * heads_width, 1
        )
        sums[layer] = jnp.concatenate(
            [sums_one[0:1], sums_two[0:1], sums_one[1:2], sums_two[1:2], bias_rows]
        )
    wait = ()
    if fast:
        attn_terms, attn_added = reduce_second(
            spots, *pending, (grad, mlp_outs[0], attn_outs[0]), (), "attn_add"
        )
        wait = (attn_added,)
    totals = reduce_small(jnp.concatenate(sums), fast, *wait).reshape(layers, 7, -1)
    if fast:
        attn_outs = attn_finish(spots, attn_outs, attn_terms, 0, layers)
    grad_input = d_mlp.astype(F32)
    if fast:
        grads = (attn_outs[0].transpose(0, 2, 1, 3), attn_outs[1], mlp_outs[0], mlp_outs[1])
    else:
        attn = jnp.stack([pair[0] for pair in plain])
        mlp = jnp.stack([pair[1] for pair in plain])
        grads = (
            attn[:, :3].transpose(0, 2, 1, 3),
            attn[:, 3].transpose(0, 2, 1),
            mlp[:, :2].transpose(0, 2, 1, 3),
            mlp[:, 2].transpose(0, 2, 1),
        )
    return (
        flat(out_blocks)[None],
        grad_input[None],
        totals[:, 0:2],
        totals[:, 2:4],
        grads[0],
        totals[:, 4:7],
        grads[1],
        grads[2],
        grads[3],
    )


def mlp_finish(spots, outs, terms, layer, layers):
    _, half, columns = terms[3].shape
    rows = 2 * half
    return kernel(
        functools.partial(finish_body, True),
        "mlp_finish",
        spots,
        terms,
        [
            (shape((layers, rows, 2, columns), F32), layer),
            (shape((layers, columns, rows), F32), layer),
        ],
        reuse=() if outs is None else ((outs[0], 0), (outs[1], 1)),
    )


def attn_finish(spots, outs, terms, layer, layers):
    matrices, half, columns = terms[3].shape
    rows = 2 * half
    return kernel(
        functools.partial(finish_body, False),
        "attn_finish",
        spots,
        terms,
        [
            (shape((layers, matrices - 1, rows, columns), F32), layer),
            (shape((layers, columns, rows), F32), layer),
        ],
        reuse=() if outs is None else ((outs[0], 0), (outs[1], 1)),
    )


def plain_grads(lefts, rights, pairs):
    whole = jnp.stack([mm(lefts[a], rights[b], TN).astype(BF) for a, b in pairs])
    return lax.psum_scatter(whole, ("fsdp", "ctx"), scatter_dimension=1, tiled=True).astype(F32)


def solution(mesh):
    return jax.shard_map(
        local,
        mesh=mesh,
        in_specs=(
            P("fsdp", "ctx", None),
            P("fsdp", "ctx", None),
            P("fsdp", None),
            P(None, None, ("fsdp", "ctx")),
            P(None, None, ("fsdp", "ctx")),
            P(None, ("fsdp", "ctx"), None, "tp"),
            P(None, None, ("fsdp", "ctx")),
            P(None, "tp", ("fsdp", "ctx")),
            P(None, ("fsdp", "ctx"), None, "tp"),
            P(None, "tp", ("fsdp", "ctx")),
        ),
        out_specs=(
            P("fsdp", "ctx", None),
            P("fsdp", "ctx", None),
            P(None, None, ("fsdp", "ctx")),
            P(None, None, ("fsdp", "ctx")),
            P(None, ("fsdp", "ctx"), None, "tp"),
            P(None, None, ("fsdp", "ctx")),
            P(None, "tp", ("fsdp", "ctx")),
            P(None, ("fsdp", "ctx"), None, "tp"),
            P(None, "tp", ("fsdp", "ctx")),
        ),
        check_vma=False,
    )
```

```python
import functools

import jax
import jax.numpy as jnp
from jax import lax
from jax.experimental import pallas as pl
from jax.experimental.pallas import tpu as pltpu
from jax.sharding import PartitionSpec as P

HD = 64
ROT = 16
LANES = 128
SCALE = 1.0 / HD**0.5
VMEM_LIMIT = 50 * 1024 * 1024
NN = (((1,), (0,)), ((), ()))
NT = (((1,), (1,)), ((), ()))
TN = (((0,), (0,)), ((), ()))
BF = jnp.bfloat16
F32 = jnp.float32
EACH = -1
HALVES = -2
TIMES = {
    "pack": 7.0,
    "qkv": 8.5,
    "attend": 8.0,
    "key_value": 6.5,
    "attend_own": 5.5,
    "attend_other": 5.5,
    "norm": 3.0,
    "mlp": 11.5,
    "mlp_back": 14.0,
    "mlp_both": 18.0,
    "norm_back": 3.5,
    "attend_back": 10.0,
    "qkv_back": 9.0,
    "mlp_grads": 10.5,
    "attn_grads": 7.0,
    "mlp_add": 4.0,
    "attn_add": 3.0,
    "mlp_finish": 7.5,
    "attn_finish": 4.5,
    "sum": 3.0,
}


def cost(name):
    return pl.CostEstimate(flops=0, bytes_accessed=int(TIMES[name] * 3.0e6), transcendentals=0)


def mm(lhs, rhs, dims):
    return lax.dot_general(lhs, rhs, dims, preferred_element_type=F32)


def shape(dims, dtype):
    return jax.ShapeDtypeStruct(tuple(dims), dtype)


class Free:
    def __init__(self, array):
        self.array = array


class Io:
    def __init__(self, ins, loads, outs, stores, held, weights, started, extra):
        self.ins, self.loads, self.outs, self.stores = ins, loads, outs, stores
        self.held, self.weights, self.started, self.extra = held, weights, started, extra
        self.there, self.held_there, self.gone = set(), set(), []

    def get(self, index):
        if index not in self.there:
            self.loads[index].wait()
            self.there.add(index)
        return self.ins[index]

    def weight(self, slot):
        if slot not in self.held_there:
            self.held_there.add(slot)
            self.begin(slot + 2)
            for copy in self.weights[slot]:
                copy.wait()
        return self.held[slot]

    def begin(self, count):
        while self.started < min(count, len(self.weights)):
            for copy in self.weights[self.started]:
                copy.start()
            self.started += 1

    def put(self, index):
        for copy in self.stores[index]:
            copy.start()
            self.gone.append(copy)

    def put_columns(self, index, value_of):
        out = self.outs[index]
        half = out.shape[1] // 2
        for side, copy in enumerate(self.stores[index]):
            columns = slice(side * half, (side + 1) * half)
            out[:, columns] = value_of(columns).astype(out.dtype)
            copy.start()
            self.gone.append(copy)


def kernel(body, name, spots, loads, outs, slots=(), eager=1, extra=(), reuse=()):
    free = [isinstance(item, Free) for item in loads]
    loads = [item.array if isinstance(item, Free) else item for item in loads]
    loads = [item if isinstance(item, tuple) else (item, None) for item in loads]
    outs = [item if isinstance(item, tuple) else (item, None) for item in outs]
    pieces, place_of = [], {}
    for group, _, _ in slots:
        for piece in group:
            if id(piece) not in place_of:
                place_of[id(piece)] = len(pieces)
                pieces.append(piece)
    slot_at = [([place_of[id(piece)] for piece in group], m, at) for group, m, at in slots]
    out_shapes = [item[0] for item in outs]
    n_in, n_piece, n_reuse = len(loads), len(pieces), len(reuse)

    def part(item):
        return tuple(item[0].shape) if item[1] in (None, HALVES) else tuple(item[0].shape[1:])

    def view(ref, index):
        return ref if index is None else ref.at[index]

    def run(*refs):
        refs = list(refs)

        def take(count):
            taken = refs[:count]
            del refs[:count]
            return taken

        starts = take(1)[0]
        in_hbm, piece_hbm, _ = take(n_in), take(n_piece), take(n_reuse)
        out_hbm = take(len(out_shapes))
        ins, results, held = take(n_in), take(len(outs)), take(len(slots))
        in_sems, out_sems = take(2)
        slot_sems = take(len(slots))
        load_copies = [
            pltpu.make_async_copy(view(ref, index), ins[at], in_sems.at[at])
            for at, (ref, (_, index)) in enumerate(zip(in_hbm, loads, strict=True))
        ]
        for copy in load_copies:
            copy.start()
        weight_sets = []
        for slot, (members, matrix, first) in enumerate(slot_at):
            copies = []
            for number, member in enumerate(members):
                piece = piece_hbm[member]
                row = pl.multiple_of(starts[first + number], 64)
                copies.append(
                    pltpu.make_async_copy(
                        piece.at[matrix],
                        held[slot].at[pl.ds(row, piece.shape[1]), :],
                        slot_sems[slot].at[number],
                    )
                )
            weight_sets.append(copies)
        stores = []
        for at, (ref, (_, index)) in enumerate(zip(out_hbm, outs, strict=True)):
            if index == EACH:
                stores.append(
                    [
                        pltpu.make_async_copy(results[at], ref.at[each], out_sems.at[at, each])
                        for each in range(ref.shape[0])
                    ]
                )
            elif index == HALVES:
                half = ref.shape[1] // 2
                stores.append(
                    [
                        pltpu.make_async_copy(
                            results[at].at[:, pl.ds(side * half, half)],
                            ref.at[:, pl.ds(side * half, half)],
                            out_sems.at[at, side],
                        )
                        for side in range(2)
                    ]
                )
            else:
                stores.append(
                    [pltpu.make_async_copy(results[at], view(ref, index), out_sems.at[at, 0])]
                )
        io = Io(ins, load_copies, results, stores, held, weight_sets, 0, refs)
        io.begin(eager)
        body(io)
        for at in range(n_in):
            io.get(at)
        for copy in io.gone:
            copy.wait()

    def in_hbm_now(array):
        return pltpu.with_memory_space_constraint(array, pltpu.HBM)

    args = [spots]
    args += [a if any_place else in_hbm_now(a) for (a, _), any_place in zip(loads, free, strict=True)]
    args += [in_hbm_now(piece) for piece in pieces]
    aliases = {len(args) + at: out for at, (_, out) in enumerate(reuse)}
    args += [in_hbm_now(array) for array, _ in reuse]
    hbm = pl.BlockSpec(memory_space=pltpu.HBM)
    most = max([out.shape[0] for out, index in outs if index == EACH], default=2)
    scratch = [pltpu.VMEM(part(item), item[0].dtype) for item in loads]
    scratch += [pltpu.VMEM(part(item), item[0].dtype) for item in outs]
    scratch += [
        pltpu.VMEM((sum(piece.shape[1] for piece in group), group[0].shape[2]), group[0].dtype)
        for group, _, _ in slots
    ]
    scratch += [
        pltpu.SemaphoreType.DMA((max(n_in, 1),)),
        pltpu.SemaphoreType.DMA((len(outs), most)),
    ]
    scratch += [pltpu.SemaphoreType.DMA((len(group),)) for group, _, _ in slots]
    return pl.pallas_call(
        run,
        out_shape=[pltpu.HBM(out.shape, out.dtype) for out in out_shapes],
        in_specs=[pl.BlockSpec(memory_space=pltpu.SMEM)]
        + [pl.BlockSpec(memory_space=pl.ANY) if any_place else hbm for any_place in free]
        + [hbm] * (n_piece + n_reuse),
        out_specs=[hbm] * len(out_shapes),
        scratch_shapes=scratch + list(extra),
        input_output_aliases=aliases,
        compiler_params=pltpu.CompilerParams(vmem_limit_bytes=VMEM_LIMIT),
        cost_estimate=cost(name),
        name=name,
    )(*args)


def normalized(v):
    centered = v - jnp.mean(v, axis=1, keepdims=True)
    variance = jnp.mean(centered * centered, axis=1, keepdims=True)
    scale = lax.rsqrt(variance + 1e-05)
    return centered * scale, scale


def norm_back(v, cot, gain):
    n, scale = normalized(v)
    e = cot * gain
    grad = scale * (
        e - jnp.mean(e, axis=1, keepdims=True) - n * jnp.mean(e * n, axis=1, keepdims=True)
    )
    return grad, n


def turn_wide(wide, tables, sign):
    keep, below, above = tables[0], tables[1], tables[2]
    turned = []
    for at in range(0, wide.shape[1], LANES):
        tile = wide[:, at : at + LANES]
        moved = pltpu.roll(tile, 8, 1) * below + pltpu.roll(tile, LANES - 8, 1) * above
        turned.append(tile * keep + sign * moved)
    return jnp.concatenate(turned, axis=1)


def total_of(terms):
    return functools.reduce(jnp.add, terms)


def qkv_body(has_norm, io):
    queries, kv = io.outs[:2]
    if has_norm:
        first_in = io.outs[2]
        n, _ = normalized(io.get(4)[...].astype(F32))
        first_in[...] = (n * io.get(2)[...] + io.get(3)[...]).astype(BF)
        io.put(2)
    else:
        first_in = io.get(2)
    bias, tables = io.get(0), io.get(1)
    for slot, index in enumerate((1, 2, 0)):
        part = mm(first_in[...], io.weight(slot)[...], NN) + bias[index : index + 1, :]
        if index < 2:
            part = turn_wide(part, tables, 1.0)
        if index == 0:
            queries[...] = part.astype(BF)
        else:
            kv[index - 1] = part.astype(BF)
    io.put(1)
    io.put(0)


def key_value_body(has_norm, io):
    kv = io.outs[0]
    if has_norm:
        first_in = io.outs[1]
        n, _ = normalized(io.get(4)[...].astype(F32))
        first_in[...] = (n * io.get(2)[...] + io.get(3)[...]).astype(BF)
        io.put(1)
    else:
        first_in = io.get(2)
    bias, tables = io.get(0), io.get(1)
    keys = mm(first_in[...], io.weight(0)[...], NN) + bias[1:2, :]
    kv[0] = turn_wide(keys, tables, 1.0).astype(BF)
    kv[1] = (mm(first_in[...], io.weight(1)[...], NN) + bias[2:3, :]).astype(BF)
    io.put(0)


def attend_own_body(io):
    queries, sums, stats = io.outs
    part = mm(io.get(2)[...], io.weight(0)[...], NN) + io.get(0)[0:1, :]
    queries[...] = turn_wide(part, io.get(1), 1.0).astype(BF)
    io.put(0)
    kv, mask = io.get(3), io.get(4)
    heads = queries.shape[1] // HD
    for head in range(heads):
        span = slice(head * HD, (head + 1) * HD)
        scores = mm(kv[0, :, span], queries[:, span], NT) * SCALE + mask[...]
        top = jnp.max(scores, axis=0, keepdims=True)
        exps = jnp.exp(scores - top)
        stats[head : head + 1, :] = top
        stats[heads + head : heads + head + 1, :] = jnp.sum(exps, axis=0, keepdims=True)
        sums[span, :] = mm(kv[1, :, span], exps.astype(BF), TN)
    io.put(1)
    io.put(2)


def attend_other_body(io):
    queries, kv, mask, sums, stats = (io.get(at) for at in range(5))
    mixed, log_total, _ = io.outs
    heads = queries.shape[1] // HD
    pair = []
    for head in range(heads):
        span = slice(head * HD, (head + 1) * HD)
        scores = mm(kv[0, :, span], queries[:, span], NT) * SCALE + mask[...]
        own_top = stats[head : head + 1, :]
        top = jnp.maximum(own_top, jnp.max(scores, axis=0, keepdims=True))
        exps = jnp.exp(scores - top)
        scale = jnp.exp(own_top - top)
        total = stats[heads + head : heads + head + 1, :] * scale
        total = total + jnp.sum(exps, axis=0, keepdims=True)
        result = sums[span, :] * scale + mm(kv[1, :, span], exps.astype(BF), TN)
        log_total[head : head + 1, :] = top + jnp.log(total)
        pair.append(result * (1.0 / total))
        if len(pair) == LANES // HD:
            wide = slice((head + 1) * HD - LANES, (head + 1) * HD)
            mixed[:, wide] = jnp.concatenate(pair, axis=0).T.astype(BF)
            pair = []
    io.put(0)
    io.put(1)
    out_weight = io.weight(0)
    io.put_columns(2, lambda columns: mm(mixed[...], out_weight[columns, :], NT))


def attend_body(n_blocks, io):
    queries = io.get(0)
    kvs = [io.get(1 + at) for at in range(n_blocks)]
    masks = [io.get(1 + n_blocks + at) for at in range(n_blocks)]
    mixed, log_total, _ = io.outs
    for head in range(queries.shape[1] // HD):
        span = slice(head * HD, (head + 1) * HD)
        query = queries[:, span]
        scores = [
            mm(kv[0, :, span], query, NT) * SCALE + mask[...]
            for kv, mask in zip(kvs, masks, strict=True)
        ]
        top = functools.reduce(jnp.maximum, [jnp.max(s, axis=0, keepdims=True) for s in scores])
        exps = [jnp.exp(s - top) for s in scores]
        total = total_of([jnp.sum(e, axis=0, keepdims=True) for e in exps])
        inverse = 1.0 / total
        result = total_of(
            [
                mm((e * inverse).astype(BF), kv[1, :, span], TN)
                for e, kv in zip(exps, kvs, strict=True)
            ]
        )
        log_total[head : head + 1, :] = top + jnp.log(total)
        mixed[:, span] = result.astype(BF)
    io.put(0)
    io.put(1)
    out_weight = io.weight(0)
    io.put_columns(2, lambda columns: mm(mixed[...], out_weight[columns, :], NT))


def terms_sum(terms):
    return total_of([terms[at].astype(F32) for at in range(terms.shape[0])])


def norm_body(io):
    stream = terms_sum(io.get(0)) + io.get(1)[...].astype(F32)
    io.outs[0][...] = stream
    io.put(0)
    n, _ = normalized(stream)
    io.outs[1][...] = (n * io.get(2)[...] + io.get(3)[...]).astype(BF)
    io.put(1)


def sum_body(io):
    io.outs[0][...] = (terms_sum(io.get(0)) + io.get(1)[...].astype(F32)).astype(BF)
    io.put(0)


def mlp_body(io):
    gate_out, up_out, hidden, _ = io.outs
    second_in = io.get(0)
    gate = mm(second_in[...], io.weight(0)[...], NN)
    gate_out[...] = gate.astype(BF)
    io.put(0)
    act = gate * jax.nn.sigmoid(gate)
    up = mm(second_in[...], io.weight(1)[...], NN)
    up_out[...] = up.astype(BF)
    io.put(1)
    hidden[...] = (act * up).astype(BF)
    io.put(2)
    down = io.weight(2)
    io.put_columns(3, lambda columns: mm(hidden[...], down[columns, :], NT))


def mlp_back_body(io):
    d_gate_up, _ = io.outs
    d_mlp = io.get(2)
    gate = io.get(0)[...].astype(F32)
    sig = jax.nn.sigmoid(gate)
    d_hidden = mm(d_mlp[...], io.weight(0)[...], NN)
    d_gate_up[1] = (d_hidden * (gate * sig)).astype(BF)
    d_gate_up[0] = (
        d_hidden * io.get(1)[...].astype(F32) * (sig * (1.0 + gate * (1.0 - sig)))
    ).astype(BF)
    io.put(0)
    gates, ups = io.weight(1), io.weight(2)

    def gradient(columns):
        return mm(d_gate_up[0], gates[columns, :], NT) + mm(d_gate_up[1], ups[columns, :], NT)

    io.put_columns(1, gradient)


def mlp_both_body(io):
    hidden, _, d_gate_up, _ = io.outs
    second_in = io.get(0)
    gate = mm(second_in[...], io.weight(0)[...], NN)
    sig = jax.nn.sigmoid(gate)
    act = gate * sig
    slope = sig * (1.0 + gate * (1.0 - sig))
    up = mm(second_in[...], io.weight(1)[...], NN)
    hidden[...] = (act * up).astype(BF)
    io.put(0)
    down = io.weight(2)
    d_hidden = mm(io.get(1)[...], down[...], NN)
    d_gate_up[1] = (d_hidden * act).astype(BF)
    d_gate_up[0] = (d_hidden * up * slope).astype(BF)
    io.put(2)
    gates, ups = io.weight(0), io.weight(1)

    def gradient(columns):
        return mm(d_gate_up[0], gates[columns, :], NT) + mm(d_gate_up[1], ups[columns, :], NT)

    io.put_columns(3, gradient)
    io.put_columns(1, lambda columns: mm(hidden[...], down[columns, :], NT))


def norm_back_body(io):
    c = terms_sum(io.get(0))
    grad, n = norm_back(io.get(1)[...].astype(F32), c, io.get(2)[...])
    grad = io.get(3)[...].astype(F32) + grad
    io.outs[0][...] = grad
    io.put(0)
    io.outs[1][...] = grad.astype(BF)
    io.put(1)
    io.outs[2][0:1, :] = jnp.sum(n * c, axis=0, keepdims=True)
    io.outs[2][1:2, :] = jnp.sum(c, axis=0, keepdims=True)
    io.put(2)


def attend_back_body(n_blocks, io):
    d_query, d_kvs = io.outs[0], io.outs[1:]
    d_mixed = io.extra[0]
    d_mixed[...] = mm(io.get(0)[...], io.weight(0)[...], NN).astype(BF)
    queries, log_total, tables = io.get(1), io.get(2), io.get(3)
    kvs = [io.get(4 + at) for at in range(n_blocks)]
    masks = [io.get(4 + n_blocks + at) for at in range(n_blocks)]
    pair = []
    for head in range(queries.shape[1] // HD):
        span = slice(head * HD, (head + 1) * HD)
        query = queries[:, span]
        d_out = d_mixed[:, span]
        row_log = log_total[head : head + 1, :]
        probs = [
            jnp.exp(mm(kv[0, :, span], query, NT) * SCALE + mask[...] - row_log)
            for kv, mask in zip(kvs, masks, strict=True)
        ]
        d_probs = [mm(kv[1, :, span], d_out, NT) for kv in kvs]
        delta = total_of(
            [jnp.sum(p * dp, axis=0, keepdims=True) for p, dp in zip(probs, d_probs, strict=True)]
        )
        d_scores = [
            (p * (dp - delta)).astype(BF) for p, dp in zip(probs, d_probs, strict=True)
        ]
        pair.append(
            total_of([mm(ds, kv[0, :, span], TN) for ds, kv in zip(d_scores, kvs, strict=True)])
            * SCALE
        )
        if len(pair) == LANES // HD:
            wide = slice((head + 1) * HD - LANES, (head + 1) * HD)
            d_query[:, wide] = turn_wide(jnp.concatenate(pair, axis=1), tables, -1.0).astype(BF)
            pair = []
        for ds, p, d_kv in zip(d_scores, probs, d_kvs, strict=True):
            d_kv[0, :, span] = (mm(ds, query, NN) * SCALE).astype(d_kv.dtype)
            d_kv[1, :, span] = mm(p.astype(BF), d_out, NN).astype(d_kv.dtype)
    for at in range(1 + n_blocks):
        io.put(at)


def qkv_back_body(n_other, io):
    d_qkv, bias, _ = io.outs
    tables = io.get(1)
    terms = [io.get(2 + at) for at in range(1 + n_other)]
    d_qkv[0] = io.get(0)[...]
    d_qkv[1] = turn_wide(
        total_of([term[0].astype(F32) for term in terms]), tables, -1.0
    ).astype(BF)
    d_qkv[2] = total_of([term[1].astype(F32) for term in terms]).astype(BF)
    io.put(0)
    for index in range(3):
        bias[index : index + 1, :] = jnp.sum(d_qkv[index].astype(F32), axis=0, keepdims=True)
    io.put(1)
    weights = [io.weight(index) for index in range(3)]

    def gradient(columns):
        return total_of([mm(d_qkv[at], weights[at][columns, :], NT) for at in range(3)])

    io.put_columns(2, gradient)


def pack_body(io):
    gate_up, down = io.get(0), io.get(1)
    if len(io.outs) == 1:
        matrices = [io.outs[0].at[at] for at in range(3)]
    else:
        matrices = [out.at[0] for out in io.outs]
    matrices[0][...] = gate_up[:, 0, :]
    matrices[1][...] = gate_up[:, 1, :]
    matrices[2][...] = down[...].T
    for at in range(len(io.outs)):
        io.put(at)


def add_body(io):
    io.outs[0][...] = (io.get(0)[...].astype(F32) + io.get(2)[...].astype(F32)).astype(BF)
    io.put(0)
    io.outs[1][...] = (io.get(1)[...].astype(F32) + io.get(3)[...].astype(F32)).astype(BF)
    io.put(1)


def finish_body(is_mlp, io):
    own, x1, y1, x2, y2 = (io.get(at) for at in range(5))
    half = own.shape[2]
    main, other = io.outs
    matrices = own.shape[1]
    for side, (one, two) in enumerate(((x1, y2), (y1, x2))):
        rows = slice(side * half, (side + 1) * half)
        for matrix in range(matrices):
            whole = (
                own[side, matrix].astype(F32) + one[matrix].astype(F32) + two[matrix].astype(F32)
            )
            if matrix == matrices - 1:
                other[:, rows] = whole.T
            elif is_mlp:
                main[rows, matrix, :] = whole
            else:
                main[matrix, rows, :] = whole
    io.put(0)
    io.put(1)


def weight_grad_body(counts, n_left, pairs, *refs):
    ids = refs[0]
    n_in, n_held = len(counts), sum(counts)
    own = refs[1 : 1 + n_in]
    peer = refs[1 + n_in : 1 + 2 * n_in]
    outs = refs[1 + 2 * n_in : 6 + 2 * n_in]
    held = refs[6 + 2 * n_in : 6 + 2 * n_in + n_held]
    stage, in_sems, out_sems = refs[6 + 2 * n_in + n_held :]
    rows = held[0].shape[0] // 2
    loads = []
    for part, side in enumerate((own, peer)):
        at = 0
        for source, count in zip(side, counts, strict=True):
            for index in range(count):
                copy = pltpu.make_async_copy(
                    source if len(source.shape) == 2 else source.at[index],
                    held[at].at[pl.ds(part * rows, rows), :],
                    in_sems.at[at, part],
                )
                copy.start()
                loads.append(copy)
                at += 1
    for copy in loads:
        copy.wait()
    half = stage.shape[2]
    own_out, x1, y1, x2, y2 = outs
    targets = (
        (x1.at[0], y1.at[0]),
        (x1.at[1], x2),
        (y2, y1.at[1]),
        (own_out.at[0], own_out.at[1]),
    )
    stores = []
    for block in range(4):
        start = pl.multiple_of(ids[block], LANES)
        for matrix, (left, right) in enumerate(pairs):
            lhs = held[left][:, pl.ds(start, 2 * half)]
            result = mm(lhs, held[n_left + right][...], TN).astype(BF)
            stage[2 * block, matrix] = result[:half]
            stage[2 * block + 1, matrix] = result[half:]
        for part in range(2):
            copy = pltpu.make_async_copy(
                stage.at[2 * block + part], targets[block][part], out_sems.at[block, part]
            )
            copy.start()
            stores.append(copy)
    for copy in stores:
        copy.wait()


def after(array, *earlier):
    return lax.optimization_barrier((array,) + earlier)[0]


def pairs_of(axis, bit):
    return [(index, index ^ bit) for index in range(lax.axis_size(axis))]


def swap_x(array):
    return lax.ppermute(array, "fsdp", pairs_of("fsdp", 2))


def swap_core(array):
    return lax.ppermute(array, "fsdp", pairs_of("fsdp", 1))


def swap_y(array):
    return lax.ppermute(array, "ctx", pairs_of("ctx", 1))


def place():
    fsdp = lax.axis_index("fsdp")
    return fsdp // 2, fsdp % 2, lax.axis_index("ctx")


class Gather:
    def __init__(self, shard):
        self.shard = shard
        self.rows = shard.shape[1]

    def near_x(self, wait=()):
        self.from_x = swap_x(after(self.shard, *wait))

    def near_y(self, wait=()):
        self.from_y = swap_y(after(self.shard, *wait))
        self.mine = [self.shard, self.from_x, self.from_y]

    def near(self, wait_x=(), wait_y=()):
        self.near_x(wait_x)
        self.near_y(wait_y)

    def swap(self, *wait):
        self.peers = [swap_core(after(piece, *wait)) for piece in self.mine]

    def far(self, way, wait_x=(), wait_y=()):
        half = self.rows // 2
        self.way = way
        if way == "x":
            self.pieces = [swap_x(after(self.from_y, *wait_x))]
        elif way == "y":
            self.pieces = [swap_y(after(self.from_x, *wait_y))]
        else:
            self.pieces = [
                swap_x(after(self.from_y[:, :half], *wait_x)),
                swap_y(after(self.from_x[:, half:], *wait_y)),
            ]

    def all(self, *wait):
        far_peers = [swap_core(after(piece, *wait)) for piece in self.pieces]
        return self.mine + self.pieces + self.peers + far_peers


def piece_rows(rows):
    x, core, y = place()

    def row(x_at, core_at, y_at):
        return ((x_at * 2 + core_at) * 2 + y_at) * rows

    offs = []
    for halves in (0, 1):
        for core_at in (core, 1 - core):
            offs += [row(x, core_at, y), row(1 - x, core_at, y), row(x, core_at, 1 - y)]
            offs.append(row(1 - x, core_at, 1 - y))
            if halves:
                offs.append(row(1 - x, core_at, 1 - y) + rows // 2)
    return offs


def gather_whole(shard):
    return [lax.all_gather(shard, ("fsdp", "ctx"), axis=1, tiled=True)]


def gather_small(packed, fast):
    if not fast:
        return lax.all_gather(packed, ("fsdp", "ctx"), axis=1, tiled=True), ()
    x, core, y = place()

    def join(array, other, bit):
        return jnp.where(bit == 0, jnp.stack([array, other]), jnp.stack([other, array]))

    from_y = swap_y(packed)
    held = join(packed, from_y, y)
    held = join(held, swap_core(held), core)
    held = join(held, swap_x(held), x)
    rows, cols = packed.shape
    return held.transpose(3, 0, 1, 2, 4).reshape(rows, 8 * cols), (from_y,)


def reduce_small(sums, fast, *wait):
    if not fast:
        part = lax.psum_scatter(sums, ("fsdp", "ctx"), scatter_dimension=1, tiled=True)
        return lax.psum(part, "tp")
    x, core, y = place()
    rows, width = sums.shape
    held = sums.reshape(rows, 2, 2, 2, width // 8).transpose(1, 3, 2, 0, 4)
    for bit, swap in ((x, swap_x), (y, swap_y), (core, swap_core)):
        keep = jnp.where(bit == 0, held[0], held[1])
        send = jnp.where(bit == 0, held[1], held[0])
        held = keep + swap(after(send, *wait) if swap is swap_y else send)
    step = 1
    while step < lax.axis_size("tp"):
        held = held + lax.ppermute(held, "tp", pairs_of("tp", step))
        step *= 2
    return held


def tensor_scatter(part, *earlier):
    size = lax.axis_size("tp")
    blocks = after(part, *earlier).reshape(size, part.shape[0] // size, part.shape[1])
    return lax.all_to_all(blocks, "tp", 0, 0, tiled=True)


def tensor_gather(copies):
    return lax.all_to_all(copies, "tp", 0, 0, tiled=True)


def flat(blocks):
    return blocks.reshape(-1, blocks.shape[-1])


def weight_grads(own, peer, n_left, pairs, earlier, name):
    counts = tuple(1 if array.ndim == 2 else array.shape[0] for array in own)
    columns = own[-1].shape[-1]
    tokens, width = own[0].shape
    peer = [
        swap_core(after(array, *earlier)) if other is None else other
        for array, other in zip(own, peer, strict=True)
    ]
    rows = width // 8
    half = rows // 2
    x, core, y = place()
    ids = jnp.stack(
        [
            ((x_at * 2 + core) * 2 + y_at) * rows
            for x_at, y_at in ((1 - x, 1 - y), (1 - x, y), (x, 1 - y), (x, y))
        ]
    ).astype(jnp.int32)
    block = (len(pairs), half, columns)
    hbm = pl.BlockSpec(memory_space=pltpu.HBM)
    scratch = [
        pltpu.VMEM((2 * tokens, array.shape[-1]), BF)
        for array, count in zip(own, counts, strict=True)
        for _ in range(count)
    ]
    scratch += [
        pltpu.VMEM((8,) + block, BF),
        pltpu.SemaphoreType.DMA((sum(counts), 2)),
        pltpu.SemaphoreType.DMA((4, 2)),
    ]
    own_sum, x1, y1, x2, y2 = pl.pallas_call(
        functools.partial(weight_grad_body, counts, n_left, pairs),
        out_shape=[pltpu.HBM((2,) + block, BF)] * 3 + [pltpu.HBM(block, BF)] * 2,
        in_specs=[pl.BlockSpec(memory_space=pltpu.SMEM)] + [hbm] * (2 * len(own)),
        out_specs=[hbm] * 5,
        scratch_shapes=scratch,
        compiler_params=pltpu.CompilerParams(vmem_limit_bytes=VMEM_LIMIT),
        cost_estimate=cost(name),
        name=name,
    )(ids, *[pltpu.with_memory_space_constraint(a, pltpu.HBM) for a in list(own) + peer])
    return (own_sum, x2, y2), (x1, y1)


def add_received(spots, parts, received, earlier, name):
    _, x2, y2 = parts
    got_x1, got_y1 = received
    block = shape(x2.shape, BF)
    return kernel(
        add_body,
        name,
        spots,
        [after(x2, *earlier), y2, (got_y1, 0), (got_x1, 0)],
        [block, block],
    )


def send_second(parts, received, sums, earlier):
    far_x = swap_x(after(sums[0], *earlier))
    far_y = swap_y(after(sums[1], *earlier))
    return [parts[0], (received[0], 1), (received[1], 1), far_x, far_y]


def reduce_second(spots, parts, received, earlier_add, earlier_send, name):
    sums = add_received(spots, parts, received, earlier_add, name)
    return send_second(parts, received, sums, earlier_send), sums[0]


def layout(lengths, first_row, row_count):
    token_index = first_row + jnp.arange(row_count, dtype=jnp.int32)
    doc_ends = jnp.cumsum(lengths)
    starts = doc_ends - lengths
    segment = jnp.sum(
        (token_index[:, None] >= doc_ends[None, :]).astype(jnp.int32), axis=1, dtype=jnp.int32
    )
    doc_begin = jnp.max(
        jnp.where(token_index[:, None] >= starts[None, :], starts[None, :], 0), axis=1
    )
    return (segment, token_index - doc_begin, token_index)


def rotary_tables(position):
    frequency = 10000.0 ** (-jnp.arange(0, ROT, 2, dtype=F32) / ROT)
    angles = position.astype(F32)[:, None] * frequency[None, :]
    cos, sin = jnp.cos(angles), jnp.sin(angles)
    rows = position.shape[0]
    blank = jnp.zeros((rows, ROT // 2), F32)
    rest = HD - ROT
    keep = jnp.concatenate([cos, cos, jnp.ones((rows, rest), F32)], axis=1)
    below = jnp.concatenate([blank, sin, jnp.zeros((rows, rest), F32)], axis=1)
    above = jnp.concatenate([-sin, blank, jnp.zeros((rows, rest), F32)], axis=1)
    return jnp.stack([jnp.tile(t, (1, LANES // HD)) for t in (keep, below, above)])


def local(
    tokens,
    cotangent,
    doc_lengths,
    norm_gains,
    norm_biases,
    qkv_weight,
    qkv_bias,
    out_weight,
    gate_up_weight,
    down_weight,
):
    rows = tokens.shape[1]
    width = tokens.shape[2]
    heads_width = qkv_weight.shape[3]
    hidden_width = gate_up_weight.shape[3]
    heads = heads_width // HD
    layers = norm_gains.shape[0]
    block_rows = qkv_weight.shape[1]
    ctx_size = lax.axis_size("ctx")
    fast = lax.axis_size("fsdp") == 4 and ctx_size == 2
    ctx_rank = lax.axis_index("ctx")
    tensor_rank = lax.axis_index("tp")

    small = jnp.concatenate(
        [
            norm_gains.reshape(2 * layers, -1),
            norm_biases.reshape(2 * layers, -1),
            qkv_bias.reshape(3 * layers, -1),
        ]
    )
    small, sent_small = gather_small(small, fast)
    small = small.astype(F32)
    gains = small[: 2 * layers].reshape(layers, 2, width)
    shifts = small[2 * layers : 4 * layers].reshape(layers, 2, width)
    biases = lax.dynamic_slice_in_dim(
        small[4 * layers :], tensor_rank * heads_width, heads_width, 1
    ).reshape(layers, 3, heads_width)

    tensor_size = lax.axis_size("tp")
    block = rows // tensor_size
    spots = piece_rows(block_rows) if fast else [jnp.int32(0)]
    spots = jnp.stack([jnp.asarray(spot, jnp.int32) for spot in spots])
    spots_at = {8: 0, 10: 8, 1: 0}

    def slot(pieces, matrix):
        return (pieces, matrix, spots_at[len(pieces)])

    shards = []
    for layer in range(layers):
        if fast:
            counts = (3,) if layer == 0 else (1, 1, 1)
            mlp_shards = kernel(
                pack_body,
                "pack",
                spots,
                [(gate_up_weight, layer), (down_weight, layer)],
                [shape((count, block_rows, hidden_width), BF) for count in counts],
            )
        else:
            mlp_shards = [
                jnp.concatenate(
                    [gate_up_weight[layer].transpose(1, 0, 2), down_weight[layer].T[None]]
                )
            ]
        qkv_shard, out_shard = qkv_weight[layer].transpose(1, 0, 2), out_weight[layer].T[None]
        shards.append((jnp.concatenate([qkv_shard, out_shard]), *mlp_shards))

    lengths = doc_lengths[0]
    seg_query, pos_query, index_query = layout(lengths, ctx_rank * rows, rows)
    tables = rotary_tables(pos_query)

    def mask_of(first, count, usable):
        seg_key, _, index_key = layout(lengths, first, count)
        allowed = (seg_query[None, :] == seg_key[:, None]) & (
            index_query[None, :] >= index_key[:, None]
        )
        return jnp.where(allowed & usable, 0.0, -1e30).astype(F32)

    if fast:
        masks = [
            mask_of(jnp.int32(0), rows, ctx_rank > 0),
            mask_of(ctx_rank * rows, rows, True),
        ]
    else:
        masks = [mask_of(jnp.int32(0), rows * ctx_size, True)]
    n_blocks = len(masks)

    wide = shape((rows, width), BF)
    wide_out = (wide, HALVES)
    inner = shape((rows, hidden_width), BF)
    headed = shape((rows, heads_width), BF)
    block_f = shape((block, width), F32)
    copies_b = (shape((tensor_size, block, width), BF), EACH)

    stream = lax.dynamic_slice_in_dim(tokens[0], tensor_rank * block, block, 0)
    first_in = None
    saved, groups = [], []
    if fast:
        attn_g, mlp_g = (Gather(shard) for shard in shards[0])
        attn_g.near((), sent_small)
        attn_g.swap()
        attn_g.far("both")
        mlp_g.near_x(attn_g.pieces[:1])
    for layer in range(layers):
        if fast:
            attn_pieces = attn_g.all()
        else:
            attn_pieces, mlp_pieces = (gather_whole(shard) for shard in shards[layer])
            mlp_slots = [slot(mlp_pieces, index) for index in range(3)]
        kv_shape = shape((2, rows, heads_width), BF)
        if layer == 0:
            args = [biases[0], tables, gains[0, 0][None], shifts[0, 0][None], tokens[0]]
            if fast:
                args[0] = after(args[0], mlp_g.shard)
        else:
            args = [biases[layer], tables, Free(first_in)]
        if fast:
            kv, *normed = kernel(
                functools.partial(key_value_body, layer == 0),
                "key_value",
                spots,
                args,
                [kv_shape] + ([wide] if layer == 0 else []),
                [slot(attn_pieces, index) for index in (1, 2)],
            )
        else:
            queries, kv, *normed = kernel(
                functools.partial(qkv_body, layer == 0),
                "qkv",
                spots,
                args,
                [headed, kv_shape] + ([wide] if layer == 0 else []),
                [slot(attn_pieces, index) for index in (1, 2, 0)],
            )
        if layer == 0:
            first_in = normed[0]
        attended = [headed, shape((heads, rows), F32), wide_out]
        if fast:
            prev = lax.ppermute(kv, "ctx", [(0, 1)])
            kv_blocks = [prev, kv]
            queries, value_sums, stats = kernel(
                attend_own_body,
                "attend_own",
                spots,
                [biases[layer], tables, Free(first_in), kv, masks[1]],
                [headed, shape((heads_width, rows), F32), shape((2 * heads, rows), F32)],
                [slot(attn_pieces, 0)],
            )
            if layer == 0:
                mlp_g.near_y((prev, queries))
            else:
                up_g.near_y((prev, queries))
                down_g.near_y((up_g.from_y,))
            mixed, log_total, part = kernel(
                attend_other_body,
                "attend_other",
                spots,
                [queries, after(prev, queries), masks[0], value_sums, stats],
                attended,
                [slot(attn_pieces, 3)],
            )
        else:
            kv_blocks = [lax.all_gather(kv, "ctx", axis=1, tiled=True)]
            mixed, log_total, part = kernel(
                functools.partial(attend_body, n_blocks),
                "attend",
                spots,
                [queries] + kv_blocks + masks,
                attended,
                [slot(attn_pieces, 3)],
            )
        terms = tensor_scatter(part)
        if fast and layer == 0:
            terms = after(terms, mlp_g.from_x)
        elif fast:
            gate_g.swap(part)
            gate_g.far("both", (part,), (part,))
            up_g.swap(part)
            terms = after(terms, down_g.from_x, up_g.from_y)
        mid, normed = kernel(
            norm_body,
            "norm",
            spots,
            [Free(terms), stream, gains[layer, 1][None], shifts[layer, 1][None]],
            [block_f, copies_b],
        )
        second_in = tensor_gather(normed)
        if fast:
            if layer == 0:
                mlp_g.swap(mid)
                mlp_g.far("both", (mid,), (mid,))
                mlp_pieces = mlp_g.all(second_in)
                mlp_slots = [slot(mlp_pieces, index) for index in range(3)]
                sent = mlp_g.pieces
            else:
                up_g.far("both", (mid,), (mid,))
                down_g.swap(mid)
                down_g.far("both", (mid,), (mid,))
                mlp_groups = (gate_g.all(), up_g.all(), down_g.all(second_in))
                mlp_slots = [slot(pieces, 0) for pieces in mlp_groups]
                sent = down_g.pieces
        second_in = flat(second_in)
        if layer < layers - 1:
            gate, up, hidden, part = kernel(
                mlp_body,
                "mlp",
                spots,
                [Free(second_in)],
                [inner, inner, inner, wide_out],
                mlp_slots,
            )
        else:
            peer = swap_core(cotangent[0]) if fast else ()
            hidden, last_part, d_gate_up, part = kernel(
                mlp_both_body,
                "mlp_both",
                spots,
                [Free(second_in), after(cotangent[0], peer)],
                [inner, wide_out, shape((2, rows, hidden_width), BF), wide_out],
                mlp_slots,
            )
            gate, up, last_mid = None, None, mid
        saved.append((stream, first_in, queries, kv_blocks, mixed, log_total, mid))
        saved[-1] += (second_in, gate, up, hidden)
        groups.append((attn_pieces, mlp_slots))
        if layer == layers - 1:
            break
        terms = tensor_scatter(part)
        if fast:
            attn_g, gate_g, up_g, down_g = (Gather(shard) for shard in shards[layer + 1])
            attn_g.near(sent[:1], sent[1:])
            attn_g.swap(part)
            attn_g.far("both", (part,), (part,))
            gate_g.near(sent[:1], sent[1:])
            up_g.near_x((gate_g.from_x,))
            down_g.near_x((up_g.from_x,))
            terms = after(terms, gate_g.shard, *attn_g.pieces, *attn_g.peers)
        stream, normed = kernel(
            norm_body,
            "norm",
            spots,
            [Free(terms), mid, gains[layer + 1, 0][None], shifts[layer + 1, 0][None]],
            [block_f, copies_b],
        )
        first_in = flat(tensor_gather(normed))
        if fast:
            first_in = after(first_in, gate_g.from_x, gate_g.from_y)

    attn_outs, mlp_outs, pending, mlp_pending = None, None, None, None
    sums = [None] * layers
    plain = [None] * layers
    grad = lax.dynamic_slice_in_dim(cotangent[0], tensor_rank * block, block, 0)
    d_mlp = cotangent[0]
    for layer in reversed(range(layers)):
        (stream, first_in, queries, kv_blocks, mixed, log_total, mid) = saved[layer][:7]
        (second_in, gate, up, hidden) = saved[layer][7:]
        attn_pieces, mlp_slots = groups[layer]
        late = layer == layers - 1
        mlp_peer = [None] * 4
        if late:
            mlp_peer[1] = peer
        else:
            if fast:
                mlp_peer[0], mlp_peer[3] = swap_core(second_in), swap_core(hidden)
                gate = after(gate, mlp_peer[0], mlp_peer[3])
            d_gate_up, part = kernel(
                mlp_back_body,
                "mlp_back",
                spots,
                [gate, up, Free(d_mlp)],
                [shape((2, rows, hidden_width), BF), wide_out],
                [mlp_slots[2], mlp_slots[0], mlp_slots[1]],
            )
        terms = tensor_scatter(part)
        pairs = ((0, 0), (0, 1), (1, 2))
        if fast:
            if pending is not None:
                part = after(part, *mlp_pending[3:])
            mlp_parts, (to_x, to_y) = weight_grads(
                [second_in, d_mlp, d_gate_up, hidden], mlp_peer, 2, pairs, (part,), "mlp_grads"
            )
            terms = after(terms, mlp_parts[0])
            if pending is not None:
                mlp_pending[0] = after(mlp_pending[0], mlp_parts[0])
                mlp_outs = mlp_finish(spots, mlp_outs, mlp_pending, layer + 1, layers)
                terms = after(terms, mlp_outs[0], *pending[1])
            got_x = swap_x(to_x)
            got_y = None if late else swap_y(to_y)
        else:
            mlp_grad = plain_grads(
                [second_in, d_mlp], [d_gate_up[0], d_gate_up[1], hidden], pairs
            )
        grad_mid, normed, sums_two = kernel(
            norm_back_body,
            "norm_back",
            spots,
            [Free(terms), mid, gains[layer, 1][None], grad],
            [block_f, copies_b, shape((2, width), F32)],
        )
        gathered = tensor_gather(normed)
        d_attn = flat(gathered)
        if layer == layers - 1:
            out_terms = tensor_scatter(last_part, gathered)
            (summed,) = kernel(sum_body, "sum", spots, [out_terms, last_mid], [copies_b])
        elif layer == layers - 2:
            out_blocks = tensor_gather(after(summed, gathered))
        kv_outs = [shape(kv.shape, BF) for kv in kv_blocks]
        if fast:
            kv_outs[-1] = shape((2, rows, heads_width), F32)
        d_query, *d_kvs = kernel(
            functools.partial(attend_back_body, n_blocks),
            "attend_back",
            spots,
            [Free(d_attn), queries, log_total, tables] + kv_blocks + masks,
            [headed] + kv_outs,
            [slot(attn_pieces, 3)],
            extra=[pltpu.VMEM((rows, heads_width), BF)],
        )
        if fast:
            own = d_kvs[1]
            other = [lax.ppermute(d_kvs[0] if late else after(d_kvs[0], got_y), "ctx", [(1, 0)])]
            if late:
                got_y = swap_y(after(to_y, other[0]))
                own = after(own, got_x)
            else:
                mlp_sums = add_received(spots, mlp_parts, (got_x, got_y), (d_kvs[0],), "mlp_add")
                own = after(own, mlp_sums[0])
                if pending is not None:
                    attn_sums = add_received(spots, *pending, (mlp_sums[0],), "attn_add")
                    own = after(own, attn_sums[0])
                    attn_terms = send_second(*pending, attn_sums, (other[0],))
                mlp_terms = send_second(mlp_parts, (got_x, got_y), mlp_sums, ())
            attn_peer = [swap_core(after(a, d_kvs[0])) for a in (first_in, d_attn)]
            attn_peer += [None, swap_core(after(mixed, d_kvs[0]))]
            own = after(own, attn_peer[0], attn_peer[1], attn_peer[3])
        else:
            own = lax.psum_scatter(d_kvs[0], "ctx", scatter_dimension=1, tiled=True)
            other = []
        if layer == layers - 1:
            own = after(own, out_terms)
        elif layer == layers - 2:
            own = after(own, out_blocks)
        d_qkv, bias_sums, part = kernel(
            functools.partial(qkv_back_body, len(other)),
            "qkv_back",
            spots,
            [d_query, tables, own] + other,
            [shape((3, rows, heads_width), BF), shape((3, heads_width), F32), wide_out],
            [slot(attn_pieces, index) for index in range(3)],
        )
        terms = tensor_scatter(part)
        if layer == layers - 1:
            terms = after(terms, summed)
        pairs = ((0, 0), (0, 1), (0, 2), (1, 3))
        if fast:
            ready = (part,) if late else (part, *mlp_terms[3:])
            attn_parts, (to_x, to_y) = weight_grads(
                [first_in, d_attn, d_qkv, mixed], attn_peer, 2, pairs, ready, "attn_grads"
            )
            pending = (attn_parts, (swap_x(to_x), swap_y(to_y)))
            terms = after(terms, attn_parts[0])
        else:
            rights = [d_qkv[0], d_qkv[1], d_qkv[2], mixed]
            plain[layer] = (plain_grads([first_in, d_attn], rights, pairs), mlp_grad)
        grad, normed, sums_one = kernel(
            norm_back_body,
            "norm_back",
            spots,
            [Free(terms), stream, gains[layer, 0][None], grad_mid],
            [block_f, copies_b, shape((2, width), F32)],
        )
        d_mlp = flat(tensor_gather(normed))
        if fast:
            if late:
                mlp_pending, mlp_added = reduce_second(
                    spots, mlp_parts, (got_x, got_y), (grad,), (), "mlp_add"
                )
                d_mlp = after(d_mlp, mlp_added)
            else:
                if mlp_pending is not None:
                    attn_terms[0] = after(attn_terms[0], grad)
                    attn_outs = attn_finish(spots, attn_outs, attn_terms, layer + 1, layers)
                mlp_terms[0] = after(mlp_terms[0], grad)
                mlp_outs = mlp_finish(spots, mlp_outs, mlp_terms, layer, layers)
        bias_rows = lax.dynamic_update_slice_in_dim(
            jnp.zeros((3, width), F32), bias_sums, tensor_rank * heads_width, 1
        )
        sums[layer] = jnp.concatenate(
            [sums_one[0:1], sums_two[0:1], sums_one[1:2], sums_two[1:2], bias_rows]
        )
    wait = ()
    if fast:
        attn_terms, attn_added = reduce_second(
            spots, *pending, (grad, mlp_outs[0], attn_outs[0]), (), "attn_add"
        )
        wait = (attn_added,)
    totals = reduce_small(jnp.concatenate(sums), fast, *wait).reshape(layers, 7, -1)
    if fast:
        attn_outs = attn_finish(spots, attn_outs, attn_terms, 0, layers)
    grad_input = d_mlp.astype(F32)
    if fast:
        grads = (attn_outs[0].transpose(0, 2, 1, 3), attn_outs[1], mlp_outs[0], mlp_outs[1])
    else:
        attn = jnp.stack([pair[0] for pair in plain])
        mlp = jnp.stack([pair[1] for pair in plain])
        grads = (
            attn[:, :3].transpose(0, 2, 1, 3),
            attn[:, 3].transpose(0, 2, 1),
            mlp[:, :2].transpose(0, 2, 1, 3),
            mlp[:, 2].transpose(0, 2, 1),
        )
    return (
        flat(out_blocks)[None],
        grad_input[None],
        totals[:, 0:2],
        totals[:, 2:4],
        grads[0],
        totals[:, 4:7],
        grads[1],
        grads[2],
        grads[3],
    )


def mlp_finish(spots, outs, terms, layer, layers):
    _, half, columns = terms[3].shape
    rows = 2 * half
    return kernel(
        functools.partial(finish_body, True),
        "mlp_finish",
        spots,
        terms,
        [
            (shape((layers, rows, 2, columns), F32), layer),
            (shape((layers, columns, rows), F32), layer),
        ],
        reuse=() if outs is None else ((outs[0], 0), (outs[1], 1)),
    )


def attn_finish(spots, outs, terms, layer, layers):
    matrices, half, columns = terms[3].shape
    rows = 2 * half
    return kernel(
        functools.partial(finish_body, False),
        "attn_finish",
        spots,
        terms,
        [
            (shape((layers, matrices - 1, rows, columns), F32), layer),
            (shape((layers, columns, rows), F32), layer),
        ],
        reuse=() if outs is None else ((outs[0], 0), (outs[1], 1)),
    )


def plain_grads(lefts, rights, pairs):
    whole = jnp.stack([mm(lefts[a], rights[b], TN).astype(BF) for a, b in pairs])
    return lax.psum_scatter(whole, ("fsdp", "ctx"), scatter_dimension=1, tiled=True).astype(F32)


def solution(mesh):
    return jax.shard_map(
        local,
        mesh=mesh,
        in_specs=(
            P("fsdp", "ctx", None),
            P("fsdp", "ctx", None),
            P("fsdp", None),
            P(None, None, ("fsdp", "ctx")),
            P(None, None, ("fsdp", "ctx")),
            P(None, ("fsdp", "ctx"), None, "tp"),
            P(None, None, ("fsdp", "ctx")),
            P(None, "tp", ("fsdp", "ctx")),
            P(None, ("fsdp", "ctx"), None, "tp"),
            P(None, "tp", ("fsdp", "ctx")),
        ),
        out_specs=(
            P("fsdp", "ctx", None),
            P("fsdp", "ctx", None),
            P(None, None, ("fsdp", "ctx")),
            P(None, None, ("fsdp", "ctx")),
            P(None, ("fsdp", "ctx"), None, "tp"),
            P(None, None, ("fsdp", "ctx")),
            P(None, "tp", ("fsdp", "ctx")),
            P(None, ("fsdp", "ctx"), None, "tp"),
            P(None, "tp", ("fsdp", "ctx")),
        ),
        check_vma=False,
    )
```

```python
import functools

import jax
import jax.numpy as jnp
from jax import lax
from jax.experimental import pallas as pl
from jax.experimental.pallas import tpu as pltpu
from jax.sharding import PartitionSpec as P

HD = 64
ROT = 16
LANES = 128
SCALE = 1.0 / HD**0.5
VMEM_LIMIT = 50 * 1024 * 1024
NN = (((1,), (0,)), ((), ()))
NT = (((1,), (1,)), ((), ()))
TN = (((0,), (0,)), ((), ()))
BF = jnp.bfloat16
F32 = jnp.float32
EACH = -1
HALVES = -2
TIMES = {
    "pack": 7.0,
    "qkv": 8.5,
    "attend": 8.0,
    "key_value": 6.5,
    "attend_own": 5.5,
    "attend_other": 5.5,
    "norm": 3.0,
    "mlp": 11.5,
    "mlp_back": 14.0,
    "mlp_both": 18.0,
    "norm_back": 3.5,
    "attend_back": 10.0,
    "qkv_back": 9.0,
    "mlp_grads": 10.5,
    "attn_grads": 7.0,
    "mlp_add": 4.0,
    "attn_add": 3.0,
    "mlp_finish": 7.5,
    "attn_finish": 4.5,
    "sum": 3.0,
}


def cost(name):
    return pl.CostEstimate(flops=0, bytes_accessed=int(TIMES[name] * 3.0e6), transcendentals=0)


def mm(lhs, rhs, dims):
    return lax.dot_general(lhs, rhs, dims, preferred_element_type=F32)


def shape(dims, dtype):
    return jax.ShapeDtypeStruct(tuple(dims), dtype)


class Free:
    def __init__(self, array):
        self.array = array


class Io:
    def __init__(self, ins, loads, outs, stores, held, weights, started, extra):
        self.ins, self.loads, self.outs, self.stores = ins, loads, outs, stores
        self.held, self.weights, self.started, self.extra = held, weights, started, extra
        self.there, self.held_there, self.gone = set(), set(), []

    def get(self, index):
        if index not in self.there:
            self.loads[index].wait()
            self.there.add(index)
        return self.ins[index]

    def weight(self, slot):
        if slot not in self.held_there:
            self.held_there.add(slot)
            self.begin(slot + 2)
            for copy in self.weights[slot]:
                copy.wait()
        return self.held[slot]

    def begin(self, count):
        while self.started < min(count, len(self.weights)):
            for copy in self.weights[self.started]:
                copy.start()
            self.started += 1

    def put(self, index):
        for copy in self.stores[index]:
            copy.start()
            self.gone.append(copy)

    def put_columns(self, index, value_of):
        out = self.outs[index]
        half = out.shape[1] // 2
        for side, copy in enumerate(self.stores[index]):
            columns = slice(side * half, (side + 1) * half)
            out[:, columns] = value_of(columns).astype(out.dtype)
            copy.start()
            self.gone.append(copy)


def kernel(body, name, spots, loads, outs, slots=(), eager=1, extra=(), reuse=()):
    free = [isinstance(item, Free) for item in loads]
    loads = [item.array if isinstance(item, Free) else item for item in loads]
    loads = [item if isinstance(item, tuple) else (item, None) for item in loads]
    outs = [item if isinstance(item, tuple) else (item, None) for item in outs]
    pieces, place_of = [], {}
    for group, _, _ in slots:
        for piece in group:
            if id(piece) not in place_of:
                place_of[id(piece)] = len(pieces)
                pieces.append(piece)
    slot_at = [([place_of[id(piece)] for piece in group], m, at) for group, m, at in slots]
    out_shapes = [item[0] for item in outs]
    n_in, n_piece, n_reuse = len(loads), len(pieces), len(reuse)

    def part(item):
        return tuple(item[0].shape) if item[1] in (None, HALVES) else tuple(item[0].shape[1:])

    def view(ref, index):
        return ref if index is None else ref.at[index]

    def run(*refs):
        refs = list(refs)

        def take(count):
            taken = refs[:count]
            del refs[:count]
            return taken

        starts = take(1)[0]
        in_hbm, piece_hbm, _ = take(n_in), take(n_piece), take(n_reuse)
        out_hbm = take(len(out_shapes))
        ins, results, held = take(n_in), take(len(outs)), take(len(slots))
        in_sems, out_sems = take(2)
        slot_sems = take(len(slots))
        load_copies = [
            pltpu.make_async_copy(view(ref, index), ins[at], in_sems.at[at])
            for at, (ref, (_, index)) in enumerate(zip(in_hbm, loads, strict=True))
        ]
        for copy in load_copies:
            copy.start()
        weight_sets = []
        for slot, (members, matrix, first) in enumerate(slot_at):
            copies = []
            for number, member in enumerate(members):
                piece = piece_hbm[member]
                row = pl.multiple_of(starts[first + number], 64)
                copies.append(
                    pltpu.make_async_copy(
                        piece.at[matrix],
                        held[slot].at[pl.ds(row, piece.shape[1]), :],
                        slot_sems[slot].at[number],
                    )
                )
            weight_sets.append(copies)
        stores = []
        for at, (ref, (_, index)) in enumerate(zip(out_hbm, outs, strict=True)):
            if index == EACH:
                stores.append(
                    [
                        pltpu.make_async_copy(results[at], ref.at[each], out_sems.at[at, each])
                        for each in range(ref.shape[0])
                    ]
                )
            elif index == HALVES:
                half = ref.shape[1] // 2
                stores.append(
                    [
                        pltpu.make_async_copy(
                            results[at].at[:, pl.ds(side * half, half)],
                            ref.at[:, pl.ds(side * half, half)],
                            out_sems.at[at, side],
                        )
                        for side in range(2)
                    ]
                )
            else:
                stores.append(
                    [pltpu.make_async_copy(results[at], view(ref, index), out_sems.at[at, 0])]
                )
        io = Io(ins, load_copies, results, stores, held, weight_sets, 0, refs)
        io.begin(eager)
        body(io)
        for at in range(n_in):
            io.get(at)
        for copy in io.gone:
            copy.wait()

    def in_hbm_now(array):
        return pltpu.with_memory_space_constraint(array, pltpu.HBM)

    args = [spots]
    args += [a if any_place else in_hbm_now(a) for (a, _), any_place in zip(loads, free, strict=True)]
    args += [in_hbm_now(piece) for piece in pieces]
    aliases = {len(args) + at: out for at, (_, out) in enumerate(reuse)}
    args += [in_hbm_now(array) for array, _ in reuse]
    hbm = pl.BlockSpec(memory_space=pltpu.HBM)
    most = max([out.shape[0] for out, index in outs if index == EACH], default=2)
    scratch = [pltpu.VMEM(part(item), item[0].dtype) for item in loads]
    scratch += [pltpu.VMEM(part(item), item[0].dtype) for item in outs]
    scratch += [
        pltpu.VMEM((sum(piece.shape[1] for piece in group), group[0].shape[2]), group[0].dtype)
        for group, _, _ in slots
    ]
    scratch += [
        pltpu.SemaphoreType.DMA((max(n_in, 1),)),
        pltpu.SemaphoreType.DMA((len(outs), most)),
    ]
    scratch += [pltpu.SemaphoreType.DMA((len(group),)) for group, _, _ in slots]
    return pl.pallas_call(
        run,
        out_shape=[pltpu.HBM(out.shape, out.dtype) for out in out_shapes],
        in_specs=[pl.BlockSpec(memory_space=pltpu.SMEM)]
        + [pl.BlockSpec(memory_space=pl.ANY) if any_place else hbm for any_place in free]
        + [hbm] * (n_piece + n_reuse),
        out_specs=[hbm] * len(out_shapes),
        scratch_shapes=scratch + list(extra),
        input_output_aliases=aliases,
        compiler_params=pltpu.CompilerParams(vmem_limit_bytes=VMEM_LIMIT),
        cost_estimate=cost(name),
        name=name,
    )(*args)


def normalized(v):
    centered = v - jnp.mean(v, axis=1, keepdims=True)
    variance = jnp.mean(centered * centered, axis=1, keepdims=True)
    scale = lax.rsqrt(variance + 1e-05)
    return centered * scale, scale


def norm_back(v, cot, gain):
    n, scale = normalized(v)
    e = cot * gain
    grad = scale * (
        e - jnp.mean(e, axis=1, keepdims=True) - n * jnp.mean(e * n, axis=1, keepdims=True)
    )
    return grad, n


def turn_wide(wide, tables, sign):
    keep, below, above = tables[0], tables[1], tables[2]
    turned = []
    for at in range(0, wide.shape[1], LANES):
        tile = wide[:, at : at + LANES]
        moved = pltpu.roll(tile, 8, 1) * below + pltpu.roll(tile, LANES - 8, 1) * above
        turned.append(tile * keep + sign * moved)
    return jnp.concatenate(turned, axis=1)


def total_of(terms):
    return functools.reduce(jnp.add, terms)


def qkv_body(has_norm, io):
    queries, kv = io.outs[:2]
    if has_norm:
        first_in = io.outs[2]
        n, _ = normalized(io.get(4)[...].astype(F32))
        first_in[...] = (n * io.get(2)[...] + io.get(3)[...]).astype(BF)
        io.put(2)
    else:
        first_in = io.get(2)
    bias, tables = io.get(0), io.get(1)
    for slot, index in enumerate((1, 2, 0)):
        part = mm(first_in[...], io.weight(slot)[...], NN) + bias[index : index + 1, :]
        if index < 2:
            part = turn_wide(part, tables, 1.0)
        if index == 0:
            queries[...] = part.astype(BF)
        else:
            kv[index - 1] = part.astype(BF)
    io.put(1)
    io.put(0)


def key_value_body(has_norm, io):
    kv = io.outs[0]
    if has_norm:
        first_in = io.outs[1]
        n, _ = normalized(io.get(4)[...].astype(F32))
        first_in[...] = (n * io.get(2)[...] + io.get(3)[...]).astype(BF)
        io.put(1)
    else:
        first_in = io.get(2)
    bias, tables = io.get(0), io.get(1)
    keys = mm(first_in[...], io.weight(0)[...], NN) + bias[1:2, :]
    kv[0] = turn_wide(keys, tables, 1.0).astype(BF)
    kv[1] = (mm(first_in[...], io.weight(1)[...], NN) + bias[2:3, :]).astype(BF)
    io.put(0)


def attend_own_body(io):
    queries, sums, stats = io.outs
    part = mm(io.get(2)[...], io.weight(0)[...], NN) + io.get(0)[0:1, :]
    queries[...] = turn_wide(part, io.get(1), 1.0).astype(BF)
    io.put(0)
    kv, mask = io.get(3), io.get(4)
    heads = queries.shape[1] // HD
    for head in range(heads):
        span = slice(head * HD, (head + 1) * HD)
        scores = mm(kv[0, :, span], queries[:, span] * SCALE, NT) + mask[...]
        top = jnp.max(scores, axis=0, keepdims=True)
        exps = jnp.exp(scores - top)
        stats[head : head + 1, :] = top
        stats[heads + head : heads + head + 1, :] = jnp.sum(exps, axis=0, keepdims=True)
        sums[span, :] = mm(kv[1, :, span], exps.astype(BF), TN)
    io.put(1)
    io.put(2)


def attend_other_body(io):
    queries, kv, mask, sums, stats = (io.get(at) for at in range(5))
    mixed, log_total, _ = io.outs
    heads = queries.shape[1] // HD
    pair = []
    for head in range(heads):
        span = slice(head * HD, (head + 1) * HD)
        scores = mm(kv[0, :, span], queries[:, span] * SCALE, NT) + mask[...]
        own_top = stats[head : head + 1, :]
        top = jnp.maximum(own_top, jnp.max(scores, axis=0, keepdims=True))
        exps = jnp.exp(scores - top)
        scale = jnp.exp(own_top - top)
        total = stats[heads + head : heads + head + 1, :] * scale
        total = total + jnp.sum(exps, axis=0, keepdims=True)
        result = sums[span, :] * scale + mm(kv[1, :, span], exps.astype(BF), TN)
        log_total[head : head + 1, :] = top + jnp.log(total)
        pair.append(result * (1.0 / total))
        if len(pair) == LANES // HD:
            wide = slice((head + 1) * HD - LANES, (head + 1) * HD)
            mixed[:, wide] = jnp.concatenate(pair, axis=0).T.astype(BF)
            pair = []
    io.put(0)
    io.put(1)
    out_weight = io.weight(0)
    io.put_columns(2, lambda columns: mm(mixed[...], out_weight[columns, :], NT))


def attend_body(n_blocks, io):
    queries = io.get(0)
    kvs = [io.get(1 + at) for at in range(n_blocks)]
    masks = [io.get(1 + n_blocks + at) for at in range(n_blocks)]
    mixed, log_total, _ = io.outs
    for head in range(queries.shape[1] // HD):
        span = slice(head * HD, (head + 1) * HD)
        query = queries[:, span] * SCALE
        scores = [
            mm(kv[0, :, span], query, NT) + mask[...]
            for kv, mask in zip(kvs, masks, strict=True)
        ]
        top = functools.reduce(jnp.maximum, [jnp.max(s, axis=0, keepdims=True) for s in scores])
        exps = [jnp.exp(s - top) for s in scores]
        total = total_of([jnp.sum(e, axis=0, keepdims=True) for e in exps])
        inverse = 1.0 / total
        result = total_of(
            [
                mm((e * inverse).astype(BF), kv[1, :, span], TN)
                for e, kv in zip(exps, kvs, strict=True)
            ]
        )
        log_total[head : head + 1, :] = top + jnp.log(total)
        mixed[:, span] = result.astype(BF)
    io.put(0)
    io.put(1)
    out_weight = io.weight(0)
    io.put_columns(2, lambda columns: mm(mixed[...], out_weight[columns, :], NT))


def terms_sum(terms):
    return total_of([terms[at].astype(F32) for at in range(terms.shape[0])])


def norm_body(io):
    stream = terms_sum(io.get(0)) + io.get(1)[...].astype(F32)
    io.outs[0][...] = stream
    io.put(0)
    n, _ = normalized(stream)
    io.outs[1][...] = (n * io.get(2)[...] + io.get(3)[...]).astype(BF)
    io.put(1)


def sum_body(io):
    io.outs[0][...] = (terms_sum(io.get(0)) + io.get(1)[...].astype(F32)).astype(BF)
    io.put(0)


def mlp_body(io):
    gate_out, up_out, hidden, _ = io.outs
    second_in = io.get(0)
    gate = mm(second_in[...], io.weight(0)[...], NN)
    gate_out[...] = gate.astype(BF)
    io.put(0)
    act = gate * jax.nn.sigmoid(gate)
    up = mm(second_in[...], io.weight(1)[...], NN)
    up_out[...] = up.astype(BF)
    io.put(1)
    hidden[...] = (act * up).astype(BF)
    io.put(2)
    down = io.weight(2)
    io.put_columns(3, lambda columns: mm(hidden[...], down[columns, :], NT))


def mlp_back_body(io):
    d_gate_up, _ = io.outs
    d_mlp = io.get(2)
    gate = io.get(0)[...].astype(F32)
    sig = jax.nn.sigmoid(gate)
    d_hidden = mm(d_mlp[...], io.weight(0)[...], NN)
    d_gate_up[1] = (d_hidden * (gate * sig)).astype(BF)
    d_gate_up[0] = (
        d_hidden * io.get(1)[...].astype(F32) * (sig * (1.0 + gate * (1.0 - sig)))
    ).astype(BF)
    io.put(0)
    gates, ups = io.weight(1), io.weight(2)

    def gradient(columns):
        return mm(d_gate_up[0], gates[columns, :], NT) + mm(d_gate_up[1], ups[columns, :], NT)

    io.put_columns(1, gradient)


def mlp_both_body(io):
    hidden, _, d_gate_up, _ = io.outs
    second_in = io.get(0)
    gate = mm(second_in[...], io.weight(0)[...], NN)
    sig = jax.nn.sigmoid(gate)
    act = gate * sig
    slope = sig * (1.0 + gate * (1.0 - sig))
    up = mm(second_in[...], io.weight(1)[...], NN)
    hidden[...] = (act * up).astype(BF)
    io.put(0)
    down = io.weight(2)
    d_hidden = mm(io.get(1)[...], down[...], NN)
    d_gate_up[1] = (d_hidden * act).astype(BF)
    d_gate_up[0] = (d_hidden * up * slope).astype(BF)
    io.put(2)
    gates, ups = io.weight(0), io.weight(1)

    def gradient(columns):
        return mm(d_gate_up[0], gates[columns, :], NT) + mm(d_gate_up[1], ups[columns, :], NT)

    io.put_columns(3, gradient)
    io.put_columns(1, lambda columns: mm(hidden[...], down[columns, :], NT))


def norm_back_body(io):
    c = terms_sum(io.get(0))
    grad, n = norm_back(io.get(1)[...].astype(F32), c, io.get(2)[...])
    grad = io.get(3)[...].astype(F32) + grad
    io.outs[0][...] = grad
    io.put(0)
    io.outs[1][...] = grad.astype(BF)
    io.put(1)
    io.outs[2][0:1, :] = jnp.sum(n * c, axis=0, keepdims=True)
    io.outs[2][1:2, :] = jnp.sum(c, axis=0, keepdims=True)
    io.put(2)


def attend_back_body(n_blocks, io):
    d_query, d_kvs = io.outs[0], io.outs[1:]
    d_mixed = io.extra[0]
    d_mixed[...] = mm(io.get(0)[...], io.weight(0)[...], NN).astype(BF)
    queries, log_total, tables = io.get(1), io.get(2), io.get(3)
    kvs = [io.get(4 + at) for at in range(n_blocks)]
    masks = [io.get(4 + n_blocks + at) for at in range(n_blocks)]
    pair = []
    for head in range(queries.shape[1] // HD):
        span = slice(head * HD, (head + 1) * HD)
        query = queries[:, span] * SCALE
        d_out = d_mixed[:, span]
        row_log = log_total[head : head + 1, :]
        probs = [
            jnp.exp(mm(kv[0, :, span], query, NT) + mask[...] - row_log)
            for kv, mask in zip(kvs, masks, strict=True)
        ]
        d_probs = [mm(kv[1, :, span], d_out, NT) for kv in kvs]
        delta = total_of(
            [jnp.sum(p * dp, axis=0, keepdims=True) for p, dp in zip(probs, d_probs, strict=True)]
        )
        d_scores = [
            (p * (dp - delta)).astype(BF) for p, dp in zip(probs, d_probs, strict=True)
        ]
        pair.append(
            total_of([mm(ds, kv[0, :, span], TN) for ds, kv in zip(d_scores, kvs, strict=True)])
            * SCALE
        )
        if len(pair) == LANES // HD:
            wide = slice((head + 1) * HD - LANES, (head + 1) * HD)
            d_query[:, wide] = turn_wide(jnp.concatenate(pair, axis=1), tables, -1.0).astype(BF)
            pair = []
        for ds, p, d_kv in zip(d_scores, probs, d_kvs, strict=True):
            d_kv[0, :, span] = mm(ds, query, NN).astype(d_kv.dtype)
            d_kv[1, :, span] = mm(p.astype(BF), d_out, NN).astype(d_kv.dtype)
    for at in range(1 + n_blocks):
        io.put(at)


def qkv_back_body(n_other, io):
    d_qkv, bias, _ = io.outs
    tables = io.get(1)
    terms = [io.get(2 + at) for at in range(1 + n_other)]
    d_qkv[0] = io.get(0)[...]
    d_qkv[1] = turn_wide(
        total_of([term[0].astype(F32) for term in terms]), tables, -1.0
    ).astype(BF)
    d_qkv[2] = total_of([term[1].astype(F32) for term in terms]).astype(BF)
    io.put(0)
    for index in range(3):
        bias[index : index + 1, :] = jnp.sum(d_qkv[index].astype(F32), axis=0, keepdims=True)
    io.put(1)
    weights = [io.weight(index) for index in range(3)]

    def gradient(columns):
        return total_of([mm(d_qkv[at], weights[at][columns, :], NT) for at in range(3)])

    io.put_columns(2, gradient)


def pack_body(io):
    gate_up, down = io.get(0), io.get(1)
    if len(io.outs) == 1:
        matrices = [io.outs[0].at[at] for at in range(3)]
    else:
        matrices = [out.at[0] for out in io.outs]
    matrices[0][...] = gate_up[:, 0, :]
    matrices[1][...] = gate_up[:, 1, :]
    matrices[2][...] = down[...].T
    for at in range(len(io.outs)):
        io.put(at)


def add_body(io):
    io.outs[0][...] = (io.get(0)[...].astype(F32) + io.get(2)[...].astype(F32)).astype(BF)
    io.put(0)
    io.outs[1][...] = (io.get(1)[...].astype(F32) + io.get(3)[...].astype(F32)).astype(BF)
    io.put(1)


def finish_body(is_mlp, io):
    own, x1, y1, x2, y2 = (io.get(at) for at in range(5))
    half = own.shape[2]
    main, other = io.outs
    matrices = own.shape[1]
    for side, (one, two) in enumerate(((x1, y2), (y1, x2))):
        rows = slice(side * half, (side + 1) * half)
        for matrix in range(matrices):
            whole = (
                own[side, matrix].astype(F32) + one[matrix].astype(F32) + two[matrix].astype(F32)
            )
            if matrix == matrices - 1:
                other[:, rows] = whole.T
            elif is_mlp:
                main[rows, matrix, :] = whole
            else:
                main[matrix, rows, :] = whole
    io.put(0)
    io.put(1)


def weight_grad_body(counts, n_left, pairs, *refs):
    ids = refs[0]
    n_in, n_held = len(counts), sum(counts)
    own = refs[1 : 1 + n_in]
    peer = refs[1 + n_in : 1 + 2 * n_in]
    outs = refs[1 + 2 * n_in : 6 + 2 * n_in]
    held = refs[6 + 2 * n_in : 6 + 2 * n_in + n_held]
    stage, in_sems, out_sems = refs[6 + 2 * n_in + n_held :]
    rows = held[0].shape[0] // 2
    loads = []
    for part, side in enumerate((own, peer)):
        at = 0
        for source, count in zip(side, counts, strict=True):
            for index in range(count):
                copy = pltpu.make_async_copy(
                    source if len(source.shape) == 2 else source.at[index],
                    held[at].at[pl.ds(part * rows, rows), :],
                    in_sems.at[at, part],
                )
                copy.start()
                loads.append(copy)
                at += 1
    for copy in loads:
        copy.wait()
    half = stage.shape[2]
    own_out, x1, y1, x2, y2 = outs
    targets = (
        (x1.at[0], y1.at[0]),
        (x1.at[1], x2),
        (y2, y1.at[1]),
        (own_out.at[0], own_out.at[1]),
    )
    stores = []
    for block in range(4):
        start = pl.multiple_of(ids[block], LANES)
        for matrix, (left, right) in enumerate(pairs):
            lhs = held[left][:, pl.ds(start, 2 * half)]
            result = mm(lhs, held[n_left + right][...], TN).astype(BF)
            stage[2 * block, matrix] = result[:half]
            stage[2 * block + 1, matrix] = result[half:]
        for part in range(2):
            copy = pltpu.make_async_copy(
                stage.at[2 * block + part], targets[block][part], out_sems.at[block, part]
            )
            copy.start()
            stores.append(copy)
    for copy in stores:
        copy.wait()


def after(array, *earlier):
    return lax.optimization_barrier((array,) + earlier)[0]


def pairs_of(axis, bit):
    return [(index, index ^ bit) for index in range(lax.axis_size(axis))]


def swap_x(array):
    return lax.ppermute(array, "fsdp", pairs_of("fsdp", 2))


def swap_core(array):
    return lax.ppermute(array, "fsdp", pairs_of("fsdp", 1))


def swap_y(array):
    return lax.ppermute(array, "ctx", pairs_of("ctx", 1))


def place():
    fsdp = lax.axis_index("fsdp")
    return fsdp // 2, fsdp % 2, lax.axis_index("ctx")


class Gather:
    def __init__(self, shard):
        self.shard = shard
        self.rows = shard.shape[1]

    def near_x(self, wait=()):
        self.from_x = swap_x(after(self.shard, *wait))

    def near_y(self, wait=()):
        self.from_y = swap_y(after(self.shard, *wait))
        self.mine = [self.shard, self.from_x, self.from_y]

    def near(self, wait_x=(), wait_y=()):
        self.near_x(wait_x)
        self.near_y(wait_y)

    def swap(self, *wait):
        self.peers = [swap_core(after(piece, *wait)) for piece in self.mine]

    def far(self, way, wait_x=(), wait_y=()):
        half = self.rows // 2
        self.way = way
        if way == "x":
            self.pieces = [swap_x(after(self.from_y, *wait_x))]
        elif way == "y":
            self.pieces = [swap_y(after(self.from_x, *wait_y))]
        else:
            self.pieces = [
                swap_x(after(self.from_y[:, :half], *wait_x)),
                swap_y(after(self.from_x[:, half:], *wait_y)),
            ]

    def all(self, *wait):
        far_peers = [swap_core(after(piece, *wait)) for piece in self.pieces]
        return self.mine + self.pieces + self.peers + far_peers


def piece_rows(rows):
    x, core, y = place()

    def row(x_at, core_at, y_at):
        return ((x_at * 2 + core_at) * 2 + y_at) * rows

    offs = []
    for halves in (0, 1):
        for core_at in (core, 1 - core):
            offs += [row(x, core_at, y), row(1 - x, core_at, y), row(x, core_at, 1 - y)]
            offs.append(row(1 - x, core_at, 1 - y))
            if halves:
                offs.append(row(1 - x, core_at, 1 - y) + rows // 2)
    return offs


def gather_whole(shard):
    return [lax.all_gather(shard, ("fsdp", "ctx"), axis=1, tiled=True)]


def gather_small(packed, fast):
    if not fast:
        return lax.all_gather(packed, ("fsdp", "ctx"), axis=1, tiled=True), ()
    x, core, y = place()

    def join(array, other, bit):
        return jnp.where(bit == 0, jnp.stack([array, other]), jnp.stack([other, array]))

    from_y = swap_y(packed)
    held = join(packed, from_y, y)
    held = join(held, swap_core(held), core)
    held = join(held, swap_x(held), x)
    rows, cols = packed.shape
    return held.transpose(3, 0, 1, 2, 4).reshape(rows, 8 * cols), (from_y,)


def reduce_small(sums, fast, *wait):
    if not fast:
        part = lax.psum_scatter(sums, ("fsdp", "ctx"), scatter_dimension=1, tiled=True)
        return lax.psum(part, "tp")
    x, core, y = place()
    rows, width = sums.shape
    held = sums.reshape(rows, 2, 2, 2, width // 8).transpose(1, 3, 2, 0, 4)
    for bit, swap in ((x, swap_x), (y, swap_y), (core, swap_core)):
        keep = jnp.where(bit == 0, held[0], held[1])
        send = jnp.where(bit == 0, held[1], held[0])
        held = keep + swap(after(send, *wait) if swap is swap_y else send)
    step = 1
    while step < lax.axis_size("tp"):
        held = held + lax.ppermute(held, "tp", pairs_of("tp", step))
        step *= 2
    return held


def tensor_scatter(part, *earlier):
    size = lax.axis_size("tp")
    blocks = after(part, *earlier).reshape(size, part.shape[0] // size, part.shape[1])
    return lax.all_to_all(blocks, "tp", 0, 0, tiled=True)


def tensor_gather(copies):
    return lax.all_to_all(copies, "tp", 0, 0, tiled=True)


def flat(blocks):
    return blocks.reshape(-1, blocks.shape[-1])


def weight_grads(own, peer, n_left, pairs, earlier, name):
    counts = tuple(1 if array.ndim == 2 else array.shape[0] for array in own)
    columns = own[-1].shape[-1]
    tokens, width = own[0].shape
    peer = [
        swap_core(after(array, *earlier)) if other is None else other
        for array, other in zip(own, peer, strict=True)
    ]
    rows = width // 8
    half = rows // 2
    x, core, y = place()
    ids = jnp.stack(
        [
            ((x_at * 2 + core) * 2 + y_at) * rows
            for x_at, y_at in ((1 - x, 1 - y), (1 - x, y), (x, 1 - y), (x, y))
        ]
    ).astype(jnp.int32)
    block = (len(pairs), half, columns)
    hbm = pl.BlockSpec(memory_space=pltpu.HBM)
    scratch = [
        pltpu.VMEM((2 * tokens, array.shape[-1]), BF)
        for array, count in zip(own, counts, strict=True)
        for _ in range(count)
    ]
    scratch += [
        pltpu.VMEM((8,) + block, BF),
        pltpu.SemaphoreType.DMA((sum(counts), 2)),
        pltpu.SemaphoreType.DMA((4, 2)),
    ]
    own_sum, x1, y1, x2, y2 = pl.pallas_call(
        functools.partial(weight_grad_body, counts, n_left, pairs),
        out_shape=[pltpu.HBM((2,) + block, BF)] * 3 + [pltpu.HBM(block, BF)] * 2,
        in_specs=[pl.BlockSpec(memory_space=pltpu.SMEM)] + [hbm] * (2 * len(own)),
        out_specs=[hbm] * 5,
        scratch_shapes=scratch,
        compiler_params=pltpu.CompilerParams(vmem_limit_bytes=VMEM_LIMIT),
        cost_estimate=cost(name),
        name=name,
    )(ids, *[pltpu.with_memory_space_constraint(a, pltpu.HBM) for a in list(own) + peer])
    return (own_sum, x2, y2), (x1, y1)


def add_received(spots, parts, received, earlier, name):
    _, x2, y2 = parts
    got_x1, got_y1 = received
    block = shape(x2.shape, BF)
    return kernel(
        add_body,
        name,
        spots,
        [after(x2, *earlier), y2, (got_y1, 0), (got_x1, 0)],
        [block, block],
    )


def send_second(parts, received, sums, earlier):
    far_x = swap_x(after(sums[0], *earlier))
    far_y = swap_y(after(sums[1], *earlier))
    return [parts[0], (received[0], 1), (received[1], 1), far_x, far_y]


def reduce_second(spots, parts, received, earlier_add, earlier_send, name):
    sums = add_received(spots, parts, received, earlier_add, name)
    return send_second(parts, received, sums, earlier_send), sums[0]


def layout(lengths, first_row, row_count):
    token_index = first_row + jnp.arange(row_count, dtype=jnp.int32)
    doc_ends = jnp.cumsum(lengths)
    starts = doc_ends - lengths
    segment = jnp.sum(
        (token_index[:, None] >= doc_ends[None, :]).astype(jnp.int32), axis=1, dtype=jnp.int32
    )
    doc_begin = jnp.max(
        jnp.where(token_index[:, None] >= starts[None, :], starts[None, :], 0), axis=1
    )
    return (segment, token_index - doc_begin, token_index)


def rotary_tables(position):
    frequency = 10000.0 ** (-jnp.arange(0, ROT, 2, dtype=F32) / ROT)
    angles = position.astype(F32)[:, None] * frequency[None, :]
    cos, sin = jnp.cos(angles), jnp.sin(angles)
    rows = position.shape[0]
    blank = jnp.zeros((rows, ROT // 2), F32)
    rest = HD - ROT
    keep = jnp.concatenate([cos, cos, jnp.ones((rows, rest), F32)], axis=1)
    below = jnp.concatenate([blank, sin, jnp.zeros((rows, rest), F32)], axis=1)
    above = jnp.concatenate([-sin, blank, jnp.zeros((rows, rest), F32)], axis=1)
    return jnp.stack([jnp.tile(t, (1, LANES // HD)) for t in (keep, below, above)])


def local(
    tokens,
    cotangent,
    doc_lengths,
    norm_gains,
    norm_biases,
    qkv_weight,
    qkv_bias,
    out_weight,
    gate_up_weight,
    down_weight,
):
    rows = tokens.shape[1]
    width = tokens.shape[2]
    heads_width = qkv_weight.shape[3]
    hidden_width = gate_up_weight.shape[3]
    heads = heads_width // HD
    layers = norm_gains.shape[0]
    block_rows = qkv_weight.shape[1]
    ctx_size = lax.axis_size("ctx")
    fast = lax.axis_size("fsdp") == 4 and ctx_size == 2
    ctx_rank = lax.axis_index("ctx")
    tensor_rank = lax.axis_index("tp")

    small = jnp.concatenate(
        [
            norm_gains.reshape(2 * layers, -1),
            norm_biases.reshape(2 * layers, -1),
            qkv_bias.reshape(3 * layers, -1),
        ]
    )
    small, sent_small = gather_small(small, fast)
    small = small.astype(F32)
    gains = small[: 2 * layers].reshape(layers, 2, width)
    shifts = small[2 * layers : 4 * layers].reshape(layers, 2, width)
    biases = lax.dynamic_slice_in_dim(
        small[4 * layers :], tensor_rank * heads_width, heads_width, 1
    ).reshape(layers, 3, heads_width)

    tensor_size = lax.axis_size("tp")
    block = rows // tensor_size
    spots = piece_rows(block_rows) if fast else [jnp.int32(0)]
    spots = jnp.stack([jnp.asarray(spot, jnp.int32) for spot in spots])
    spots_at = {8: 0, 10: 8, 1: 0}

    def slot(pieces, matrix):
        return (pieces, matrix, spots_at[len(pieces)])

    shards = []
    for layer in range(layers):
        if fast:
            counts = (3,) if layer == 0 else (1, 1, 1)
            mlp_shards = kernel(
                pack_body,
                "pack",
                spots,
                [(gate_up_weight, layer), (down_weight, layer)],
                [shape((count, block_rows, hidden_width), BF) for count in counts],
            )
        else:
            mlp_shards = [
                jnp.concatenate(
                    [gate_up_weight[layer].transpose(1, 0, 2), down_weight[layer].T[None]]
                )
            ]
        qkv_shard, out_shard = qkv_weight[layer].transpose(1, 0, 2), out_weight[layer].T[None]
        shards.append((jnp.concatenate([qkv_shard, out_shard]), *mlp_shards))

    lengths = doc_lengths[0]
    seg_query, pos_query, index_query = layout(lengths, ctx_rank * rows, rows)
    tables = rotary_tables(pos_query)

    def mask_of(first, count, usable):
        seg_key, _, index_key = layout(lengths, first, count)
        allowed = (seg_query[None, :] == seg_key[:, None]) & (
            index_query[None, :] >= index_key[:, None]
        )
        return jnp.where(allowed & usable, 0.0, -1e30).astype(F32)

    if fast:
        masks = [
            mask_of(jnp.int32(0), rows, ctx_rank > 0),
            mask_of(ctx_rank * rows, rows, True),
        ]
    else:
        masks = [mask_of(jnp.int32(0), rows * ctx_size, True)]
    n_blocks = len(masks)

    wide = shape((rows, width), BF)
    wide_out = (wide, HALVES)
    inner = shape((rows, hidden_width), BF)
    headed = shape((rows, heads_width), BF)
    block_f = shape((block, width), F32)
    copies_b = (shape((tensor_size, block, width), BF), EACH)

    stream = lax.dynamic_slice_in_dim(tokens[0], tensor_rank * block, block, 0)
    first_in = None
    saved, groups = [], []
    if fast:
        attn_g, mlp_g = (Gather(shard) for shard in shards[0])
        attn_g.near((), sent_small)
        attn_g.swap()
        attn_g.far("both")
        mlp_g.near_x(attn_g.pieces[:1])
    for layer in range(layers):
        if fast:
            attn_pieces = attn_g.all()
        else:
            attn_pieces, mlp_pieces = (gather_whole(shard) for shard in shards[layer])
            mlp_slots = [slot(mlp_pieces, index) for index in range(3)]
        kv_shape = shape((2, rows, heads_width), BF)
        if layer == 0:
            args = [biases[0], tables, gains[0, 0][None], shifts[0, 0][None], tokens[0]]
            if fast:
                args[0] = after(args[0], mlp_g.shard)
        else:
            args = [biases[layer], tables, Free(first_in)]
        if fast:
            kv, *normed = kernel(
                functools.partial(key_value_body, layer == 0),
                "key_value",
                spots,
                args,
                [kv_shape] + ([wide] if layer == 0 else []),
                [slot(attn_pieces, index) for index in (1, 2)],
            )
        else:
            queries, kv, *normed = kernel(
                functools.partial(qkv_body, layer == 0),
                "qkv",
                spots,
                args,
                [headed, kv_shape] + ([wide] if layer == 0 else []),
                [slot(attn_pieces, index) for index in (1, 2, 0)],
            )
        if layer == 0:
            first_in = normed[0]
        attended = [headed, shape((heads, rows), F32), wide_out]
        if fast:
            prev = lax.ppermute(kv, "ctx", [(0, 1)])
            kv_blocks = [prev, kv]
            queries, value_sums, stats = kernel(
                attend_own_body,
                "attend_own",
                spots,
                [biases[layer], tables, Free(first_in), kv, masks[1]],
                [headed, shape((heads_width, rows), F32), shape((2 * heads, rows), F32)],
                [slot(attn_pieces, 0)],
            )
            if layer == 0:
                mlp_g.near_y((prev, queries))
            else:
                up_g.near_y((prev, queries))
                down_g.near_y((up_g.from_y,))
            mixed, log_total, part = kernel(
                attend_other_body,
                "attend_other",
                spots,
                [queries, after(prev, queries), masks[0], value_sums, stats],
                attended,
                [slot(attn_pieces, 3)],
            )
        else:
            kv_blocks = [lax.all_gather(kv, "ctx", axis=1, tiled=True)]
            mixed, log_total, part = kernel(
                functools.partial(attend_body, n_blocks),
                "attend",
                spots,
                [queries] + kv_blocks + masks,
                attended,
                [slot(attn_pieces, 3)],
            )
        terms = tensor_scatter(part)
        if fast and layer == 0:
            terms = after(terms, mlp_g.from_x)
        elif fast:
            gate_g.swap(part)
            gate_g.far("both", (part,), (part,))
            up_g.swap(part)
            terms = after(terms, down_g.from_x, up_g.from_y)
        mid, normed = kernel(
            norm_body,
            "norm",
            spots,
            [Free(terms), stream, gains[layer, 1][None], shifts[layer, 1][None]],
            [block_f, copies_b],
        )
        second_in = tensor_gather(normed)
        if fast:
            if layer == 0:
                mlp_g.swap(mid)
                mlp_g.far("both", (mid,), (mid,))
                mlp_pieces = mlp_g.all(second_in)
                mlp_slots = [slot(mlp_pieces, index) for index in range(3)]
                sent = mlp_g.pieces
            else:
                up_g.far("both", (mid,), (mid,))
                down_g.swap(mid)
                down_g.far("both", (mid,), (mid,))
                mlp_groups = (gate_g.all(), up_g.all(), down_g.all(second_in))
                mlp_slots = [slot(pieces, 0) for pieces in mlp_groups]
                sent = down_g.pieces
        second_in = flat(second_in)
        if layer < layers - 1:
            gate, up, hidden, part = kernel(
                mlp_body,
                "mlp",
                spots,
                [Free(second_in)],
                [inner, inner, inner, wide_out],
                mlp_slots,
            )
        else:
            peer = swap_core(cotangent[0]) if fast else ()
            hidden, last_part, d_gate_up, part = kernel(
                mlp_both_body,
                "mlp_both",
                spots,
                [Free(second_in), after(cotangent[0], peer)],
                [inner, wide_out, shape((2, rows, hidden_width), BF), wide_out],
                mlp_slots,
            )
            gate, up, last_mid = None, None, mid
        saved.append((stream, first_in, queries, kv_blocks, mixed, log_total, mid))
        saved[-1] += (second_in, gate, up, hidden)
        groups.append((attn_pieces, mlp_slots))
        if layer == layers - 1:
            break
        terms = tensor_scatter(part)
        if fast:
            attn_g, gate_g, up_g, down_g = (Gather(shard) for shard in shards[layer + 1])
            attn_g.near(sent[:1], sent[1:])
            attn_g.swap(part)
            attn_g.far("both", (part,), (part,))
            gate_g.near(sent[:1], sent[1:])
            up_g.near_x((gate_g.from_x,))
            down_g.near_x((up_g.from_x,))
            terms = after(terms, gate_g.shard, *attn_g.pieces, *attn_g.peers)
        stream, normed = kernel(
            norm_body,
            "norm",
            spots,
            [Free(terms), mid, gains[layer + 1, 0][None], shifts[layer + 1, 0][None]],
            [block_f, copies_b],
        )
        first_in = flat(tensor_gather(normed))
        if fast:
            first_in = after(first_in, gate_g.from_x, gate_g.from_y)

    attn_outs, mlp_outs, pending, mlp_pending = None, None, None, None
    sums = [None] * layers
    plain = [None] * layers
    grad = lax.dynamic_slice_in_dim(cotangent[0], tensor_rank * block, block, 0)
    d_mlp = cotangent[0]
    for layer in reversed(range(layers)):
        (stream, first_in, queries, kv_blocks, mixed, log_total, mid) = saved[layer][:7]
        (second_in, gate, up, hidden) = saved[layer][7:]
        attn_pieces, mlp_slots = groups[layer]
        late = layer == layers - 1
        mlp_peer = [None] * 4
        if late:
            mlp_peer[1] = peer
        else:
            if fast:
                mlp_peer[0], mlp_peer[3] = swap_core(second_in), swap_core(hidden)
                gate = after(gate, mlp_peer[0], mlp_peer[3])
            d_gate_up, part = kernel(
                mlp_back_body,
                "mlp_back",
                spots,
                [gate, up, Free(d_mlp)],
                [shape((2, rows, hidden_width), BF), wide_out],
                [mlp_slots[2], mlp_slots[0], mlp_slots[1]],
            )
        terms = tensor_scatter(part)
        pairs = ((0, 0), (0, 1), (1, 2))
        if fast:
            if pending is not None:
                part = after(part, *mlp_pending[3:])
            mlp_parts, (to_x, to_y) = weight_grads(
                [second_in, d_mlp, d_gate_up, hidden], mlp_peer, 2, pairs, (part,), "mlp_grads"
            )
            terms = after(terms, mlp_parts[0])
            if pending is not None:
                mlp_pending[0] = after(mlp_pending[0], mlp_parts[0])
                mlp_outs = mlp_finish(spots, mlp_outs, mlp_pending, layer + 1, layers)
                terms = after(terms, mlp_outs[0], *pending[1])
            got_x = swap_x(to_x)
            got_y = None if late else swap_y(to_y)
        else:
            mlp_grad = plain_grads(
                [second_in, d_mlp], [d_gate_up[0], d_gate_up[1], hidden], pairs
            )
        grad_mid, normed, sums_two = kernel(
            norm_back_body,
            "norm_back",
            spots,
            [Free(terms), mid, gains[layer, 1][None], grad],
            [block_f, copies_b, shape((2, width), F32)],
        )
        gathered = tensor_gather(normed)
        d_attn = flat(gathered)
        if layer == layers - 1:
            out_terms = tensor_scatter(last_part, gathered)
            (summed,) = kernel(sum_body, "sum", spots, [out_terms, last_mid], [copies_b])
        elif layer == layers - 2:
            out_blocks = tensor_gather(after(summed, gathered))
        kv_outs = [shape(kv.shape, BF) for kv in kv_blocks]
        if fast:
            kv_outs[-1] = shape((2, rows, heads_width), F32)
        d_query, *d_kvs = kernel(
            functools.partial(attend_back_body, n_blocks),
            "attend_back",
            spots,
            [Free(d_attn), queries, log_total, tables] + kv_blocks + masks,
            [headed] + kv_outs,
            [slot(attn_pieces, 3)],
            extra=[pltpu.VMEM((rows, heads_width), BF)],
        )
        if fast:
            own = d_kvs[1]
            other = [lax.ppermute(d_kvs[0] if late else after(d_kvs[0], got_y), "ctx", [(1, 0)])]
            if late:
                got_y = swap_y(after(to_y, other[0]))
                own = after(own, got_x)
            else:
                mlp_sums = add_received(spots, mlp_parts, (got_x, got_y), (d_kvs[0],), "mlp_add")
                own = after(own, mlp_sums[0])
                if pending is not None:
                    attn_sums = add_received(spots, *pending, (mlp_sums[0],), "attn_add")
                    own = after(own, attn_sums[0])
                    attn_terms = send_second(*pending, attn_sums, (other[0],))
                mlp_terms = send_second(mlp_parts, (got_x, got_y), mlp_sums, ())
            attn_peer = [swap_core(after(a, d_kvs[0])) for a in (first_in, d_attn)]
            attn_peer += [None, swap_core(after(mixed, d_kvs[0]))]
            own = after(own, attn_peer[0], attn_peer[1], attn_peer[3])
        else:
            own = lax.psum_scatter(d_kvs[0], "ctx", scatter_dimension=1, tiled=True)
            other = []
        if layer == layers - 1:
            own = after(own, out_terms)
        elif layer == layers - 2:
            own = after(own, out_blocks)
        d_qkv, bias_sums, part = kernel(
            functools.partial(qkv_back_body, len(other)),
            "qkv_back",
            spots,
            [d_query, tables, own] + other,
            [shape((3, rows, heads_width), BF), shape((3, heads_width), F32), wide_out],
            [slot(attn_pieces, index) for index in range(3)],
        )
        terms = tensor_scatter(part)
        if layer == layers - 1:
            terms = after(terms, summed)
        pairs = ((0, 0), (0, 1), (0, 2), (1, 3))
        if fast:
            ready = (part,) if late else (part, *mlp_terms[3:])
            attn_parts, (to_x, to_y) = weight_grads(
                [first_in, d_attn, d_qkv, mixed], attn_peer, 2, pairs, ready, "attn_grads"
            )
            pending = (attn_parts, (swap_x(to_x), swap_y(to_y)))
            terms = after(terms, attn_parts[0])
        else:
            rights = [d_qkv[0], d_qkv[1], d_qkv[2], mixed]
            plain[layer] = (plain_grads([first_in, d_attn], rights, pairs), mlp_grad)
        grad, normed, sums_one = kernel(
            norm_back_body,
            "norm_back",
            spots,
            [Free(terms), stream, gains[layer, 0][None], grad_mid],
            [block_f, copies_b, shape((2, width), F32)],
        )
        d_mlp = flat(tensor_gather(normed))
        if fast:
            if late:
                mlp_pending, mlp_added = reduce_second(
                    spots, mlp_parts, (got_x, got_y), (grad,), (), "mlp_add"
                )
                d_mlp = after(d_mlp, mlp_added)
            else:
                if mlp_pending is not None:
                    attn_terms[0] = after(attn_terms[0], grad)
                    attn_outs = attn_finish(spots, attn_outs, attn_terms, layer + 1, layers)
                mlp_terms[0] = after(mlp_terms[0], grad)
                mlp_outs = mlp_finish(spots, mlp_outs, mlp_terms, layer, layers)
        bias_rows = lax.dynamic_update_slice_in_dim(
            jnp.zeros((3, width), F32), bias_sums, tensor_rank * heads_width, 1
        )
        sums[layer] = jnp.concatenate(
            [sums_one[0:1], sums_two[0:1], sums_one[1:2], sums_two[1:2], bias_rows]
        )
    wait = ()
    if fast:
        attn_terms, attn_added = reduce_second(
            spots, *pending, (grad, mlp_outs[0], attn_outs[0]), (), "attn_add"
        )
        wait = (attn_added,)
    totals = reduce_small(jnp.concatenate(sums), fast, *wait).reshape(layers, 7, -1)
    if fast:
        attn_outs = attn_finish(spots, attn_outs, attn_terms, 0, layers)
    grad_input = d_mlp.astype(F32)
    if fast:
        grads = (attn_outs[0].transpose(0, 2, 1, 3), attn_outs[1], mlp_outs[0], mlp_outs[1])
    else:
        attn = jnp.stack([pair[0] for pair in plain])
        mlp = jnp.stack([pair[1] for pair in plain])
        grads = (
            attn[:, :3].transpose(0, 2, 1, 3),
            attn[:, 3].transpose(0, 2, 1),
            mlp[:, :2].transpose(0, 2, 1, 3),
            mlp[:, 2].transpose(0, 2, 1),
        )
    return (
        flat(out_blocks)[None],
        grad_input[None],
        totals[:, 0:2],
        totals[:, 2:4],
        grads[0],
        totals[:, 4:7],
        grads[1],
        grads[2],
        grads[3],
    )


def mlp_finish(spots, outs, terms, layer, layers):
    _, half, columns = terms[3].shape
    rows = 2 * half
    return kernel(
        functools.partial(finish_body, True),
        "mlp_finish",
        spots,
        terms,
        [
            (shape((layers, rows, 2, columns), F32), layer),
            (shape((layers, columns, rows), F32), layer),
        ],
        reuse=() if outs is None else ((outs[0], 0), (outs[1], 1)),
    )


def attn_finish(spots, outs, terms, layer, layers):
    matrices, half, columns = terms[3].shape
    rows = 2 * half
    return kernel(
        functools.partial(finish_body, False),
        "attn_finish",
        spots,
        terms,
        [
            (shape((layers, matrices - 1, rows, columns), F32), layer),
            (shape((layers, columns, rows), F32), layer),
        ],
        reuse=() if outs is None else ((outs[0], 0), (outs[1], 1)),
    )


def plain_grads(lefts, rights, pairs):
    whole = jnp.stack([mm(lefts[a], rights[b], TN).astype(BF) for a, b in pairs])
    return lax.psum_scatter(whole, ("fsdp", "ctx"), scatter_dimension=1, tiled=True).astype(F32)


def solution(mesh):
    return jax.shard_map(
        local,
        mesh=mesh,
        in_specs=(
            P("fsdp", "ctx", None),
            P("fsdp", "ctx", None),
            P("fsdp", None),
            P(None, None, ("fsdp", "ctx")),
            P(None, None, ("fsdp", "ctx")),
            P(None, ("fsdp", "ctx"), None, "tp"),
            P(None, None, ("fsdp", "ctx")),
            P(None, "tp", ("fsdp", "ctx")),
            P(None, ("fsdp", "ctx"), None, "tp"),
            P(None, "tp", ("fsdp", "ctx")),
        ),
        out_specs=(
            P("fsdp", "ctx", None),
            P("fsdp", "ctx", None),
            P(None, None, ("fsdp", "ctx")),
            P(None, None, ("fsdp", "ctx")),
            P(None, ("fsdp", "ctx"), None, "tp"),
            P(None, None, ("fsdp", "ctx")),
            P(None, "tp", ("fsdp", "ctx")),
            P(None, ("fsdp", "ctx"), None, "tp"),
            P(None, "tp", ("fsdp", "ctx")),
        ),
        check_vma=False,
    )
```
